32 devices in a mesh: section: 4 (over x, core), expert: 8 (over z, y).
Axes of the slice: x: 2, y: 2, z: 4, core: 2. Of those that a mesh axis runs over, the one named last changes fastest.
Arguments:
- inputs: bfloat16 [2, 1024, 1024], P(None, 'expert'), may hold values from -6 to 6
- norm_gain: float32 [4, 1024], P('section'), may hold values from 0.25 to 1.75
- w_up: bfloat16 [4, 8, 1024, 2048], P('section', 'expert'), may hold values from -0.1875 to 0.1875
- w_down: bfloat16 [4, 8, 2048, 1024], P('section', 'expert'), may hold values from -0.125 to 0.125
- expert_ids: int32 [4, 2, 1024, 2], P('section', None, 'expert'), may hold values from 0 to 7, as said below
- gates: float32 [4, 2, 1024, 2], P('section', None, 'expert'), may hold values from 0.1 to 1
- out_grad: bfloat16 [2, 1024, 1024], P(None, 'expert'), may hold values from -6 to 6
Outputs:
- section_out: bfloat16 [4, 2, 1024, 1024], P('section', None, 'expert')
- in_grad: bfloat16 [4, 2, 1024, 1024], P('section', None, 'expert')
The draws below stay inside these ranges and needn't reach their ends.
Inputs may be any that keep to these rules, and one draw needn't show every extreme that they name: `expert_ids`: for every layer and micro-batch the two experts of a row differ; in each aligned block of 128 rows (the rows of one device) no expert is named more than 40 times, and one expert, the same in every block of that layer and micro-batch, is named exactly 40 times.
All inputs are finite; a program needn't handle non-finite values.
Results may differ from the reference program's by a relative error of at most 0.012.
Values may be sent and summed in bfloat16 or wider, within the bound.
No kernel may reach another device: no remote copies, remote signals or barrier semaphores. Data moves between devices by JAX's collectives and lax.ppermute only.
A program may use at most 64 MiB of HBM per device.

```python
import math
import jax
import jax.numpy as jnp
from jax import lax

D = 1024
FF = 2048
TOK_DEV = 128
MICRO = 2
SECTIONS = 4
EXPERTS = 8
TOKENS = 1024
CAP = 40


def block_routes(block_key, hot_expert):
    key_order, key_amount, key_rows, key_flip = jax.random.split(block_key, 4)
    shuffled = jax.random.permutation(key_order, EXPERTS).astype(jnp.int32)
    is_hot = (shuffled == hot_expert).astype(jnp.int32)
    order = shuffled[jnp.argsort(-is_hot, stable=True)]
    amounts = jax.random.randint(key_amount, (EXPERTS,), 1, CAP + 1).astype(jnp.int32)
    amounts = amounts.at[0].set(CAP)
    pair_total = 2 * TOK_DEV
    before = jnp.cumsum(amounts) - amounts
    take_first = jnp.clip(pair_total - before, 0, amounts)
    remaining = pair_total - jnp.sum(take_first)
    room_left = CAP - take_first
    before_room = jnp.cumsum(room_left) - room_left
    take_second = jnp.clip(remaining - before_room, 0, room_left)
    counts = (take_first + take_second).astype(jnp.int32)
    labels = jnp.repeat(order, counts, total_repeat_length=pair_total)
    row_order = jax.random.permutation(key_rows, TOK_DEV)
    first_pick = labels[:TOK_DEV][row_order]
    second_pick = labels[TOK_DEV:][row_order]
    swap_pick = jax.random.randint(key_flip, (TOK_DEV,), 0, 2)
    left_pick = jnp.where(swap_pick == 1, second_pick, first_pick)
    right_pick = jnp.where(swap_pick == 1, first_pick, second_pick)
    return jnp.stack([left_pick, right_pick], axis=-1).astype(jnp.int32)


def layer_routes(layer_key):
    key_hot, key_blocks = jax.random.split(layer_key)
    hot_expert = jax.random.randint(key_hot, (), 0, EXPERTS).astype(jnp.int32)
    block_keys = jax.random.split(key_blocks, EXPERTS)

    def per_block(block_key):
        return block_routes(block_key, hot_expert)
    return jax.vmap(per_block)(block_keys).reshape(TOKENS, 2)


def draw_expert_ids(key, part):
    base_key = jax.random.fold_in(key, 17)
    key_list = jax.random.split(base_key, SECTIONS * MICRO)
    routes_all = jax.vmap(layer_routes)(key_list)
    return routes_all.reshape(SECTIONS, MICRO, TOKENS, 2).astype(jnp.int32)


def block_levels(key, dims, pieces, smallest, top_value):
    def one(axis_at, blocks):
        steps = jax.random.uniform(jax.random.fold_in(jax.random.fold_in(key, 6), axis_at), (blocks,), jnp.float32, smallest / len(pieces), top_value / len(pieces))
        return jnp.repeat(jnp.exp(steps), dims[axis_at] // blocks).reshape((-1,) + (1,) * (len(dims) - axis_at - 1))

    factor_of = one(*pieces[0])
    for cut in pieces[1:]:
        factor_of = factor_of * one(*cut)
    return factor_of


def normal_values(rng, dims, scale, most, pieces=(), kind=jnp.bfloat16):
    drawn = jax.random.normal(rng, dims, jnp.float32) * scale
    if len(pieces) > 0:
        drawn = block_levels(rng, dims, pieces, -0.22, 0.18) * drawn
    return jnp.clip(drawn, min=-most, max=most).astype(kind)


def setup_inputs(seed: int = 0) -> dict:
    arg_keys = jax.random.split(jax.random.key(seed), 8)
    return {
        "inputs": normal_values(arg_keys[0], (MICRO, TOKENS, D), 1.0, 6.0, ((1, 8),)),
        "norm_gain": jnp.clip(1.0 + 0.15 * jax.random.normal(arg_keys[1], (SECTIONS, D), jnp.float32), 0.25, 1.75),
        "w_up": normal_values(arg_keys[2], (SECTIONS, EXPERTS, D, FF), D ** -0.5, 0.1875, ((0, 4), (1, 8))),
        "w_down": normal_values(arg_keys[3], (SECTIONS, EXPERTS, FF, D), FF ** -0.5, 0.125, ((0, 4), (1, 8))),
        "expert_ids": draw_expert_ids(jax.random.fold_in(arg_keys[7], 71), 0),
        "gates": jnp.clip(jnp.exp(math.log(1.0) - 2.3025851 * jax.random.uniform(arg_keys[5], (SECTIONS, MICRO, TOKENS, 2), jnp.float32) ** block_levels(arg_keys[5], (SECTIONS, MICRO, TOKENS, 2), ((0, 4), (2, 8)), -0.2, 0.2)), 0.1, 1.0),
        "out_grad": normal_values(arg_keys[6], (MICRO, TOKENS, D), 1.0, 6.0, ((1, 8),)),
    }


epsilon = 1e-05
gelu_coef = 0.7978845608028654
cubic_coef = 0.044715
contract_last = (((1,), (1,)), ((), ()))

def gelu_value(pre_act):
    tanh_arg = gelu_coef * (pre_act + cubic_coef * pre_act * pre_act * pre_act)
    return 0.5 * pre_act * (1.0 + jnp.tanh(tanh_arg))

def gelu_slope(pre_act):
    tanh_arg = gelu_coef * (pre_act + cubic_coef * pre_act * pre_act * pre_act)
    tangent = jnp.tanh(tanh_arg)
    return 0.5 * (1.0 + tangent) + 0.5 * pre_act * (1.0 - tangent * tangent) * gelu_coef * (1.0 + 3.0 * cubic_coef * pre_act * pre_act)

def normalize(state_rows, gain_row):
    values = state_rows.astype(jnp.float32)
    inv_rms = lax.rsqrt(lax.optimization_barrier(jnp.mean(values * values, axis=-1, keepdims=True)) + epsilon)
    return (values * inv_rms * gain_row).astype(jnp.bfloat16)

def norm_backward(upstream, state_rows, normed_grad, gain_row):
    values = state_rows.astype(jnp.float32)
    inv_rms = lax.rsqrt(lax.optimization_barrier(jnp.mean(values * values, axis=-1, keepdims=True)) + epsilon)
    spread = normed_grad * gain_row
    along = lax.optimization_barrier(jnp.mean(spread * values, axis=-1, keepdims=True))
    return (upstream.astype(jnp.float32) + inv_rms * spread - values * inv_rms * inv_rms * inv_rms * along).astype(jnp.bfloat16)

def slot_targets(block_picks, experts, capacity):
    flat_picks = block_picks.reshape(-1).astype(jnp.int32)
    onehot = (flat_picks[:, None] == jnp.arange(experts, dtype=jnp.int32)[None, :]).astype(jnp.int32)
    earlier = jnp.cumsum(onehot, axis=0) - onehot
    slot_index = lax.optimization_barrier(jnp.sum(earlier * onehot, axis=1)).astype(jnp.int32)
    return flat_picks * capacity + slot_index

def positions(picks):
    slots_all = EXPERTS * CAP

    def per_block(block_picks):
        return slot_targets(block_picks, EXPERTS, CAP)
    local_target = jax.vmap(per_block)(picks.reshape(EXPERTS, TOK_DEV, 2))
    expert = local_target // CAP
    slot_index = local_target - expert * CAP
    source = jnp.arange(EXPERTS, dtype=jnp.int32)[:, None]
    return (expert * slots_all + source * CAP + slot_index).reshape(-1).astype(jnp.int32)

def scatter_pairs(pair_rows, flat_index):
    buffer = jnp.zeros((EXPERTS * EXPERTS * CAP, D), pair_rows.dtype)
    return buffer.at[flat_index].set(pair_rows).reshape(EXPERTS, EXPERTS * CAP, D)

def layer_forward(state_rows, gain_row, up_all, down_all, picks, weights):
    flat_index = positions(picks)
    normed = normalize(state_rows, gain_row)
    buffer = scatter_pairs(jnp.repeat(normed, 2, axis=0), flat_index)

    def one_expert(expert_item):
        rows_in, up_matrix, down_matrix = expert_item
        pre_act = jnp.dot(rows_in, up_matrix, preferred_element_type=jnp.float32)
        active = gelu_value(pre_act).astype(jnp.bfloat16)
        return jnp.dot(active, down_matrix, preferred_element_type=jnp.float32).astype(jnp.bfloat16)
    outputs = lax.map(one_expert, (buffer, up_all, down_all)).reshape(-1, D)
    pair_rows = outputs[flat_index].reshape(TOKENS, 2, D).astype(jnp.float32)
    mixed_rows = state_rows.astype(jnp.float32) + lax.optimization_barrier(jnp.sum(weights[:, :, None] * pair_rows, axis=1))
    return mixed_rows.astype(jnp.bfloat16)

def layer_backward(upstream, state_rows, gain_row, up_all, down_all, picks, weights):
    flat_index = positions(picks)
    normed = normalize(state_rows, gain_row)
    row_buffer = scatter_pairs(jnp.repeat(normed, 2, axis=0), flat_index)
    pair_grad = (weights[:, :, None] * upstream.astype(jnp.float32)[:, None, :]).astype(jnp.bfloat16).reshape(TOKENS * 2, D)
    grad_buffer = scatter_pairs(pair_grad, flat_index)

    def one_expert(expert_item):
        rows_in, grad_rows, up_matrix, down_matrix = expert_item
        pre_act = jnp.dot(rows_in, up_matrix, preferred_element_type=jnp.float32)
        act_grad = lax.dot_general(grad_rows, down_matrix, contract_last, preferred_element_type=jnp.float32)
        pre_grad = (act_grad * gelu_slope(pre_act)).astype(jnp.bfloat16)
        return lax.dot_general(pre_grad, up_matrix, contract_last, preferred_element_type=jnp.float32).astype(jnp.bfloat16)
    returned = lax.map(one_expert, (row_buffer, grad_buffer, up_all, down_all)).reshape(-1, D)
    normed_grad = lax.optimization_barrier(jnp.sum(returned[flat_index].reshape(TOKENS, 2, D).astype(jnp.float32), axis=1))
    return norm_backward(upstream, state_rows, normed_grad, gain_row)

def reference(inputs, norm_gain, w_up, w_down, expert_ids, gates, out_grad):
    saved_in = []
    section_outs = []
    for layer in range(SECTIONS):
        saved_in.append([])
        section_outs.append([])
    for batch_index in range(MICRO):
        state_rows = inputs[batch_index]
        for layer in range(SECTIONS):
            saved_in[layer].append(state_rows)
            state_rows = layer_forward(state_rows, norm_gain[layer], w_up[layer], w_down[layer], expert_ids[layer, batch_index], gates[layer, batch_index])
            section_outs[layer].append(state_rows)
    grads_in = []
    for layer in range(SECTIONS):
        grads_in.append([None] * MICRO)
    for batch_index in range(MICRO):
        upstream = out_grad[batch_index]
        for layer in range(SECTIONS - 1, -1, -1):
            upstream = layer_backward(upstream, saved_in[layer][batch_index], norm_gain[layer], w_up[layer], w_down[layer], expert_ids[layer, batch_index], gates[layer, batch_index])
            grads_in[layer][batch_index] = upstream
    section_out = jnp.stack([jnp.stack(section_outs[layer]) for layer in range(SECTIONS)])
    in_grad = jnp.stack([jnp.stack(grads_in[layer]) for layer in range(SECTIONS)])
    return (section_out, in_grad)
```

```python
import functools
import jax
import jax.numpy as jnp
from jax import lax
from jax.experimental import pallas as pl
from jax.experimental.pallas import tpu as pltpu
from jax.sharding import PartitionSpec as P

epsilon = 1e-05
gelu_coef = 0.7978845608028654
cubic_coef = 0.044715
contract_last = (((1,), (1,)), ((), ()))
f32 = jnp.float32
bf16 = jnp.bfloat16
vmem_spec = pl.BlockSpec(memory_space=pltpu.VMEM)
any_spec = pl.BlockSpec(memory_space=pl.ANY)


def gelu_parts(pre):
    square = pre * pre
    tangent = jnp.tanh(gelu_coef * pre * (1.0 + cubic_coef * square))
    half = 0.5 * (1.0 + tangent)
    slope = half + 0.5 * pre * (1.0 - tangent * tangent) * gelu_coef * (
        1.0 + 3.0 * cubic_coef * square
    )
    return pre * half, slope


def inverse_rms(values):
    return lax.rsqrt(jnp.mean(values * values, axis=-1, keepdims=True) + epsilon)


def normalize(values, gain_row):
    return (values * inverse_rms(values) * gain_row).astype(bf16)


def chip_index():
    return lax.axis_index("section") // 2


def core_index():
    return lax.axis_index("section") % 2


def unpack_pairs(returned, targets):
    rows, slots = targets.shape[0], returned.shape[0]
    lanes = lax.broadcasted_iota(jnp.int32, (rows, slots), 1)
    picked = []
    for k in range(2):
        chosen = (targets[:, k : k + 1] == lanes).astype(f32).astype(bf16)
        picked.append(jnp.dot(chosen, returned, preferred_element_type=f32))
    return picked


def slot_hits(targets_t, slots):
    rows = targets_t.shape[1]
    sublanes = lax.broadcasted_iota(jnp.int32, (slots, rows), 0)
    return [targets_t[k : k + 1, :] == sublanes for k in range(2)]


def pack_rows(rows, hits):
    chosen = jnp.where(hits[0] | hits[1], 1.0, 0.0).astype(bf16)
    return jnp.dot(chosen, rows, preferred_element_type=f32)


def slot_gates(hits, gates_t):
    total = jnp.where(hits[0], gates_t[0:1, :], 0.0) + jnp.where(hits[1], gates_t[1:2, :], 0.0)
    return jnp.sum(total, axis=1, keepdims=True)


def small_call(body, out_shapes, args):
    return pl.pallas_call(
        body,
        out_shape=out_shapes,
        in_specs=[vmem_spec] * len(args),
        out_specs=[vmem_spec] * len(out_shapes),
        compiler_params=pltpu.CompilerParams(vmem_limit_bytes=32 * 1024 * 1024),
    )(*args)


def shape_of(rows, columns, kind=bf16):
    return jax.ShapeDtypeStruct((rows, columns), kind)


def first_pack(state, gain, targets_t, grad, grad_targets_t, grad_gates_t, slots, last_chip):
    def body(state_ref, gain_ref, tt_ref, grad_ref, gtt_ref, ggt_ref, out_ref):
        is_last = chip_index() == last_chip

        @pl.when(is_last)
        def _():
            hits = slot_hits(gtt_ref[...], slots)
            out_ref[...] = (
                pack_rows(grad_ref[...], hits) * slot_gates(hits, ggt_ref[...])
            ).astype(bf16)

        @pl.when(jnp.logical_not(is_last))
        def _():
            normed = normalize(state_ref[...].astype(f32), gain_ref[...])
            out_ref[...] = pack_rows(normed, slot_hits(tt_ref[...], slots)).astype(bf16)

    return small_call(
        body,
        [shape_of(slots, state.shape[1])],
        (state, gain, targets_t, grad, grad_targets_t, grad_gates_t),
    )[0]


def select_pack(arrived, state, gain, targets_t, slots, chip):
    def body(arrived_ref, state_ref, gain_ref, tt_ref, state_out, out_ref):
        mine = chip_index() == chip

        @pl.when(mine)
        def _():
            state_out[...] = arrived_ref[...]

        @pl.when(jnp.logical_not(mine))
        def _():
            state_out[...] = state_ref[...]

        normed = normalize(state_out[...].astype(f32), gain_ref[...])
        out_ref[...] = pack_rows(normed, slot_hits(tt_ref[...], slots)).astype(bf16)

    return small_call(
        body,
        [shape_of(*state.shape), shape_of(slots, state.shape[1])],
        (arrived, state, gain, targets_t),
    )


def mix(returned, state, targets, gates):
    first, second = unpack_pairs(returned, targets)
    return (state.astype(f32) + (gates[:, 0:1] * first + gates[:, 1:2] * second)).astype(bf16)


def combine(returned, state, targets, gates):
    def body(ret_ref, state_ref, t_ref, g_ref, out_ref):
        out_ref[...] = mix(ret_ref[...], state_ref[...], t_ref[...], g_ref[...])

    return small_call(body, [shape_of(*state.shape)], (returned, state, targets, gates))[0]


def combine_pack(returned, state, targets, gates, gain, targets_t):
    slots = returned.shape[0]

    def body(ret_ref, state_ref, t_ref, g_ref, gain_ref, tt_ref, state_out, out_ref):
        mixed = mix(ret_ref[...], state_ref[...], t_ref[...], g_ref[...])
        state_out[...] = mixed
        normed = normalize(mixed.astype(f32), gain_ref[...])
        out_ref[...] = pack_rows(normed, slot_hits(tt_ref[...], slots)).astype(bf16)

    return small_call(
        body,
        [shape_of(*state.shape), shape_of(slots, state.shape[1])],
        (returned, state, targets, gates, gain, targets_t),
    )


def grad_mix(returned, upstream, state, targets, gain_row):
    first, second = unpack_pairs(returned, targets)
    values = state.astype(f32)
    inv_rms = inverse_rms(values)
    spread = (first + second) * gain_row
    along = jnp.mean(spread * values, axis=-1, keepdims=True)
    return (
        upstream.astype(f32) + inv_rms * spread - values * inv_rms * inv_rms * inv_rms * along
    ).astype(bf16)


def grad_combine(returned, upstream, state, targets, gain):
    def body(ret_ref, up_ref, state_ref, t_ref, gain_ref, out_ref):
        out_ref[...] = grad_mix(
            ret_ref[...], up_ref[...], state_ref[...], t_ref[...], gain_ref[...]
        )

    return small_call(
        body, [shape_of(*state.shape)], (returned, upstream, state, targets, gain)
    )[0]


def grad_combine_pack(returned, upstream, state, targets, gain, targets_t, gates_t):
    slots = returned.shape[0]

    def body(ret_ref, up_ref, state_ref, t_ref, gain_ref, tt_ref, gt_ref, grad_out, out_ref):
        mixed = grad_mix(ret_ref[...], up_ref[...], state_ref[...], t_ref[...], gain_ref[...])
        grad_out[...] = mixed
        hits = slot_hits(tt_ref[...], slots)
        out_ref[...] = (pack_rows(mixed, hits) * slot_gates(hits, gt_ref[...])).astype(bf16)

    return small_call(
        body,
        [shape_of(*state.shape), shape_of(slots, state.shape[1])],
        (returned, upstream, state, targets, gain, targets_t, gates_t),
    )


def grad_pack(upstream, targets_t, gates_t, slots):
    def body(up_ref, tt_ref, gt_ref, out_ref):
        hits = slot_hits(tt_ref[...], slots)
        out_ref[...] = (pack_rows(up_ref[...], hits) * slot_gates(hits, gt_ref[...])).astype(bf16)

    return small_call(body, [shape_of(slots, upstream.shape[1])], (upstream, targets_t, gates_t))[0]


def tile_width(hidden):
    return 512 if hidden % 512 == 0 else hidden


def weight_copies(parity, own_up, own_down, sib_up, sib_down, up_buf, down_buf, up_sem, down_sem):
    tiles, _, width = up_buf.shape
    own_layer = core_index() == parity

    def up_copy(source, i):
        return pltpu.make_async_copy(
            source.at[:, pl.ds(i * width, width)], up_buf.at[i], up_sem.at[i]
        )

    def down_copy(source, i):
        return pltpu.make_async_copy(
            source.at[pl.ds(i * width, width), :], down_buf.at[i], down_sem.at[i]
        )

    def start_all(up_source, down_source, down_first):
        for i in range(tiles):
            if down_first:
                down_copy(down_source, i).start()
                up_copy(up_source, i).start()
            else:
                up_copy(up_source, i).start()
                down_copy(down_source, i).start()

    def start(down_first):
        @pl.when(own_layer)
        def _():
            start_all(own_up, own_down, down_first)

        @pl.when(jnp.logical_not(own_layer))
        def _():
            start_all(sib_up, sib_down, down_first)

    return start, lambda i: up_copy(own_up, i).wait(), lambda i: down_copy(own_down, i).wait()


def mlp_scratch(features, hidden):
    width = tile_width(hidden)
    tiles = hidden // width
    return [
        pltpu.VMEM((tiles, features, width), bf16),
        pltpu.VMEM((tiles, width, features), bf16),
        pltpu.SemaphoreType.DMA((tiles,)),
        pltpu.SemaphoreType.DMA((tiles,)),
    ]


def mlp_call(body, out_shapes, out_specs, arrays, weights, scratch, flops, moved):
    return pl.pallas_call(
        body,
        out_shape=out_shapes,
        in_specs=[vmem_spec] * len(arrays) + [any_spec] * 4,
        out_specs=out_specs,
        scratch_shapes=scratch,
        compiler_params=pltpu.CompilerParams(vmem_limit_bytes=44 * 1024 * 1024),
        cost_estimate=pl.CostEstimate(flops=flops, bytes_accessed=moved, transcendentals=0),
    )(*arrays, *weights)


def expert_forward(rows, weights, parity, keep_slope):
    slots, features = rows.shape
    hidden = weights[0].shape[1]
    width = tile_width(hidden)
    tiles = hidden // width

    def body(x_ref, *refs):
        hbm, refs = refs[:4], refs[4:]
        if keep_slope:
            out_ref, slope_ref = refs[:2]
            up_buf, down_buf, up_sem, down_sem, acc = refs[2:]
        else:
            out_ref = refs[0]
            up_buf, down_buf, up_sem, down_sem, acc = refs[1:]
        start, wait_up, wait_down = weight_copies(
            parity, *hbm, up_buf, down_buf, up_sem, down_sem
        )
        start(False)
        for i in range(tiles):
            wait_up(i)
            pre = jnp.dot(x_ref[...], up_buf[i], preferred_element_type=f32)
            active, slope = gelu_parts(pre)
            if keep_slope:
                slope_ref[:, i * width : (i + 1) * width] = slope
            wait_down(i)
            part = jnp.dot(active.astype(bf16), down_buf[i], preferred_element_type=f32)
            if i == 0:
                acc[...] = part
            elif i < tiles - 1:
                acc[...] += part
            else:
                out_ref[...] = (acc[...] + part).astype(bf16)

    out_shapes = [shape_of(slots, features)]
    if keep_slope:
        out_shapes.append(shape_of(slots, hidden, f32))
    return mlp_call(
        body,
        out_shapes,
        [vmem_spec] * len(out_shapes),
        (rows,),
        weights,
        mlp_scratch(features, hidden) + [pltpu.VMEM((slots, features), f32)],
        4 * slots * features * hidden,
        4 * features * hidden + 4 * slots * features + 4 * slots * hidden * int(keep_slope),
    )


def expert_backward(grads, slope, weights, parity, other=None, other_chip=None):
    slots, features = grads.shape
    hidden = weights[0].shape[1]
    width = tile_width(hidden)
    tiles = hidden // width
    arrays = (grads, slope) if other is None else (grads, slope, other)

    def body(g_ref, slope_ref, *refs):
        if other is not None:
            other_ref, refs = refs[0], refs[1:]
        hbm, refs = refs[:4], refs[4:]
        out_ref, up_buf, down_buf, up_sem, down_sem, acc = refs
        start, wait_up, wait_down = weight_copies(
            parity, *hbm, up_buf, down_buf, up_sem, down_sem
        )
        start(True)
        for i in range(tiles):
            wait_down(i)
            act_grad = lax.dot_general(
                g_ref[...], down_buf[i], contract_last, preferred_element_type=f32
            )
            pre_grad = (act_grad * slope_ref[:, i * width : (i + 1) * width]).astype(bf16)
            wait_up(i)
            part = lax.dot_general(
                pre_grad, up_buf[i], contract_last, preferred_element_type=f32
            )
            if i == 0:
                acc[...] = part
            elif i < tiles - 1:
                acc[...] += part
            else:
                out_ref[...] = (acc[...] + part).astype(bf16)
        if other is not None:
            @pl.when(chip_index() == other_chip)
            def _():
                out_ref[...] = other_ref[...]

    return mlp_call(
        body,
        [shape_of(slots, features)],
        [vmem_spec],
        arrays,
        weights,
        mlp_scratch(features, hidden) + [pltpu.VMEM((slots, features), f32)],
        4 * slots * features * hidden,
        4 * features * hidden + 4 * slots * features + 4 * slots * hidden,
    )[0]


def act_gradient(grads, weights, parity):
    slots, features = grads.shape
    hidden = weights[0].shape[1]
    width = tile_width(hidden)
    tiles = hidden // width

    def body(g_ref, own_down, sib_down, out_ref, buf, sem):
        own_layer = core_index() == parity

        def copy(source, i):
            return pltpu.make_async_copy(
                source.at[pl.ds(i * width, width), :], buf.at[i], sem.at[i]
            )

        @pl.when(own_layer)
        def _():
            for i in range(tiles):
                copy(own_down, i).start()

        @pl.when(jnp.logical_not(own_layer))
        def _():
            for i in range(tiles):
                copy(sib_down, i).start()

        for i in range(tiles):
            copy(own_down, i).wait()
            out_ref[:, i * width : (i + 1) * width] = lax.dot_general(
                g_ref[...], buf[i], contract_last, preferred_element_type=f32
            )

    return pl.pallas_call(
        body,
        out_shape=shape_of(slots, hidden, f32),
        in_specs=[vmem_spec, any_spec, any_spec],
        out_specs=vmem_spec,
        scratch_shapes=[
            pltpu.VMEM((tiles, width, features), bf16),
            pltpu.SemaphoreType.DMA((tiles,)),
        ],
        compiler_params=pltpu.CompilerParams(vmem_limit_bytes=32 * 1024 * 1024),
        cost_estimate=pl.CostEstimate(
            flops=2 * slots * features * hidden,
            bytes_accessed=2 * features * hidden + 4 * slots * hidden,
            transcendentals=0,
        ),
    )(grads, weights[1], weights[3])


def turn_around(rows, act_grad, weights, parity):
    slots, features = rows.shape
    hidden = weights[0].shape[1]
    width = tile_width(hidden)
    tiles = hidden // width

    def body(x_ref, ag_ref, own_up, sib_up, out_ref, slope_ref, active_ref, buf, sem, acc):
        own_layer = core_index() == parity

        def copy(source, i):
            return pltpu.make_async_copy(
                source.at[:, pl.ds(i * width, width)], buf.at[i], sem.at[i]
            )

        @pl.when(own_layer)
        def _():
            for i in range(tiles):
                copy(own_up, i).start()

        @pl.when(jnp.logical_not(own_layer))
        def _():
            for i in range(tiles):
                copy(sib_up, i).start()

        for i in range(tiles):
            copy(own_up, i).wait()
            columns = slice(i * width, (i + 1) * width)
            pre = jnp.dot(x_ref[...], buf[i], preferred_element_type=f32)
            active, slope = gelu_parts(pre)
            slope_ref[:, columns] = slope
            active_ref[:, columns] = active.astype(bf16)
            pre_grad = (ag_ref[:, columns] * slope).astype(bf16)
            part = lax.dot_general(pre_grad, buf[i], contract_last, preferred_element_type=f32)
            if i == 0:
                acc[...] = part
            elif i < tiles - 1:
                acc[...] += part
            else:
                out_ref[...] = (acc[...] + part).astype(bf16)

    return pl.pallas_call(
        body,
        out_shape=[shape_of(slots, features), shape_of(slots, hidden, f32), shape_of(slots, hidden)],
        in_specs=[vmem_spec, vmem_spec, any_spec, any_spec],
        out_specs=[vmem_spec] * 3,
        scratch_shapes=[
            pltpu.VMEM((tiles, features, width), bf16),
            pltpu.SemaphoreType.DMA((tiles,)),
            pltpu.VMEM((slots, features), f32),
        ],
        compiler_params=pltpu.CompilerParams(vmem_limit_bytes=44 * 1024 * 1024),
        cost_estimate=pl.CostEstimate(
            flops=4 * slots * features * hidden,
            bytes_accessed=2 * features * hidden + 10 * slots * hidden,
            transcendentals=0,
        ),
    )(rows, act_grad, weights[0], weights[2])


def slot_targets(picks_t, experts, capacity):
    rows = picks_t.shape[1]
    onehot = (picks_t[:, :, None] == jnp.arange(experts, dtype=jnp.int32)[None, None, :])
    named = jnp.sum(onehot.astype(f32), axis=0).astype(bf16)
    at = jnp.arange(rows, dtype=jnp.int32)
    earlier = (at[None, :] < at[:, None]).astype(bf16)
    rank = jnp.dot(earlier, named, preferred_element_type=f32)
    rank_of_pick = jnp.sum(jnp.where(onehot, rank[None], 0.0), axis=2).astype(jnp.int32)
    return picks_t * capacity + rank_of_pick


def local(inputs, norm_gain, w_up, w_down, expert_ids, gates, out_grad):
    sections = lax.axis_size("section")
    experts = lax.axis_size("expert")
    chips = sections // 2
    last = chips - 1
    chip, core = chip_index(), core_index()
    batches, rows_dev, features = inputs.shape
    capacity = max(2, 5 * rows_dev // (2 * experts))
    slots = experts * capacity

    def swap_cores(x):
        return lax.ppermute(x, "section", [(s, s ^ 1) for s in range(sections)])

    def shift_chips(x, by):
        return lax.ppermute(
            x, "section", [(s, (s + 2 * by) % sections) for s in range(sections)]
        )

    def to_experts(x):
        return lax.all_to_all(x, "expert", split_axis=0, concat_axis=0, tiled=True)

    folds = features // rows_dev
    small = [
        jnp.concatenate(
            [
                expert_ids[0, m].T.astype(f32),
                gates[0, m].T,
                norm_gain[0].reshape(folds, rows_dev),
            ]
        )
        for m in range(2)
    ]
    own_small = jnp.where(core == 0, small[0], small[1])
    sib_small = swap_cores(jnp.where(core == 0, small[1], small[0]))
    params = []
    for parity in range(2):
        chosen = jnp.where(core == parity, own_small, sib_small)
        targets_t = slot_targets(chosen[:2].astype(jnp.int32), experts, capacity)
        gates_t = chosen[2:4]
        gain = chosen[4:].reshape(1, features)
        params.append((targets_t, targets_t.T, gates_t, gates_t.T, gain))
    (even_tt, even_t, even_gt, even_g, even_gain) = params[0]
    (odd_tt, odd_t, odd_gt, odd_g, odd_gain) = params[1]

    state = jnp.where(core == 0, inputs[0], inputs[1])
    last_grad = jnp.where(core == 0, out_grad[0], out_grad[1])
    own_up, own_down = w_up[0, 0], w_down[0, 0]
    weights = (own_up, own_down, swap_cores(own_up), swap_cores(own_down))

    send = first_pack(state, even_gain, even_tt, last_grad, odd_tt, odd_gt, slots, last)
    odd_out = None
    act_grad = None
    for turn in range(chips):
        if turn > 0:
            arrived = shift_chips(odd_out_now, 1)
            state, send = select_pack(arrived, state, even_gain, even_tt, slots, turn)
        received = to_experts(send)
        if turn < last:
            (outputs,) = expert_forward(received, weights, 0, False)
        else:
            outputs, even_slope = expert_forward(received, weights, 0, True)
        returned = to_experts(outputs)
        if turn == 0:
            act_grad = act_gradient(received, weights, 1)
        middle, send = combine_pack(returned, state, even_t, even_g, odd_gain, odd_tt)
        received = to_experts(send)
        if turn < last:
            (outputs,) = expert_forward(received, weights, 1, False)
            returned = to_experts(outputs)
            odd_out_now = combine(returned, middle, odd_t, odd_g)
            odd_out = (
                odd_out_now if odd_out is None else jnp.where(chip == turn, odd_out_now, odd_out)
            )

    back, odd_slope, odd_active = turn_around(received, act_grad, weights, 1)
    returned = to_experts(back)
    odd_down = jnp.dot(
        odd_active,
        jnp.where(core == 1, weights[1], weights[3]),
        preferred_element_type=f32,
    ).astype(bf16)
    upstream = last_grad
    even_grad = odd_grad = None
    for turn in range(last, -1, -1):
        if turn < last:
            upstream = shift_chips(even_now, -1)
            send = grad_pack(upstream, odd_tt, odd_gt, slots)
            received = to_experts(send)
            if turn == last - 1:
                back = expert_backward(received, odd_slope, weights, 1, odd_down, last)
            else:
                back = expert_backward(received, odd_slope, weights, 1)
            returned = to_experts(back)
            if turn == last - 1:
                final_out = combine(returned, middle, odd_t, odd_g)
                odd_out = jnp.where(chip == last, final_out, odd_out)
        odd_now, send = grad_combine_pack(
            returned, upstream, middle, odd_t, odd_gain, even_tt, even_gt
        )
        odd_grad = odd_now if odd_grad is None else jnp.where(chip == turn, odd_now, odd_grad)
        received = to_experts(send)
        back = expert_backward(received, even_slope, weights, 0)
        returned = to_experts(back)
        even_now = grad_combine(returned, odd_now, state, even_t, even_gain)
        even_grad = even_now if even_grad is None else jnp.where(chip == turn, even_now, even_grad)

    def gather_batches(even, odd):
        own = jnp.where(core == 0, even, odd)
        other = swap_cores(jnp.where(core == 0, odd, even))
        return jnp.where(core == 0, jnp.stack([own, other]), jnp.stack([other, own]))[None]

    return (gather_batches(middle, odd_out), gather_batches(even_grad, odd_grad))


def solution(mesh):
    return jax.shard_map(
        local,
        mesh=mesh,
        in_specs=(
            P(None, "expert", None),
            P("section", None),
            P("section", "expert", None, None),
            P("section", "expert", None, None),
            P("section", None, "expert", None),
            P("section", None, "expert", None),
            P(None, "expert", None),
        ),
        out_specs=(P("section", None, "expert", None), P("section", None, "expert", None)),
        check_vma=False,
    )
```

```python
import jax
import jax.numpy as jnp
from jax import lax
from jax.experimental import pallas as pl
from jax.experimental.pallas import tpu as pltpu
from jax.sharding import PartitionSpec as P

epsilon = 1e-05
gelu_coef = 0.7978845608028654
cubic_coef = 0.044715
contract_last = (((1,), (1,)), ((), ()))
f32 = jnp.float32
bf16 = jnp.bfloat16
vmem_spec = pl.BlockSpec(memory_space=pltpu.VMEM)
any_spec = pl.BlockSpec(memory_space=pl.ANY)
forward_cut = 512
backward_cut = 1024
feature_cut = 512
small_limit = 12 * 1024 * 1024
mlp_limit = 60 * 1024 * 1024


def gelu_parts(pre):
    square = pre * pre
    tangent = jnp.tanh(gelu_coef * pre * (1.0 + cubic_coef * square))
    half = 0.5 * (1.0 + tangent)
    slope = half + 0.5 * pre * (1.0 - tangent * tangent) * gelu_coef * (
        1.0 + 3.0 * cubic_coef * square
    )
    return pre * half, slope


def inverse_rms(values):
    return lax.rsqrt(jnp.mean(values * values, axis=-1, keepdims=True) + epsilon)


def normalize(values, gain_row):
    return (values * inverse_rms(values) * gain_row).astype(bf16)


def chip_index():
    return lax.axis_index("section") // 2


def core_index():
    return lax.axis_index("section") % 2


def unpack_pairs(returned, targets):
    rows, slots = targets.shape[0], returned.shape[0]
    lanes = lax.broadcasted_iota(jnp.int32, (rows, slots), 1)
    picked = []
    for k in range(2):
        chosen = (targets[:, k : k + 1] == lanes).astype(f32).astype(bf16)
        picked.append(jnp.dot(chosen, returned, preferred_element_type=f32))
    return picked


def slot_hits(targets_t, slots):
    rows = targets_t.shape[1]
    sublanes = lax.broadcasted_iota(jnp.int32, (slots, rows), 0)
    return [targets_t[k : k + 1, :] == sublanes for k in range(2)]


def pack_rows(rows, hits):
    chosen = jnp.where(hits[0] | hits[1], 1.0, 0.0).astype(bf16)
    return jnp.dot(chosen, rows, preferred_element_type=f32)


def slot_gates(hits, gates_t):
    total = jnp.where(hits[0], gates_t[0:1, :], 0.0) + jnp.where(hits[1], gates_t[1:2, :], 0.0)
    return jnp.sum(total, axis=1, keepdims=True)


def small_call(body, out_shapes, args):
    return pl.pallas_call(
        body,
        out_shape=out_shapes,
        in_specs=[vmem_spec] * len(args),
        out_specs=[vmem_spec] * len(out_shapes),
        compiler_params=pltpu.CompilerParams(vmem_limit_bytes=small_limit),
    )(*args)


def shape_of(rows, columns, kind=bf16):
    return jax.ShapeDtypeStruct((rows, columns), kind)


def first_pack(state, gain, targets_t, grad, grad_targets_t, grad_gates_t, slots, last_chip):
    def body(state_ref, gain_ref, tt_ref, grad_ref, gtt_ref, ggt_ref, out_ref):
        is_last = chip_index() == last_chip

        @pl.when(is_last)
        def _():
            hits = slot_hits(gtt_ref[...], slots)
            out_ref[...] = (
                pack_rows(grad_ref[...], hits) * slot_gates(hits, ggt_ref[...])
            ).astype(bf16)

        @pl.when(jnp.logical_not(is_last))
        def _():
            normed = normalize(state_ref[...].astype(f32), gain_ref[...])
            out_ref[...] = pack_rows(normed, slot_hits(tt_ref[...], slots)).astype(bf16)

    return small_call(
        body,
        [shape_of(slots, state.shape[1])],
        (state, gain, targets_t, grad, grad_targets_t, grad_gates_t),
    )[0]


def select_pack(arrived, state, gain, targets_t, slots, chip):
    def body(arrived_ref, state_ref, gain_ref, tt_ref, state_out, out_ref):
        mine = chip_index() == chip

        @pl.when(mine)
        def _():
            state_out[...] = arrived_ref[...]

        @pl.when(jnp.logical_not(mine))
        def _():
            state_out[...] = state_ref[...]

        normed = normalize(state_out[...].astype(f32), gain_ref[...])
        out_ref[...] = pack_rows(normed, slot_hits(tt_ref[...], slots)).astype(bf16)

    return small_call(
        body,
        [shape_of(*state.shape), shape_of(slots, state.shape[1])],
        (arrived, state, gain, targets_t),
    )


def mix(returned, state, targets, gates):
    first, second = unpack_pairs(returned, targets)
    return (state.astype(f32) + (gates[:, 0:1] * first + gates[:, 1:2] * second)).astype(bf16)


def combine(returned, state, targets, gates):
    def body(ret_ref, state_ref, t_ref, g_ref, out_ref):
        out_ref[...] = mix(ret_ref[...], state_ref[...], t_ref[...], g_ref[...])

    return small_call(body, [shape_of(*state.shape)], (returned, state, targets, gates))[0]


def combine_pack(returned, state, targets, gates, gain, targets_t):
    slots = returned.shape[0]

    def body(ret_ref, state_ref, t_ref, g_ref, gain_ref, tt_ref, state_out, out_ref):
        mixed = mix(ret_ref[...], state_ref[...], t_ref[...], g_ref[...])
        state_out[...] = mixed
        normed = normalize(mixed.astype(f32), gain_ref[...])
        out_ref[...] = pack_rows(normed, slot_hits(tt_ref[...], slots)).astype(bf16)

    return small_call(
        body,
        [shape_of(*state.shape), shape_of(slots, state.shape[1])],
        (returned, state, targets, gates, gain, targets_t),
    )


def grad_mix(returned, upstream, state, targets, gain_row):
    first, second = unpack_pairs(returned, targets)
    values = state.astype(f32)
    inv_rms = inverse_rms(values)
    spread = (first + second) * gain_row
    along = jnp.mean(spread * values, axis=-1, keepdims=True)
    return (
        upstream.astype(f32) + inv_rms * spread - values * inv_rms * inv_rms * inv_rms * along
    ).astype(bf16)


def grad_combine(returned, upstream, state, targets, gain):
    def body(ret_ref, up_ref, state_ref, t_ref, gain_ref, out_ref):
        out_ref[...] = grad_mix(
            ret_ref[...], up_ref[...], state_ref[...], t_ref[...], gain_ref[...]
        )

    return small_call(
        body, [shape_of(*state.shape)], (returned, upstream, state, targets, gain)
    )[0]


def grad_combine_pack(returned, upstream, state, targets, gain, targets_t, gates_t):
    slots = returned.shape[0]

    def body(ret_ref, up_ref, state_ref, t_ref, gain_ref, tt_ref, gt_ref, grad_out, out_ref):
        mixed = grad_mix(ret_ref[...], up_ref[...], state_ref[...], t_ref[...], gain_ref[...])
        grad_out[...] = mixed
        hits = slot_hits(tt_ref[...], slots)
        out_ref[...] = (pack_rows(mixed, hits) * slot_gates(hits, gt_ref[...])).astype(bf16)

    return small_call(
        body,
        [shape_of(*state.shape), shape_of(slots, state.shape[1])],
        (returned, upstream, state, targets, gain, targets_t, gates_t),
    )


def grad_pack(upstream, targets_t, gates_t, slots):
    def body(up_ref, tt_ref, gt_ref, out_ref):
        hits = slot_hits(tt_ref[...], slots)
        out_ref[...] = (pack_rows(up_ref[...], hits) * slot_gates(hits, gt_ref[...])).astype(bf16)

    return small_call(body, [shape_of(slots, upstream.shape[1])], (upstream, targets_t, gates_t))[0]


def cuts(size, width):
    width = width if size % width == 0 else size
    return [slice(at, at + width) for at in range(0, size, width)]


class TileCopies:
    def __init__(self, where, semaphores):
        self.where = where
        self.semaphores = semaphores

    def copy(self, source, target, i):
        at = self.where[i]
        return pltpu.make_async_copy(source.at[at], target.at[at], self.semaphores.at[i])


def start_from(parity, own, sibling, begin):
    own_layer = core_index() == parity

    @pl.when(own_layer)
    def _():
        begin(*own)

    @pl.when(jnp.logical_not(own_layer))
    def _():
        begin(*sibling)


def column_tiles(size, width):
    return [(slice(None), cut) for cut in cuts(size, width)]


def row_tiles(size, width):
    return [(cut, slice(None)) for cut in cuts(size, width)]


def mlp_call(body, out_shapes, arrays, scratch, flops, moved):
    return pl.pallas_call(
        body,
        out_shape=out_shapes,
        in_specs=[any_spec] * len(arrays),
        out_specs=[any_spec] * len(out_shapes),
        scratch_shapes=scratch,
        compiler_params=pltpu.CompilerParams(vmem_limit_bytes=mlp_limit),
        cost_estimate=pl.CostEstimate(flops=flops, bytes_accessed=moved, transcendentals=0),
    )(*arrays)


def copy_slots(tiles):
    return pltpu.SemaphoreType.DMA((len(tiles),))


def expert_forward(rows, weights, parity, keep_slope):
    slots, features = rows.shape
    hidden = weights[0].shape[1]
    up_tiles, down_tiles = column_tiles(hidden, forward_cut), column_tiles(features, feature_cut)

    def body(rows_ref, own_up, own_down, sib_up, sib_down, out_ref, *refs):
        if keep_slope:
            slope_ref, refs = refs[0], refs[1:]
            slope_buf, slope_sem = refs[-2:]
            slope_out = TileCopies(up_tiles, slope_sem)
        up_buf, down_buf, active, x_ref, out_buf, up_sem, down_sem, x_sem, out_sem = refs[:9]
        rows_in = pltpu.make_async_copy(rows_ref, x_ref, x_sem)
        rows_in.start()
        rows_out = TileCopies(down_tiles, out_sem)
        up_in, down_in = TileCopies(up_tiles, up_sem), TileCopies(down_tiles, down_sem)

        def begin_up(up):
            for i in range(len(up_tiles)):
                up_in.copy(up, up_buf, i).start()

        def begin_down(down):
            for i in range(len(down_tiles)):
                down_in.copy(down, down_buf, i).start()

        start_from(parity, (own_up,), (sib_up,), begin_up)
        for i, at in enumerate(up_tiles):
            up_in.copy(own_up, up_buf, i).wait()
            if i == 0:
                rows_in.wait()
                start_from(parity, (own_down,), (sib_down,), begin_down)
            pre = jnp.dot(x_ref[...], up_buf[at], preferred_element_type=f32)
            value, slope = gelu_parts(pre)
            active[at] = value.astype(bf16)
            if keep_slope:
                slope_buf[at] = slope
                slope_out.copy(slope_buf, slope_ref, i).start()
        for i, at in enumerate(down_tiles):
            down_in.copy(own_down, down_buf, i).wait()
            out_buf[at] = jnp.dot(active[...], down_buf[at], preferred_element_type=f32).astype(bf16)
            rows_out.copy(out_buf, out_ref, i).start()
        for i in range(len(down_tiles)):
            rows_out.copy(out_buf, out_ref, i).wait()
        if keep_slope:
            for i in range(len(up_tiles)):
                slope_out.copy(slope_buf, slope_ref, i).wait()

    out_shapes = [shape_of(slots, features)]
    scratch = [
        pltpu.VMEM((features, hidden), bf16),
        pltpu.VMEM((hidden, features), bf16),
        pltpu.VMEM((slots, hidden), bf16),
        pltpu.VMEM((slots, features), bf16),
        pltpu.VMEM((slots, features), bf16),
        copy_slots(up_tiles),
        copy_slots(down_tiles),
        pltpu.SemaphoreType.DMA,
        copy_slots(down_tiles),
    ]
    if keep_slope:
        out_shapes.append(shape_of(slots, hidden, f32))
        scratch += [pltpu.VMEM((slots, hidden), f32), copy_slots(up_tiles)]
    return mlp_call(
        body,
        out_shapes,
        (rows, *weights),
        scratch,
        4 * slots * features * hidden,
        4 * features * hidden + 4 * slots * features + 4 * slots * hidden * int(keep_slope),
    )


def expert_backward(grads, slope, weights, parity, other=None, other_chip=None):
    slots, features = grads.shape
    hidden = weights[0].shape[1]
    down_tiles, up_tiles = row_tiles(hidden, backward_cut), row_tiles(features, feature_cut)
    slope_tiles = column_tiles(hidden, backward_cut)
    out_tiles = column_tiles(features, feature_cut)
    arrays = (grads,) if other is None else (grads, other)

    def body(grads_ref, *refs):
        if other is not None:
            other_ref, refs = refs[0], refs[1:]
        own_up, own_down, sib_up, sib_down, slope_ref, out_ref = refs[:6]
        up_buf, down_buf, slope_buf, pre_grad, g_ref, out_buf = refs[6:12]
        up_sem, down_sem, slope_sem, g_sem, out_sem = refs[12:17]
        if other is not None:
            other_buf = refs[17]
        grads_in = pltpu.make_async_copy(grads_ref, g_ref, g_sem)
        grads_in.start()
        rows_out = TileCopies(out_tiles, out_sem)
        up_in, down_in = TileCopies(up_tiles, up_sem), TileCopies(down_tiles, down_sem)
        slope_in = TileCopies(slope_tiles, slope_sem)

        def begin_down(down):
            for i in range(len(down_tiles)):
                down_in.copy(down, down_buf, i).start()
                slope_in.copy(slope_ref, slope_buf, i).start()

        def begin_up(up):
            for i in range(len(up_tiles)):
                up_in.copy(up, up_buf, i).start()

        start_from(parity, (own_down,), (sib_down,), begin_down)
        for i, at in enumerate(down_tiles):
            down_in.copy(own_down, down_buf, i).wait()
            if i == 0:
                grads_in.wait()
                start_from(parity, (own_up,), (sib_up,), begin_up)
                if other is not None:
                    pltpu.make_async_copy(other_ref, other_buf, g_sem).start()
            act_grad = lax.dot_general(
                g_ref[...], down_buf[at], contract_last, preferred_element_type=f32
            )
            slope_in.copy(slope_ref, slope_buf, i).wait()
            pre_grad[slope_tiles[i]] = (act_grad * slope_buf[slope_tiles[i]]).astype(bf16)
        for i, at in enumerate(up_tiles):
            up_in.copy(own_up, up_buf, i).wait()
            out_buf[out_tiles[i]] = lax.dot_general(
                pre_grad[...], up_buf[at], contract_last, preferred_element_type=f32
            ).astype(bf16)
            if other is None:
                rows_out.copy(out_buf, out_ref, i).start()
        if other is None:
            for i in range(len(out_tiles)):
                rows_out.copy(out_buf, out_ref, i).wait()
        else:
            whole = out_sem.at[0]
            pltpu.make_async_copy(other_ref, other_buf, g_sem).wait()

            @pl.when(chip_index() == other_chip)
            def _():
                pltpu.make_async_copy(other_buf, out_ref, whole).start()

            @pl.when(chip_index() != other_chip)
            def _():
                pltpu.make_async_copy(out_buf, out_ref, whole).start()

            pltpu.make_async_copy(out_buf, out_ref, whole).wait()

    return mlp_call(
        body,
        [shape_of(slots, features)],
        (*arrays, *weights, slope),
        [
            pltpu.VMEM((features, hidden), bf16),
            pltpu.VMEM((hidden, features), bf16),
            pltpu.VMEM((slots, hidden), f32),
            pltpu.VMEM((slots, hidden), bf16),
            pltpu.VMEM((slots, features), bf16),
            pltpu.VMEM((slots, features), bf16),
            copy_slots(up_tiles),
            copy_slots(down_tiles),
            copy_slots(slope_tiles),
            pltpu.SemaphoreType.DMA,
            copy_slots(out_tiles),
        ]
        + ([] if other is None else [pltpu.VMEM((slots, features), bf16)]),
        4 * slots * features * hidden,
        4 * features * hidden + 4 * slots * features + 4 * slots * hidden,
    )[0]


def act_gradient(grads, weights, parity):
    slots, features = grads.shape
    hidden = weights[0].shape[1]
    down_tiles, out_tiles = row_tiles(hidden, backward_cut), column_tiles(hidden, backward_cut)

    def body(grads_ref, own_down, sib_down, out_ref, down_buf, g_ref, out_buf, down_sem, g_sem, out_sem):
        grads_in = pltpu.make_async_copy(grads_ref, g_ref, g_sem)
        grads_in.start()
        down_in, grads_out = TileCopies(down_tiles, down_sem), TileCopies(out_tiles, out_sem)

        def begin(down):
            for i in range(len(down_tiles)):
                down_in.copy(down, down_buf, i).start()

        start_from(parity, (own_down,), (sib_down,), begin)
        for i, at in enumerate(down_tiles):
            down_in.copy(own_down, down_buf, i).wait()
            if i == 0:
                grads_in.wait()
            out_buf[out_tiles[i]] = lax.dot_general(
                g_ref[...], down_buf[at], contract_last, preferred_element_type=f32
            )
            grads_out.copy(out_buf, out_ref, i).start()
        for i in range(len(out_tiles)):
            grads_out.copy(out_buf, out_ref, i).wait()

    return mlp_call(
        body,
        [shape_of(slots, hidden, f32)],
        (grads, weights[1], weights[3]),
        [
            pltpu.VMEM((hidden, features), bf16),
            pltpu.VMEM((slots, features), bf16),
            pltpu.VMEM((slots, hidden), f32),
            copy_slots(down_tiles),
            pltpu.SemaphoreType.DMA,
            copy_slots(out_tiles),
        ],
        2 * slots * features * hidden,
        2 * features * hidden + 4 * slots * hidden,
    )[0]


def turn_around(rows, act_grad, weights, parity):
    slots, features = rows.shape
    hidden = weights[0].shape[1]
    tiles, out_tiles = column_tiles(hidden, backward_cut), column_tiles(features, feature_cut)
    up_rows = row_tiles(features, feature_cut)

    def body(rows_ref, own_up, sib_up, ag_ref, out_ref, slope_ref, active_ref, *refs):
        up_buf, ag_buf, slope_buf, active_buf, pre_grad, x_ref, out_buf = refs[:7]
        up_in, grad_in, slope_out, active_out = [TileCopies(tiles, sem) for sem in refs[7:11]]
        rows_out = TileCopies(out_tiles, refs[11])
        rows_in = pltpu.make_async_copy(rows_ref, x_ref, refs[12])
        rows_in.start()

        def begin(up):
            for i in range(len(tiles)):
                up_in.copy(up, up_buf, i).start()
                grad_in.copy(ag_ref, ag_buf, i).start()

        start_from(parity, (own_up,), (sib_up,), begin)
        for i, at in enumerate(tiles):
            up_in.copy(own_up, up_buf, i).wait()
            if i == 0:
                rows_in.wait()
            pre = jnp.dot(x_ref[...], up_buf[at], preferred_element_type=f32)
            value, slope = gelu_parts(pre)
            slope_buf[at] = slope
            active_buf[at] = value.astype(bf16)
            slope_out.copy(slope_buf, slope_ref, i).start()
            active_out.copy(active_buf, active_ref, i).start()
            grad_in.copy(ag_ref, ag_buf, i).wait()
            pre_grad[at] = (ag_buf[at] * slope).astype(bf16)
        for i, (at, rows_at) in enumerate(zip(out_tiles, up_rows)):
            out_buf[at] = lax.dot_general(
                pre_grad[...], up_buf[rows_at], contract_last, preferred_element_type=f32
            ).astype(bf16)
            rows_out.copy(out_buf, out_ref, i).start()
        for i in range(len(out_tiles)):
            rows_out.copy(out_buf, out_ref, i).wait()
        for i in range(len(tiles)):
            slope_out.copy(slope_buf, slope_ref, i).wait()
            active_out.copy(active_buf, active_ref, i).wait()

    return mlp_call(
        body,
        [shape_of(slots, features), shape_of(slots, hidden, f32), shape_of(slots, hidden)],
        (rows, weights[0], weights[2], act_grad),
        [
            pltpu.VMEM((features, hidden), bf16),
            pltpu.VMEM((slots, hidden), f32),
            pltpu.VMEM((slots, hidden), f32),
            pltpu.VMEM((slots, hidden), bf16),
            pltpu.VMEM((slots, hidden), bf16),
            pltpu.VMEM((slots, features), bf16),
            pltpu.VMEM((slots, features), bf16),
            copy_slots(tiles),
            copy_slots(tiles),
            copy_slots(tiles),
            copy_slots(tiles),
            copy_slots(out_tiles),
            pltpu.SemaphoreType.DMA,
        ],
        4 * slots * features * hidden,
        2 * features * hidden + 10 * slots * hidden,
    )


def slot_targets(picks_t, experts, capacity):
    rows = picks_t.shape[1]
    onehot = (picks_t[:, :, None] == jnp.arange(experts, dtype=jnp.int32)[None, None, :])
    named = jnp.sum(onehot.astype(f32), axis=0).astype(bf16)
    at = jnp.arange(rows, dtype=jnp.int32)
    earlier = (at[None, :] < at[:, None]).astype(bf16)
    rank = jnp.dot(earlier, named, preferred_element_type=f32)
    rank_of_pick = jnp.sum(jnp.where(onehot, rank[None], 0.0), axis=2).astype(jnp.int32)
    return picks_t * capacity + rank_of_pick


def local(inputs, norm_gain, w_up, w_down, expert_ids, gates, out_grad):
    sections = lax.axis_size("section")
    experts = lax.axis_size("expert")
    chips = sections // 2
    last = chips - 1
    chip, core = chip_index(), core_index()
    batches, rows_dev, features = inputs.shape
    capacity = max(2, 5 * rows_dev // (2 * experts))
    slots = experts * capacity

    def swap_cores(x):
        return lax.ppermute(x, "section", [(s, s ^ 1) for s in range(sections)])

    def shift_chips(x, by):
        return lax.ppermute(
            x, "section", [(s, (s + 2 * by) % sections) for s in range(sections)]
        )

    def to_experts(x):
        return lax.all_to_all(x, "expert", split_axis=0, concat_axis=0, tiled=True)

    folds = features // rows_dev
    small = [
        jnp.concatenate(
            [
                expert_ids[0, m].T.astype(f32),
                gates[0, m].T,
                norm_gain[0].reshape(folds, rows_dev),
            ]
        )
        for m in range(2)
    ]
    own_small = jnp.where(core == 0, small[0], small[1])
    sib_small = swap_cores(jnp.where(core == 0, small[1], small[0]))
    params = []
    for parity in range(2):
        chosen = jnp.where(core == parity, own_small, sib_small)
        targets_t = slot_targets(chosen[:2].astype(jnp.int32), experts, capacity)
        gates_t = chosen[2:4]
        gain = chosen[4:].reshape(1, features)
        params.append((targets_t, targets_t.T, gates_t, gates_t.T, gain))
    (even_tt, even_t, even_gt, even_g, even_gain) = params[0]
    (odd_tt, odd_t, odd_gt, odd_g, odd_gain) = params[1]

    state = jnp.where(core == 0, inputs[0], inputs[1])
    last_grad = jnp.where(core == 0, out_grad[0], out_grad[1])
    own_up, own_down = w_up[0, 0], w_down[0, 0]
    weights = (own_up, own_down, swap_cores(own_up), swap_cores(own_down))

    send = first_pack(state, even_gain, even_tt, last_grad, odd_tt, odd_gt, slots, last)
    odd_out = None
    act_grad = None
    for turn in range(chips):
        if turn > 0:
            arrived = shift_chips(odd_out_now, 1)
            state, send = select_pack(arrived, state, even_gain, even_tt, slots, turn)
        received = to_experts(send)
        if turn < last:
            (outputs,) = expert_forward(received, weights, 0, False)
        else:
            outputs, even_slope = expert_forward(received, weights, 0, True)
        returned = to_experts(outputs)
        if turn == 0:
            act_grad = act_gradient(received, weights, 1)
        middle, send = combine_pack(returned, state, even_t, even_g, odd_gain, odd_tt)
        received = to_experts(send)
        if turn < last:
            (outputs,) = expert_forward(received, weights, 1, False)
            returned = to_experts(outputs)
            odd_out_now = combine(returned, middle, odd_t, odd_g)
            odd_out = (
                odd_out_now if odd_out is None else jnp.where(chip == turn, odd_out_now, odd_out)
            )

    back, odd_slope, odd_active = turn_around(received, act_grad, weights, 1)
    returned = to_experts(back)
    odd_down = jnp.dot(
        odd_active,
        jnp.where(core == 1, weights[1], weights[3]),
        preferred_element_type=f32,
    ).astype(bf16)
    upstream = last_grad
    even_grad = odd_grad = None
    for turn in range(last, -1, -1):
        if turn < last:
            upstream = shift_chips(even_now, -1)
            send = grad_pack(upstream, odd_tt, odd_gt, slots)
            received = to_experts(send)
            if turn == last - 1:
                back = expert_backward(received, odd_slope, weights, 1, odd_down, last)
            else:
                back = expert_backward(received, odd_slope, weights, 1)
            returned = to_experts(back)
            if turn == last - 1:
                final_out = combine(returned, middle, odd_t, odd_g)
                odd_out = jnp.where(chip == last, final_out, odd_out)
        odd_now, send = grad_combine_pack(
            returned, upstream, middle, odd_t, odd_gain, even_tt, even_gt
        )
        odd_grad = odd_now if odd_grad is None else jnp.where(chip == turn, odd_now, odd_grad)
        received = to_experts(send)
        back = expert_backward(received, even_slope, weights, 0)
        returned = to_experts(back)
        even_now = grad_combine(returned, odd_now, state, even_t, even_gain)
        even_grad = even_now if even_grad is None else jnp.where(chip == turn, even_now, even_grad)

    def gather_batches(even, odd):
        own = jnp.where(core == 0, even, odd)
        other = swap_cores(jnp.where(core == 0, odd, even))
        return jnp.where(core == 0, jnp.stack([own, other]), jnp.stack([other, own]))[None]

    return (gather_batches(middle, odd_out), gather_batches(even_grad, odd_grad))


def solution(mesh):
    return jax.shard_map(
        local,
        mesh=mesh,
        in_specs=(
            P(None, "expert", None),
            P("section", None),
            P("section", "expert", None, None),
            P("section", "expert", None, None),
            P("section", None, "expert", None),
            P("section", None, "expert", None),
            P(None, "expert", None),
        ),
        out_specs=(P("section", None, "expert", None), P("section", None, "expert", None)),
        check_vma=False,
    )
```

```python
import jax
import jax.numpy as jnp
from jax import lax
from jax.experimental import pallas as pl
from jax.experimental.pallas import tpu as pltpu
from jax.sharding import PartitionSpec as P

epsilon = 1e-05
gelu_coef = 0.7978845608028654
cubic_coef = 0.044715
contract_last = (((1,), (1,)), ((), ()))
f32 = jnp.float32
bf16 = jnp.bfloat16
vmem_spec = pl.BlockSpec(memory_space=pltpu.VMEM)
any_spec = pl.BlockSpec(memory_space=pl.ANY)
forward_cut = 512
backward_cut = 1024
feature_cut = 512
small_limit = 12 * 1024 * 1024
mlp_limit = 60 * 1024 * 1024


def gelu_parts(pre):
    square = pre * pre
    tangent = jnp.tanh(gelu_coef * pre * (1.0 + cubic_coef * square))
    half = 0.5 * (1.0 + tangent)
    slope = half + 0.5 * pre * (1.0 - tangent * tangent) * gelu_coef * (
        1.0 + 3.0 * cubic_coef * square
    )
    return pre * half, slope


def inverse_rms(values):
    return lax.rsqrt(jnp.mean(values * values, axis=-1, keepdims=True) + epsilon)


def normalize(values, gain_row):
    return (values * inverse_rms(values) * gain_row).astype(bf16)


def chip_index():
    return lax.axis_index("section") // 2


def core_index():
    return lax.axis_index("section") % 2


def unpack_pairs(returned, targets):
    rows, slots = targets.shape[0], returned.shape[0]
    lanes = lax.broadcasted_iota(jnp.int32, (rows, slots), 1)
    picked = []
    for k in range(2):
        chosen = (targets[:, k : k + 1] == lanes).astype(f32).astype(bf16)
        picked.append(jnp.dot(chosen, returned, preferred_element_type=f32))
    return picked


def slot_hits(targets_t, slots):
    rows = targets_t.shape[1]
    sublanes = lax.broadcasted_iota(jnp.int32, (slots, rows), 0)
    return [targets_t[k : k + 1, :] == sublanes for k in range(2)]


def pack_rows(rows, hits):
    chosen = jnp.where(hits[0] | hits[1], 1.0, 0.0).astype(bf16)
    return jnp.dot(chosen, rows, preferred_element_type=f32)


def slot_gates(hits, gates_t):
    total = jnp.where(hits[0], gates_t[0:1, :], 0.0) + jnp.where(hits[1], gates_t[1:2, :], 0.0)
    return jnp.sum(total, axis=1, keepdims=True)


def small_call(body, out_shapes, args):
    return pl.pallas_call(
        body,
        out_shape=out_shapes,
        in_specs=[vmem_spec] * len(args),
        out_specs=[vmem_spec] * len(out_shapes),
        compiler_params=pltpu.CompilerParams(vmem_limit_bytes=small_limit),
    )(*args)


def shape_of(rows, columns, kind=bf16):
    return jax.ShapeDtypeStruct((rows, columns), kind)


def gather_params(ids_t, gates_t, gain):
    def body(ids_hbm, gates_hbm, gain_hbm, own_ref, send_ref, ids_ref, gates_ref, gain_ref, sem):
        copies = [
            pltpu.make_async_copy(source, target, sem.at[i])
            for i, (source, target) in enumerate(
                ((ids_hbm, ids_ref), (gates_hbm, gates_ref), (gain_hbm, gain_ref))
            )
        ]
        for copy in copies:
            copy.start()
        for copy in copies:
            copy.wait()
        for out_ref, batch in ((own_ref, core_index()), (send_ref, 1 - core_index())):
            out_ref[0:2] = ids_ref[batch].astype(f32)
            out_ref[2:4] = gates_ref[batch]
            out_ref[4:] = gain_ref[...]

    rows = 4 + gain.shape[0]
    return pl.pallas_call(
        body,
        out_shape=[shape_of(rows, gain.shape[1], f32)] * 2,
        in_specs=[any_spec] * 3,
        out_specs=[vmem_spec] * 2,
        scratch_shapes=[
            pltpu.VMEM(ids_t.shape, jnp.int32),
            pltpu.VMEM(gates_t.shape, f32),
            pltpu.VMEM(gain.shape, f32),
            pltpu.SemaphoreType.DMA((3,)),
        ],
        compiler_params=pltpu.CompilerParams(vmem_limit_bytes=mlp_limit),
    )(ids_t, gates_t, gain)


def as_column(row):
    size = row.shape[1]
    down = lax.broadcasted_iota(jnp.int32, (size, size), 0)
    across = lax.broadcasted_iota(jnp.int32, (size, size), 1)
    return jnp.sum(jnp.where(down == across, row, 0.0), axis=1, keepdims=True)


def slot_rows(ids_t, experts, capacity):
    rows = ids_t.shape[1]
    expert = lax.broadcasted_iota(jnp.int32, (experts, rows), 0).astype(f32)
    hits = [(ids_t[k : k + 1, :] == expert).astype(f32) for k in range(2)]
    before = lax.broadcasted_iota(jnp.int32, (rows, rows), 0)
    after = lax.broadcasted_iota(jnp.int32, (rows, rows), 1)
    earlier = (before < after).astype(f32)
    rank = jnp.dot(hits[0] + hits[1], earlier, preferred_element_type=f32)
    return [
        ids_t[k : k + 1, :] * float(capacity) + jnp.sum(hits[k] * rank, axis=0, keepdims=True)
        for k in range(2)
    ]


def prepare_pack(own_small, sib_small, inputs, out_grad, experts, capacity, last_chip):
    rows, features = inputs.shape[1:]
    slots = experts * capacity
    params = [
        jax.ShapeDtypeStruct((2, rows), jnp.int32),
        jax.ShapeDtypeStruct((rows, 2), jnp.int32),
        shape_of(2, rows, f32),
        shape_of(rows, 2, f32),
        shape_of(1, features, f32),
    ]

    def body(own_ref, sib_ref, inputs_ref, out_grad_ref, *refs):
        even, odd = refs[:5], refs[5:10]
        state_ref, grad_ref, out_ref, sem = refs[10:]
        state_in = pltpu.make_async_copy(inputs_ref.at[core_index()], state_ref, sem.at[0])
        grad_in = pltpu.make_async_copy(out_grad_ref.at[core_index()], grad_ref, sem.at[1])
        state_in.start()
        grad_in.start()
        for parity, (tt_ref, t_ref, gt_ref, g_ref, gain_ref) in ((0, even), (1, odd)):
            chosen = jnp.where(core_index() == parity, own_ref[...], sib_ref[...])
            gt_ref[...] = chosen[2:4]
            at = slot_rows(chosen[0:2], experts, capacity)
            for k in range(2):
                tt_ref[k : k + 1, :] = at[k].astype(jnp.int32)
                t_ref[:, k : k + 1] = as_column(at[k]).astype(jnp.int32)
                g_ref[:, k : k + 1] = as_column(chosen[2 + k : 3 + k])
            for i in range(features // rows):
                gain_ref[:, i * rows : (i + 1) * rows] = chosen[4 + i : 5 + i]
        state_in.wait()
        grad_in.wait()
        is_last = chip_index() == last_chip

        @pl.when(is_last)
        def _():
            hits = slot_hits(odd[0][...], slots)
            out_ref[...] = (
                pack_rows(grad_ref[...], hits) * slot_gates(hits, odd[2][...])
            ).astype(bf16)

        @pl.when(jnp.logical_not(is_last))
        def _():
            normed = normalize(state_ref[...].astype(f32), even[4][...])
            out_ref[...] = pack_rows(normed, slot_hits(even[0][...], slots)).astype(bf16)

    out_shapes = params + params + [shape_of(rows, features)] * 2 + [shape_of(slots, features)]
    made = pl.pallas_call(
        body,
        out_shape=out_shapes,
        in_specs=[vmem_spec, vmem_spec, any_spec, any_spec],
        out_specs=[vmem_spec] * len(out_shapes),
        scratch_shapes=[pltpu.SemaphoreType.DMA((2,))],
        compiler_params=pltpu.CompilerParams(vmem_limit_bytes=small_limit),
    )(own_small, sib_small, inputs, out_grad)
    return made[:5], made[5:10], made[10], made[11], made[12]


def select_pack(arrived, state, gain, targets_t, slots, chip):
    def body(arrived_ref, state_ref, gain_ref, tt_ref, state_out, out_ref):
        mine = chip_index() == chip

        @pl.when(mine)
        def _():
            state_out[...] = arrived_ref[...]

        @pl.when(jnp.logical_not(mine))
        def _():
            state_out[...] = state_ref[...]

        normed = normalize(state_out[...].astype(f32), gain_ref[...])
        out_ref[...] = pack_rows(normed, slot_hits(tt_ref[...], slots)).astype(bf16)

    return small_call(
        body,
        [shape_of(*state.shape), shape_of(slots, state.shape[1])],
        (arrived, state, gain, targets_t),
    )


def mix(returned, state, targets, gates):
    first, second = unpack_pairs(returned, targets)
    return (state.astype(f32) + (gates[:, 0:1] * first + gates[:, 1:2] * second)).astype(bf16)


def combine(returned, state, targets, gates):
    def body(ret_ref, state_ref, t_ref, g_ref, out_ref):
        out_ref[...] = mix(ret_ref[...], state_ref[...], t_ref[...], g_ref[...])

    return small_call(body, [shape_of(*state.shape)], (returned, state, targets, gates))[0]


def combine_pack(returned, state, targets, gates, gain, targets_t):
    slots = returned.shape[0]

    def body(ret_ref, state_ref, t_ref, g_ref, gain_ref, tt_ref, state_out, out_ref):
        mixed = mix(ret_ref[...], state_ref[...], t_ref[...], g_ref[...])
        state_out[...] = mixed
        normed = normalize(mixed.astype(f32), gain_ref[...])
        out_ref[...] = pack_rows(normed, slot_hits(tt_ref[...], slots)).astype(bf16)

    return small_call(
        body,
        [shape_of(*state.shape), shape_of(slots, state.shape[1])],
        (returned, state, targets, gates, gain, targets_t),
    )


def grad_mix(returned, upstream, state, targets, gain_row):
    first, second = unpack_pairs(returned, targets)
    values = state.astype(f32)
    inv_rms = inverse_rms(values)
    spread = (first + second) * gain_row
    along = jnp.mean(spread * values, axis=-1, keepdims=True)
    return (
        upstream.astype(f32) + inv_rms * spread - values * inv_rms * inv_rms * inv_rms * along
    ).astype(bf16)


def grad_combine(returned, upstream, state, targets, gain):
    def body(ret_ref, up_ref, state_ref, t_ref, gain_ref, out_ref):
        out_ref[...] = grad_mix(
            ret_ref[...], up_ref[...], state_ref[...], t_ref[...], gain_ref[...]
        )

    return small_call(
        body, [shape_of(*state.shape)], (returned, upstream, state, targets, gain)
    )[0]


def grad_combine_pack(returned, upstream, state, targets, gain, targets_t, gates_t):
    slots = returned.shape[0]

    def body(ret_ref, up_ref, state_ref, t_ref, gain_ref, tt_ref, gt_ref, grad_out, out_ref):
        mixed = grad_mix(ret_ref[...], up_ref[...], state_ref[...], t_ref[...], gain_ref[...])
        grad_out[...] = mixed
        hits = slot_hits(tt_ref[...], slots)
        out_ref[...] = (pack_rows(mixed, hits) * slot_gates(hits, gt_ref[...])).astype(bf16)

    return small_call(
        body,
        [shape_of(*state.shape), shape_of(slots, state.shape[1])],
        (returned, upstream, state, targets, gain, targets_t, gates_t),
    )


def grad_pack(upstream, targets_t, gates_t, slots):
    def body(up_ref, tt_ref, gt_ref, out_ref):
        hits = slot_hits(tt_ref[...], slots)
        out_ref[...] = (pack_rows(up_ref[...], hits) * slot_gates(hits, gt_ref[...])).astype(bf16)

    return small_call(body, [shape_of(slots, upstream.shape[1])], (upstream, targets_t, gates_t))[0]


def cuts(size, width):
    width = width if size % width == 0 else size
    return [slice(at, at + width) for at in range(0, size, width)]


class TileCopies:
    def __init__(self, where, semaphores):
        self.where = where
        self.semaphores = semaphores

    def copy(self, source, target, i):
        at = self.where[i]
        return pltpu.make_async_copy(source.at[at], target.at[at], self.semaphores.at[i])


def start_from(parity, own, sibling, begin):
    own_layer = core_index() == parity

    @pl.when(own_layer)
    def _():
        begin(*own)

    @pl.when(jnp.logical_not(own_layer))
    def _():
        begin(*sibling)


def column_tiles(size, width):
    return [(slice(None), cut) for cut in cuts(size, width)]


def row_tiles(size, width):
    return [(cut, slice(None)) for cut in cuts(size, width)]


def mlp_call(body, out_shapes, arrays, scratch, flops, moved):
    return pl.pallas_call(
        body,
        out_shape=out_shapes,
        in_specs=[any_spec] * len(arrays),
        out_specs=[any_spec] * len(out_shapes),
        scratch_shapes=scratch,
        compiler_params=pltpu.CompilerParams(vmem_limit_bytes=mlp_limit),
        cost_estimate=pl.CostEstimate(flops=flops, bytes_accessed=moved, transcendentals=0),
    )(*arrays)


def copy_slots(tiles):
    return pltpu.SemaphoreType.DMA((len(tiles),))


def expert_forward(rows, weights, parity, keep_slope):
    slots, features = rows.shape
    hidden = weights[0].shape[1]
    up_tiles, down_tiles = column_tiles(hidden, forward_cut), column_tiles(features, feature_cut)

    def body(rows_ref, own_up, own_down, sib_up, sib_down, out_ref, *refs):
        if keep_slope:
            slope_ref, refs = refs[0], refs[1:]
            slope_buf, slope_sem = refs[-2:]
            slope_out = TileCopies(up_tiles, slope_sem)
        up_buf, down_buf, active, x_ref, out_buf, up_sem, down_sem, x_sem, out_sem = refs[:9]
        rows_in = pltpu.make_async_copy(rows_ref, x_ref, x_sem)
        rows_in.start()
        rows_out = TileCopies(down_tiles, out_sem)
        up_in, down_in = TileCopies(up_tiles, up_sem), TileCopies(down_tiles, down_sem)

        def begin_up(up):
            for i in range(len(up_tiles)):
                up_in.copy(up, up_buf, i).start()

        def begin_down(down):
            for i in range(len(down_tiles)):
                down_in.copy(down, down_buf, i).start()

        start_from(parity, (own_up,), (sib_up,), begin_up)
        for i, at in enumerate(up_tiles):
            up_in.copy(own_up, up_buf, i).wait()
            if i == 0:
                rows_in.wait()
                start_from(parity, (own_down,), (sib_down,), begin_down)
            pre = jnp.dot(x_ref[...], up_buf[at], preferred_element_type=f32)
            value, slope = gelu_parts(pre)
            active[at] = value.astype(bf16)
            if keep_slope:
                slope_buf[at] = slope.astype(bf16)
                slope_out.copy(slope_buf, slope_ref, i).start()
        for i, at in enumerate(down_tiles):
            down_in.copy(own_down, down_buf, i).wait()
            out_buf[at] = jnp.dot(active[...], down_buf[at], preferred_element_type=f32).astype(bf16)
            rows_out.copy(out_buf, out_ref, i).start()
        for i in range(len(down_tiles)):
            rows_out.copy(out_buf, out_ref, i).wait()
        if keep_slope:
            for i in range(len(up_tiles)):
                slope_out.copy(slope_buf, slope_ref, i).wait()

    out_shapes = [shape_of(slots, features)]
    scratch = [
        pltpu.VMEM((features, hidden), bf16),
        pltpu.VMEM((hidden, features), bf16),
        pltpu.VMEM((slots, hidden), bf16),
        pltpu.VMEM((slots, features), bf16),
        pltpu.VMEM((slots, features), bf16),
        copy_slots(up_tiles),
        copy_slots(down_tiles),
        pltpu.SemaphoreType.DMA,
        copy_slots(down_tiles),
    ]
    if keep_slope:
        out_shapes.append(shape_of(slots, hidden))
        scratch += [pltpu.VMEM((slots, hidden), bf16), copy_slots(up_tiles)]
    return mlp_call(
        body,
        out_shapes,
        (rows, *weights),
        scratch,
        4 * slots * features * hidden,
        4 * features * hidden + 4 * slots * features + 4 * slots * hidden * int(keep_slope),
    )


def expert_backward(grads, slope, weights, parity, other=None, other_chip=None):
    slots, features = grads.shape
    hidden = weights[0].shape[1]
    down_tiles, up_tiles = row_tiles(hidden, backward_cut), row_tiles(features, feature_cut)
    slope_tiles = column_tiles(hidden, backward_cut)
    out_tiles = column_tiles(features, feature_cut)
    arrays = (grads,) if other is None else (grads, other)

    def body(grads_ref, *refs):
        if other is not None:
            other_ref, refs = refs[0], refs[1:]
        own_up, own_down, sib_up, sib_down, slope_ref, out_ref = refs[:6]
        up_buf, down_buf, slope_buf, pre_grad, g_ref, out_buf = refs[6:12]
        up_sem, down_sem, slope_sem, g_sem, out_sem = refs[12:17]
        if other is not None:
            other_buf = refs[17]
        grads_in = pltpu.make_async_copy(grads_ref, g_ref, g_sem)
        grads_in.start()
        rows_out = TileCopies(out_tiles, out_sem)
        up_in, down_in = TileCopies(up_tiles, up_sem), TileCopies(down_tiles, down_sem)
        slope_in = TileCopies(slope_tiles, slope_sem)

        def begin_down(down):
            for i in range(len(down_tiles)):
                down_in.copy(down, down_buf, i).start()
                slope_in.copy(slope_ref, slope_buf, i).start()

        def begin_up(up):
            for i in range(len(up_tiles)):
                up_in.copy(up, up_buf, i).start()

        start_from(parity, (own_down,), (sib_down,), begin_down)
        for i, at in enumerate(down_tiles):
            down_in.copy(own_down, down_buf, i).wait()
            if i == 0:
                grads_in.wait()
                start_from(parity, (own_up,), (sib_up,), begin_up)
                if other is not None:
                    pltpu.make_async_copy(other_ref, other_buf, g_sem).start()
            act_grad = lax.dot_general(
                g_ref[...], down_buf[at], contract_last, preferred_element_type=f32
            )
            slope_in.copy(slope_ref, slope_buf, i).wait()
            pre_grad[slope_tiles[i]] = (act_grad * slope_buf[slope_tiles[i]].astype(f32)).astype(bf16)
        for i, at in enumerate(up_tiles):
            up_in.copy(own_up, up_buf, i).wait()
            out_buf[out_tiles[i]] = lax.dot_general(
                pre_grad[...], up_buf[at], contract_last, preferred_element_type=f32
            ).astype(bf16)
            if other is None:
                rows_out.copy(out_buf, out_ref, i).start()
        if other is None:
            for i in range(len(out_tiles)):
                rows_out.copy(out_buf, out_ref, i).wait()
        else:
            whole = out_sem.at[0]
            pltpu.make_async_copy(other_ref, other_buf, g_sem).wait()

            @pl.when(chip_index() == other_chip)
            def _():
                pltpu.make_async_copy(other_buf, out_ref, whole).start()

            @pl.when(chip_index() != other_chip)
            def _():
                pltpu.make_async_copy(out_buf, out_ref, whole).start()

            pltpu.make_async_copy(out_buf, out_ref, whole).wait()

    return mlp_call(
        body,
        [shape_of(slots, features)],
        (*arrays, *weights, slope),
        [
            pltpu.VMEM((features, hidden), bf16),
            pltpu.VMEM((hidden, features), bf16),
            pltpu.VMEM((slots, hidden), bf16),
            pltpu.VMEM((slots, hidden), bf16),
            pltpu.VMEM((slots, features), bf16),
            pltpu.VMEM((slots, features), bf16),
            copy_slots(up_tiles),
            copy_slots(down_tiles),
            copy_slots(slope_tiles),
            pltpu.SemaphoreType.DMA,
            copy_slots(out_tiles),
        ]
        + ([] if other is None else [pltpu.VMEM((slots, features), bf16)]),
        4 * slots * features * hidden,
        4 * features * hidden + 4 * slots * features + 4 * slots * hidden,
    )[0]


def act_gradient(grads, weights, parity):
    slots, features = grads.shape
    hidden = weights[0].shape[1]
    down_tiles, out_tiles = row_tiles(hidden, backward_cut), column_tiles(hidden, backward_cut)

    def body(grads_ref, own_down, sib_down, out_ref, down_buf, g_ref, out_buf, down_sem, g_sem, out_sem):
        grads_in = pltpu.make_async_copy(grads_ref, g_ref, g_sem)
        grads_in.start()
        down_in, grads_out = TileCopies(down_tiles, down_sem), TileCopies(out_tiles, out_sem)

        def begin(down):
            for i in range(len(down_tiles)):
                down_in.copy(down, down_buf, i).start()

        start_from(parity, (own_down,), (sib_down,), begin)
        for i, at in enumerate(down_tiles):
            down_in.copy(own_down, down_buf, i).wait()
            if i == 0:
                grads_in.wait()
            out_buf[out_tiles[i]] = lax.dot_general(
                g_ref[...], down_buf[at], contract_last, preferred_element_type=f32
            )
            grads_out.copy(out_buf, out_ref, i).start()
        for i in range(len(out_tiles)):
            grads_out.copy(out_buf, out_ref, i).wait()

    return mlp_call(
        body,
        [shape_of(slots, hidden, f32)],
        (grads, weights[1], weights[3]),
        [
            pltpu.VMEM((hidden, features), bf16),
            pltpu.VMEM((slots, features), bf16),
            pltpu.VMEM((slots, hidden), f32),
            copy_slots(down_tiles),
            pltpu.SemaphoreType.DMA,
            copy_slots(out_tiles),
        ],
        2 * slots * features * hidden,
        2 * features * hidden + 4 * slots * hidden,
    )[0]


def turn_around(rows, act_grad, weights, parity):
    slots, features = rows.shape
    hidden = weights[0].shape[1]
    tiles, out_tiles = column_tiles(hidden, backward_cut), column_tiles(features, feature_cut)
    up_rows = row_tiles(features, feature_cut)

    def body(rows_ref, own_up, sib_up, ag_ref, out_ref, slope_ref, active_ref, *refs):
        up_buf, ag_buf, slope_buf, active_buf, pre_grad, x_ref, out_buf = refs[:7]
        up_in, grad_in, slope_out, active_out = [TileCopies(tiles, sem) for sem in refs[7:11]]
        rows_out = TileCopies(out_tiles, refs[11])
        rows_in = pltpu.make_async_copy(rows_ref, x_ref, refs[12])
        rows_in.start()

        def begin(up):
            for i in range(len(tiles)):
                up_in.copy(up, up_buf, i).start()
                grad_in.copy(ag_ref, ag_buf, i).start()

        start_from(parity, (own_up,), (sib_up,), begin)
        for i, at in enumerate(tiles):
            up_in.copy(own_up, up_buf, i).wait()
            if i == 0:
                rows_in.wait()
            pre = jnp.dot(x_ref[...], up_buf[at], preferred_element_type=f32)
            value, slope = gelu_parts(pre)
            slope_buf[at] = slope.astype(bf16)
            active_buf[at] = value.astype(bf16)
            slope_out.copy(slope_buf, slope_ref, i).start()
            active_out.copy(active_buf, active_ref, i).start()
            grad_in.copy(ag_ref, ag_buf, i).wait()
            pre_grad[at] = (ag_buf[at] * slope).astype(bf16)
        for i, (at, rows_at) in enumerate(zip(out_tiles, up_rows)):
            out_buf[at] = lax.dot_general(
                pre_grad[...], up_buf[rows_at], contract_last, preferred_element_type=f32
            ).astype(bf16)
            rows_out.copy(out_buf, out_ref, i).start()
        for i in range(len(out_tiles)):
            rows_out.copy(out_buf, out_ref, i).wait()
        for i in range(len(tiles)):
            slope_out.copy(slope_buf, slope_ref, i).wait()
            active_out.copy(active_buf, active_ref, i).wait()

    return mlp_call(
        body,
        [shape_of(slots, features), shape_of(slots, hidden), shape_of(slots, hidden)],
        (rows, weights[0], weights[2], act_grad),
        [
            pltpu.VMEM((features, hidden), bf16),
            pltpu.VMEM((slots, hidden), f32),
            pltpu.VMEM((slots, hidden), bf16),
            pltpu.VMEM((slots, hidden), bf16),
            pltpu.VMEM((slots, hidden), bf16),
            pltpu.VMEM((slots, features), bf16),
            pltpu.VMEM((slots, features), bf16),
            copy_slots(tiles),
            copy_slots(tiles),
            copy_slots(tiles),
            copy_slots(tiles),
            copy_slots(out_tiles),
            pltpu.SemaphoreType.DMA,
        ],
        4 * slots * features * hidden,
        2 * features * hidden + 10 * slots * hidden,
    )


def local(inputs, norm_gain, w_up, w_down, expert_ids, gates, out_grad):
    sections = lax.axis_size("section")
    experts = lax.axis_size("expert")
    chips = sections // 2
    last = chips - 1
    chip, core = chip_index(), core_index()
    batches, rows_dev, features = inputs.shape
    capacity = max(2, 5 * rows_dev // (2 * experts))
    slots = experts * capacity

    def swap_cores(x):
        return lax.ppermute(x, "section", [(s, s ^ 1) for s in range(sections)])

    def shift_chips(x, by):
        return lax.ppermute(
            x, "section", [(s, (s + 2 * by) % sections) for s in range(sections)]
        )

    def to_experts(x):
        return lax.all_to_all(x, "expert", split_axis=0, concat_axis=0, tiled=True)

    own_small, to_send = gather_params(
        jnp.swapaxes(expert_ids[0], 1, 2),
        jnp.swapaxes(gates[0], 1, 2),
        norm_gain[0].reshape(features // rows_dev, rows_dev),
    )
    sib_small = swap_cores(to_send)
    own_up, own_down = w_up[0, 0], w_down[0, 0]
    sib_small, up_to_send, down_to_send = lax.optimization_barrier((sib_small, own_up, own_down))
    weights = (own_up, own_down, swap_cores(up_to_send), swap_cores(down_to_send))

    even, odd, state, last_grad, send = prepare_pack(
        own_small, sib_small, inputs, out_grad, experts, capacity, last
    )
    (even_tt, even_t, even_gt, even_g, even_gain) = even
    (odd_tt, odd_t, odd_gt, odd_g, odd_gain) = odd
    odd_out = None
    act_grad = None
    for turn in range(chips):
        if turn > 0:
            arrived = shift_chips(odd_out_now, 1)
            state, send = select_pack(arrived, state, even_gain, even_tt, slots, turn)
        received = to_experts(send)
        if turn < last:
            (outputs,) = expert_forward(received, weights, 0, False)
        else:
            outputs, even_slope = expert_forward(received, weights, 0, True)
        returned = to_experts(outputs)
        if turn == 0:
            act_grad = act_gradient(received, weights, 1)
        middle, send = combine_pack(returned, state, even_t, even_g, odd_gain, odd_tt)
        received = to_experts(send)
        if turn < last:
            (outputs,) = expert_forward(received, weights, 1, False)
            returned = to_experts(outputs)
            odd_out_now = combine(returned, middle, odd_t, odd_g)
            odd_out = (
                odd_out_now if odd_out is None else jnp.where(chip == turn, odd_out_now, odd_out)
            )

    back, odd_slope, odd_active = turn_around(received, act_grad, weights, 1)
    returned = to_experts(back)
    odd_down = jnp.dot(
        odd_active,
        jnp.where(core == 1, weights[1], weights[3]),
        preferred_element_type=f32,
    ).astype(bf16)
    upstream = last_grad
    even_grad = odd_grad = None
    for turn in range(last, -1, -1):
        if turn < last:
            upstream = shift_chips(even_now, -1)
            send = grad_pack(upstream, odd_tt, odd_gt, slots)
            received = to_experts(send)
            if turn == last - 1:
                back = expert_backward(received, odd_slope, weights, 1, odd_down, last)
            else:
                back = expert_backward(received, odd_slope, weights, 1)
            returned = to_experts(back)
            if turn == last - 1:
                final_out = combine(returned, middle, odd_t, odd_g)
                odd_out = jnp.where(chip == last, final_out, odd_out)
        odd_now, send = grad_combine_pack(
            returned, upstream, middle, odd_t, odd_gain, even_tt, even_gt
        )
        odd_grad = odd_now if odd_grad is None else jnp.where(chip == turn, odd_now, odd_grad)
        received = to_experts(send)
        back = expert_backward(received, even_slope, weights, 0)
        returned = to_experts(back)
        even_now = grad_combine(returned, odd_now, state, even_t, even_gain)
        even_grad = even_now if even_grad is None else jnp.where(chip == turn, even_now, even_grad)

    def gather_batches(even, odd):
        own = jnp.where(core == 0, even, odd)
        other = swap_cores(jnp.where(core == 0, odd, even))
        return jnp.where(core == 0, jnp.stack([own, other]), jnp.stack([other, own]))[None]

    return (gather_batches(middle, odd_out), gather_batches(even_grad, odd_grad))


def solution(mesh):
    return jax.shard_map(
        local,
        mesh=mesh,
        in_specs=(
            P(None, "expert", None),
            P("section", None),
            P("section", "expert", None, None),
            P("section", "expert", None, None),
            P("section", None, "expert", None),
            P("section", None, "expert", None),
            P(None, "expert", None),
        ),
        out_specs=(P("section", None, "expert", None), P("section", None, "expert", None)),
        check_vma=False,
    )
```

```python
import jax
import jax.numpy as jnp
from jax import lax
from jax.experimental import pallas as pl
from jax.experimental.pallas import tpu as pltpu
from jax.sharding import PartitionSpec as P

epsilon = 1e-05
gelu_coef = 0.7978845608028654
cubic_coef = 0.044715
contract_last = (((1,), (1,)), ((), ()))
f32 = jnp.float32
bf16 = jnp.bfloat16
vmem_spec = pl.BlockSpec(memory_space=pltpu.VMEM)
any_spec = pl.BlockSpec(memory_space=pl.ANY)
forward_cut = 512
backward_cut = 1024
feature_cut = 512
small_limit = 12 * 1024 * 1024
mlp_limit = 60 * 1024 * 1024


def gelu_parts(pre):
    square = pre * pre
    tangent = jnp.tanh(gelu_coef * pre * (1.0 + cubic_coef * square))
    half = 0.5 * (1.0 + tangent)
    slope = half + 0.5 * pre * (1.0 - tangent * tangent) * gelu_coef * (
        1.0 + 3.0 * cubic_coef * square
    )
    return pre * half, slope


def inverse_rms(values):
    return lax.rsqrt(jnp.mean(values * values, axis=-1, keepdims=True) + epsilon)


def normalize(values, gain_row):
    return (values * inverse_rms(values) * gain_row).astype(bf16)


def chip_index():
    return lax.axis_index("section") // 2


def core_index():
    return lax.axis_index("section") % 2


def unpack_pairs(returned, targets):
    rows, slots = targets.shape[0], returned.shape[0]
    lanes = lax.broadcasted_iota(jnp.int32, (rows, slots), 1)
    picked = []
    for k in range(2):
        chosen = (targets[:, k : k + 1] == lanes).astype(f32).astype(bf16)
        picked.append(jnp.dot(chosen, returned, preferred_element_type=f32))
    return picked


def slot_hits(targets_t, slots):
    rows = targets_t.shape[1]
    sublanes = lax.broadcasted_iota(jnp.int32, (slots, rows), 0)
    return [targets_t[k : k + 1, :] == sublanes for k in range(2)]


def pack_rows(rows, hits):
    chosen = jnp.where(hits[0] | hits[1], 1.0, 0.0).astype(bf16)
    return jnp.dot(chosen, rows, preferred_element_type=f32)


def slot_gates(hits, gates_t):
    total = jnp.where(hits[0], gates_t[0:1, :], 0.0) + jnp.where(hits[1], gates_t[1:2, :], 0.0)
    return jnp.sum(total, axis=1, keepdims=True)


def small_call(body, out_shapes, args, earlier=()):
    def with_earlier(*refs):
        body(*refs[: len(args)], *refs[len(args) + len(earlier) :])

    return pl.pallas_call(
        with_earlier,
        out_shape=out_shapes,
        in_specs=[vmem_spec] * len(args) + [any_spec] * len(earlier),
        out_specs=[vmem_spec] * len(out_shapes),
        compiler_params=pltpu.CompilerParams(vmem_limit_bytes=small_limit),
    )(*args, *earlier)


def shape_of(rows, columns, kind=bf16):
    return jax.ShapeDtypeStruct((rows, columns), kind)


def gather_params(ids_t, gates_t, gain):
    def body(ids_hbm, gates_hbm, gain_hbm, own_ref, send_ref, ids_ref, gates_ref, gain_ref, sem):
        copies = [
            pltpu.make_async_copy(source, target, sem.at[i])
            for i, (source, target) in enumerate(
                ((ids_hbm, ids_ref), (gates_hbm, gates_ref), (gain_hbm, gain_ref))
            )
        ]
        for copy in copies:
            copy.start()
        for copy in copies:
            copy.wait()
        for out_ref, batch in ((own_ref, core_index()), (send_ref, 1 - core_index())):
            out_ref[0:2] = ids_ref[batch].astype(f32)
            out_ref[2:4] = gates_ref[batch]
            out_ref[4:] = gain_ref[...]

    rows = 4 + gain.shape[0]
    return pl.pallas_call(
        body,
        out_shape=[shape_of(rows, gain.shape[1], f32)] * 2,
        in_specs=[any_spec] * 3,
        out_specs=[vmem_spec] * 2,
        scratch_shapes=[
            pltpu.VMEM(ids_t.shape, jnp.int32),
            pltpu.VMEM(gates_t.shape, f32),
            pltpu.VMEM(gain.shape, f32),
            pltpu.SemaphoreType.DMA((3,)),
        ],
        compiler_params=pltpu.CompilerParams(vmem_limit_bytes=mlp_limit),
    )(ids_t, gates_t, gain)


def as_column(row):
    size = row.shape[1]
    down = lax.broadcasted_iota(jnp.int32, (size, size), 0)
    across = lax.broadcasted_iota(jnp.int32, (size, size), 1)
    return jnp.sum(jnp.where(down == across, row, 0.0), axis=1, keepdims=True)


def slot_rows(ids_t, experts, capacity):
    rows = ids_t.shape[1]
    expert = lax.broadcasted_iota(jnp.int32, (experts, rows), 0).astype(f32)
    hits = [(ids_t[k : k + 1, :] == expert).astype(f32) for k in range(2)]
    before = lax.broadcasted_iota(jnp.int32, (rows, rows), 0)
    after = lax.broadcasted_iota(jnp.int32, (rows, rows), 1)
    earlier = (before < after).astype(f32)
    rank = jnp.dot(hits[0] + hits[1], earlier, preferred_element_type=f32)
    return [
        ids_t[k : k + 1, :] * float(capacity) + jnp.sum(hits[k] * rank, axis=0, keepdims=True)
        for k in range(2)
    ]


def prepare_pack(own_small, sib_small, state, out_grad, experts, capacity, last_chip):
    rows, features = state.shape
    slots = experts * capacity
    params = [
        jax.ShapeDtypeStruct((2, rows), jnp.int32),
        jax.ShapeDtypeStruct((rows, 2), jnp.int32),
        shape_of(2, rows, f32),
        shape_of(rows, 2, f32),
        shape_of(1, features, f32),
    ]

    def body(own_ref, sib_ref, state_ref, grad_ref, *refs):
        even, odd, out_ref = refs[:5], refs[5:10], refs[10]
        for parity, (tt_ref, t_ref, gt_ref, g_ref, gain_ref) in ((0, even), (1, odd)):
            chosen = jnp.where(core_index() == parity, own_ref[...], sib_ref[...])
            gt_ref[...] = chosen[2:4]
            at = slot_rows(chosen[0:2], experts, capacity)
            for k in range(2):
                tt_ref[k : k + 1, :] = at[k].astype(jnp.int32)
                t_ref[:, k : k + 1] = as_column(at[k]).astype(jnp.int32)
                g_ref[:, k : k + 1] = as_column(chosen[2 + k : 3 + k])
            for i in range(features // rows):
                gain_ref[:, i * rows : (i + 1) * rows] = chosen[4 + i : 5 + i]
        is_last = chip_index() == last_chip

        @pl.when(is_last)
        def _():
            hits = slot_hits(odd[0][...], slots)
            out_ref[...] = (
                pack_rows(grad_ref[...], hits) * slot_gates(hits, odd[2][...])
            ).astype(bf16)

        @pl.when(jnp.logical_not(is_last))
        def _():
            normed = normalize(state_ref[...].astype(f32), even[4][...])
            out_ref[...] = pack_rows(normed, slot_hits(even[0][...], slots)).astype(bf16)

    out_shapes = params + params + [shape_of(slots, features)]
    made = small_call(body, out_shapes, (own_small, sib_small, state, out_grad))
    return made[:5], made[5:10], made[10]


def select_pack(arrived, state, gain, targets_t, slots, chip):
    def body(arrived_ref, state_ref, gain_ref, tt_ref, state_out, out_ref):
        mine = chip_index() == chip

        @pl.when(mine)
        def _():
            state_out[...] = arrived_ref[...]

        @pl.when(jnp.logical_not(mine))
        def _():
            state_out[...] = state_ref[...]

        normed = normalize(state_out[...].astype(f32), gain_ref[...])
        out_ref[...] = pack_rows(normed, slot_hits(tt_ref[...], slots)).astype(bf16)

    return small_call(
        body,
        [shape_of(*state.shape), shape_of(slots, state.shape[1])],
        (arrived, state, gain, targets_t),
    )


def mix(returned, state, targets, gates):
    first, second = unpack_pairs(returned, targets)
    return (state.astype(f32) + (gates[:, 0:1] * first + gates[:, 1:2] * second)).astype(bf16)


def combine(returned, state, targets, gates):
    def body(ret_ref, state_ref, t_ref, g_ref, out_ref):
        out_ref[...] = mix(ret_ref[...], state_ref[...], t_ref[...], g_ref[...])

    return small_call(body, [shape_of(*state.shape)], (returned, state, targets, gates))[0]


def combine_pack(returned, state, targets, gates, gain, targets_t, earlier=()):
    slots = returned.shape[0]

    def body(ret_ref, state_ref, t_ref, g_ref, gain_ref, tt_ref, state_out, out_ref):
        mixed = mix(ret_ref[...], state_ref[...], t_ref[...], g_ref[...])
        state_out[...] = mixed
        normed = normalize(mixed.astype(f32), gain_ref[...])
        out_ref[...] = pack_rows(normed, slot_hits(tt_ref[...], slots)).astype(bf16)

    return small_call(
        body,
        [shape_of(*state.shape), shape_of(slots, state.shape[1])],
        (returned, state, targets, gates, gain, targets_t),
        earlier,
    )


def grad_mix(returned, upstream, state, targets, gain_row):
    first, second = unpack_pairs(returned, targets)
    values = state.astype(f32)
    inv_rms = inverse_rms(values)
    spread = (first + second) * gain_row
    along = jnp.mean(spread * values, axis=-1, keepdims=True)
    return (
        upstream.astype(f32) + inv_rms * spread - values * inv_rms * inv_rms * inv_rms * along
    ).astype(bf16)


def grad_combine(returned, upstream, state, targets, gain):
    def body(ret_ref, up_ref, state_ref, t_ref, gain_ref, out_ref):
        out_ref[...] = grad_mix(
            ret_ref[...], up_ref[...], state_ref[...], t_ref[...], gain_ref[...]
        )

    return small_call(
        body, [shape_of(*state.shape)], (returned, upstream, state, targets, gain)
    )[0]


def grad_combine_pack(
    returned, upstream, state, targets, gain, targets_t, gates_t, earlier=()
):
    slots = returned.shape[0]

    def body(ret_ref, up_ref, state_ref, t_ref, gain_ref, tt_ref, gt_ref, grad_out, out_ref):
        mixed = grad_mix(ret_ref[...], up_ref[...], state_ref[...], t_ref[...], gain_ref[...])
        grad_out[...] = mixed
        hits = slot_hits(tt_ref[...], slots)
        out_ref[...] = (pack_rows(mixed, hits) * slot_gates(hits, gt_ref[...])).astype(bf16)

    return small_call(
        body,
        [shape_of(*state.shape), shape_of(slots, state.shape[1])],
        (returned, upstream, state, targets, gain, targets_t, gates_t),
        earlier,
    )


def grad_pack(upstream, targets_t, gates_t, slots):
    def body(up_ref, tt_ref, gt_ref, out_ref):
        hits = slot_hits(tt_ref[...], slots)
        out_ref[...] = (pack_rows(up_ref[...], hits) * slot_gates(hits, gt_ref[...])).astype(bf16)

    return small_call(body, [shape_of(slots, upstream.shape[1])], (upstream, targets_t, gates_t))[0]


def cuts(size, width):
    width = width if size % width == 0 else size
    return [slice(at, at + width) for at in range(0, size, width)]


class TileCopies:
    def __init__(self, where, semaphores):
        self.where = where
        self.semaphores = semaphores

    def copy(self, source, target, i):
        at = self.where[i]
        return pltpu.make_async_copy(source.at[at], target.at[at], self.semaphores.at[i])


def start_from(parity, own, sibling, begin):
    own_layer = core_index() == parity

    @pl.when(own_layer)
    def _():
        begin(*own)

    @pl.when(jnp.logical_not(own_layer))
    def _():
        begin(*sibling)


def column_tiles(size, width):
    return [(slice(None), cut) for cut in cuts(size, width)]


def row_tiles(size, width):
    return [(cut, slice(None)) for cut in cuts(size, width)]


def mlp_call(body, out_shapes, arrays, scratch, flops, moved):
    return pl.pallas_call(
        body,
        out_shape=out_shapes,
        in_specs=[any_spec] * len(arrays),
        out_specs=[any_spec] * len(out_shapes),
        scratch_shapes=scratch,
        compiler_params=pltpu.CompilerParams(vmem_limit_bytes=mlp_limit),
        cost_estimate=pl.CostEstimate(flops=flops, bytes_accessed=moved, transcendentals=0),
    )(*arrays)


def copy_slots(tiles):
    return pltpu.SemaphoreType.DMA((len(tiles),))


def expert_forward(rows, weights, parity, keep_slope):
    slots, features = rows.shape
    hidden = weights[0].shape[1]
    up_tiles, down_tiles = column_tiles(hidden, forward_cut), column_tiles(features, feature_cut)

    def body(rows_ref, own_up, own_down, sib_up, sib_down, out_ref, *refs):
        if keep_slope:
            slope_ref, refs = refs[0], refs[1:]
            slope_buf, slope_sem = refs[-2:]
            slope_out = TileCopies(up_tiles, slope_sem)
        up_buf, down_buf, active, x_ref, out_buf, up_sem, down_sem, x_sem, out_sem = refs[:9]
        rows_in = pltpu.make_async_copy(rows_ref, x_ref, x_sem)
        rows_in.start()
        rows_out = TileCopies(down_tiles, out_sem)
        up_in, down_in = TileCopies(up_tiles, up_sem), TileCopies(down_tiles, down_sem)

        def begin_up(up):
            for i in range(len(up_tiles)):
                up_in.copy(up, up_buf, i).start()

        def begin_down(down):
            for i in range(len(down_tiles)):
                down_in.copy(down, down_buf, i).start()

        start_from(parity, (own_up,), (sib_up,), begin_up)
        for i, at in enumerate(up_tiles):
            up_in.copy(own_up, up_buf, i).wait()
            if i == 0:
                rows_in.wait()
                start_from(parity, (own_down,), (sib_down,), begin_down)
            pre = jnp.dot(x_ref[...], up_buf[at], preferred_element_type=f32)
            value, slope = gelu_parts(pre)
            active[at] = value.astype(bf16)
            if keep_slope:
                slope_buf[at] = slope.astype(bf16)
                slope_out.copy(slope_buf, slope_ref, i).start()
        for i, at in enumerate(down_tiles):
            down_in.copy(own_down, down_buf, i).wait()
            out_buf[at] = jnp.dot(active[...], down_buf[at], preferred_element_type=f32).astype(bf16)
            rows_out.copy(out_buf, out_ref, i).start()
        for i in range(len(down_tiles)):
            rows_out.copy(out_buf, out_ref, i).wait()
        if keep_slope:
            for i in range(len(up_tiles)):
                slope_out.copy(slope_buf, slope_ref, i).wait()

    out_shapes = [shape_of(slots, features)]
    scratch = [
        pltpu.VMEM((features, hidden), bf16),
        pltpu.VMEM((hidden, features), bf16),
        pltpu.VMEM((slots, hidden), bf16),
        pltpu.VMEM((slots, features), bf16),
        pltpu.VMEM((slots, features), bf16),
        copy_slots(up_tiles),
        copy_slots(down_tiles),
        pltpu.SemaphoreType.DMA,
        copy_slots(down_tiles),
    ]
    if keep_slope:
        out_shapes.append(shape_of(slots, hidden))
        scratch += [pltpu.VMEM((slots, hidden), bf16), copy_slots(up_tiles)]
    return mlp_call(
        body,
        out_shapes,
        (rows, *weights),
        scratch,
        4 * slots * features * hidden,
        4 * features * hidden + 4 * slots * features + 4 * slots * hidden * int(keep_slope),
    )


def expert_backward(grads, slope, weights, parity, other=None, other_chip=None):
    slots, features = grads.shape
    hidden = weights[0].shape[1]
    down_tiles, up_tiles = row_tiles(hidden, backward_cut), row_tiles(features, feature_cut)
    slope_tiles = column_tiles(hidden, backward_cut)
    out_tiles = column_tiles(features, feature_cut)
    arrays = (grads,) if other is None else (grads, other)

    def body(grads_ref, *refs):
        if other is not None:
            other_ref, refs = refs[0], refs[1:]
        own_up, own_down, sib_up, sib_down, slope_ref, out_ref = refs[:6]
        up_buf, down_buf, slope_buf, pre_grad, g_ref, out_buf = refs[6:12]
        up_sem, down_sem, slope_sem, g_sem, out_sem = refs[12:17]
        if other is not None:
            other_buf = refs[17]
        grads_in = pltpu.make_async_copy(grads_ref, g_ref, g_sem)
        grads_in.start()
        rows_out = TileCopies(out_tiles, out_sem)
        up_in, down_in = TileCopies(up_tiles, up_sem), TileCopies(down_tiles, down_sem)
        slope_in = TileCopies(slope_tiles, slope_sem)

        def begin_down(down):
            for i in range(len(down_tiles)):
                down_in.copy(down, down_buf, i).start()
                slope_in.copy(slope_ref, slope_buf, i).start()

        def begin_up(up):
            for i in range(len(up_tiles)):
                up_in.copy(up, up_buf, i).start()

        start_from(parity, (own_down,), (sib_down,), begin_down)
        for i, at in enumerate(down_tiles):
            down_in.copy(own_down, down_buf, i).wait()
            if i == 0:
                grads_in.wait()
                start_from(parity, (own_up,), (sib_up,), begin_up)
                if other is not None:
                    pltpu.make_async_copy(other_ref, other_buf, g_sem).start()
            act_grad = lax.dot_general(
                g_ref[...], down_buf[at], contract_last, preferred_element_type=f32
            )
            slope_in.copy(slope_ref, slope_buf, i).wait()
            pre_grad[slope_tiles[i]] = (act_grad * slope_buf[slope_tiles[i]].astype(f32)).astype(bf16)
        for i, at in enumerate(up_tiles):
            up_in.copy(own_up, up_buf, i).wait()
            out_buf[out_tiles[i]] = lax.dot_general(
                pre_grad[...], up_buf[at], contract_last, preferred_element_type=f32
            ).astype(bf16)
            if other is None:
                rows_out.copy(out_buf, out_ref, i).start()
        if other is None:
            for i in range(len(out_tiles)):
                rows_out.copy(out_buf, out_ref, i).wait()
        else:
            whole = out_sem.at[0]
            pltpu.make_async_copy(other_ref, other_buf, g_sem).wait()

            @pl.when(chip_index() == other_chip)
            def _():
                pltpu.make_async_copy(other_buf, out_ref, whole).start()

            @pl.when(chip_index() != other_chip)
            def _():
                pltpu.make_async_copy(out_buf, out_ref, whole).start()

            pltpu.make_async_copy(out_buf, out_ref, whole).wait()

    return mlp_call(
        body,
        [shape_of(slots, features)],
        (*arrays, *weights, slope),
        [
            pltpu.VMEM((features, hidden), bf16),
            pltpu.VMEM((hidden, features), bf16),
            pltpu.VMEM((slots, hidden), bf16),
            pltpu.VMEM((slots, hidden), bf16),
            pltpu.VMEM((slots, features), bf16),
            pltpu.VMEM((slots, features), bf16),
            copy_slots(up_tiles),
            copy_slots(down_tiles),
            copy_slots(slope_tiles),
            pltpu.SemaphoreType.DMA,
            copy_slots(out_tiles),
        ]
        + ([] if other is None else [pltpu.VMEM((slots, features), bf16)]),
        4 * slots * features * hidden,
        4 * features * hidden + 4 * slots * features + 4 * slots * hidden,
    )[0]


def act_gradient(grads, weights, parity):
    slots, features = grads.shape
    hidden = weights[0].shape[1]
    down_tiles, out_tiles = row_tiles(hidden, backward_cut), column_tiles(hidden, backward_cut)

    def body(grads_ref, own_down, sib_down, out_ref, down_buf, g_ref, out_buf, down_sem, g_sem, out_sem):
        grads_in = pltpu.make_async_copy(grads_ref, g_ref, g_sem)
        grads_in.start()
        down_in, grads_out = TileCopies(down_tiles, down_sem), TileCopies(out_tiles, out_sem)

        def begin(down):
            for i in range(len(down_tiles)):
                down_in.copy(down, down_buf, i).start()

        start_from(parity, (own_down,), (sib_down,), begin)
        for i, at in enumerate(down_tiles):
            down_in.copy(own_down, down_buf, i).wait()
            if i == 0:
                grads_in.wait()
            out_buf[out_tiles[i]] = lax.dot_general(
                g_ref[...], down_buf[at], contract_last, preferred_element_type=f32
            )
            grads_out.copy(out_buf, out_ref, i).start()
        for i in range(len(out_tiles)):
            grads_out.copy(out_buf, out_ref, i).wait()

    return mlp_call(
        body,
        [shape_of(slots, hidden, f32)],
        (grads, weights[1], weights[3]),
        [
            pltpu.VMEM((hidden, features), bf16),
            pltpu.VMEM((slots, features), bf16),
            pltpu.VMEM((slots, hidden), f32),
            copy_slots(down_tiles),
            pltpu.SemaphoreType.DMA,
            copy_slots(out_tiles),
        ],
        2 * slots * features * hidden,
        2 * features * hidden + 4 * slots * hidden,
    )[0]


def turn_around(rows, act_grad, weights, parity):
    slots, features = rows.shape
    hidden = weights[0].shape[1]
    tiles, out_tiles = column_tiles(hidden, backward_cut), column_tiles(features, feature_cut)
    up_rows = row_tiles(features, feature_cut)

    def body(rows_ref, own_up, sib_up, ag_ref, out_ref, slope_ref, active_ref, *refs):
        up_buf, ag_buf, slope_buf, active_buf, pre_grad, x_ref, out_buf = refs[:7]
        up_in, grad_in, slope_out, active_out = [TileCopies(tiles, sem) for sem in refs[7:11]]
        rows_out = TileCopies(out_tiles, refs[11])
        rows_in = pltpu.make_async_copy(rows_ref, x_ref, refs[12])
        rows_in.start()

        def begin(up):
            for i in range(len(tiles)):
                up_in.copy(up, up_buf, i).start()
                grad_in.copy(ag_ref, ag_buf, i).start()

        start_from(parity, (own_up,), (sib_up,), begin)
        for i, at in enumerate(tiles):
            up_in.copy(own_up, up_buf, i).wait()
            if i == 0:
                rows_in.wait()
            pre = jnp.dot(x_ref[...], up_buf[at], preferred_element_type=f32)
            value, slope = gelu_parts(pre)
            slope_buf[at] = slope.astype(bf16)
            active_buf[at] = value.astype(bf16)
            slope_out.copy(slope_buf, slope_ref, i).start()
            active_out.copy(active_buf, active_ref, i).start()
            grad_in.copy(ag_ref, ag_buf, i).wait()
            pre_grad[at] = (ag_buf[at] * slope).astype(bf16)
        for i, (at, rows_at) in enumerate(zip(out_tiles, up_rows)):
            out_buf[at] = lax.dot_general(
                pre_grad[...], up_buf[rows_at], contract_last, preferred_element_type=f32
            ).astype(bf16)
            rows_out.copy(out_buf, out_ref, i).start()
        for i in range(len(out_tiles)):
            rows_out.copy(out_buf, out_ref, i).wait()
        for i in range(len(tiles)):
            slope_out.copy(slope_buf, slope_ref, i).wait()
            active_out.copy(active_buf, active_ref, i).wait()

    return mlp_call(
        body,
        [shape_of(slots, features), shape_of(slots, hidden), shape_of(slots, hidden)],
        (rows, weights[0], weights[2], act_grad),
        [
            pltpu.VMEM((features, hidden), bf16),
            pltpu.VMEM((slots, hidden), f32),
            pltpu.VMEM((slots, hidden), bf16),
            pltpu.VMEM((slots, hidden), bf16),
            pltpu.VMEM((slots, hidden), bf16),
            pltpu.VMEM((slots, features), bf16),
            pltpu.VMEM((slots, features), bf16),
            copy_slots(tiles),
            copy_slots(tiles),
            copy_slots(tiles),
            copy_slots(tiles),
            copy_slots(out_tiles),
            pltpu.SemaphoreType.DMA,
        ],
        4 * slots * features * hidden,
        2 * features * hidden + 10 * slots * hidden,
    )


def local(inputs, norm_gain, w_up, w_down, expert_ids, gates, out_grad):
    sections = lax.axis_size("section")
    experts = lax.axis_size("expert")
    chips = sections // 2
    last = chips - 1
    chip, core = chip_index(), core_index()
    batches, rows_dev, features = inputs.shape
    capacity = max(2, 5 * rows_dev // (2 * experts))
    slots = experts * capacity

    def swap_cores(x):
        return lax.ppermute(x, "section", [(s, s ^ 1) for s in range(sections)])

    def shift_chips(x, by):
        return lax.ppermute(
            x, "section", [(s, (s + 2 * by) % sections) for s in range(sections)]
        )

    def to_experts(x):
        return lax.all_to_all(x, "expert", split_axis=0, concat_axis=0, tiled=True)

    own_small, to_send = gather_params(
        jnp.swapaxes(expert_ids[0], 1, 2),
        jnp.swapaxes(gates[0], 1, 2),
        norm_gain[0].reshape(features // rows_dev, rows_dev),
    )
    sib_small = swap_cores(to_send)
    state = jnp.where(core == 0, inputs[0], inputs[1])
    last_grad = jnp.where(core == 0, out_grad[0], out_grad[1])
    own_up, own_down = w_up[0, 0], w_down[0, 0]
    sib_small, state, last_grad, up_to_send, down_to_send = lax.optimization_barrier(
        (sib_small, state, last_grad, own_up, own_down)
    )
    weights = (own_up, own_down, swap_cores(up_to_send), swap_cores(down_to_send))

    even, odd, send = prepare_pack(
        own_small, sib_small, state, last_grad, experts, capacity, last
    )
    (even_tt, even_t, even_gt, even_g, even_gain) = even
    (odd_tt, odd_t, odd_gt, odd_g, odd_gain) = odd
    odd_out = None
    act_grad = None
    for turn in range(chips):
        if turn > 0:
            arrived = shift_chips(odd_out_now, 1)
            state, send = select_pack(arrived, state, even_gain, even_tt, slots, turn)
        received = to_experts(send)
        if turn < last:
            (outputs,) = expert_forward(received, weights, 0, False)
        else:
            outputs, even_slope = expert_forward(received, weights, 0, True)
        returned = to_experts(outputs)
        if turn == 0:
            act_grad = act_gradient(received, weights, 1)
        middle, send = combine_pack(
            returned, state, even_t, even_g, odd_gain, odd_tt, (act_grad[:8, :128],) if turn == last else ()
        )
        received = to_experts(send)
        if turn < last:
            (outputs,) = expert_forward(received, weights, 1, False)
            returned = to_experts(outputs)
            odd_out_now = combine(returned, middle, odd_t, odd_g)
            odd_out = (
                odd_out_now if odd_out is None else jnp.where(chip == turn, odd_out_now, odd_out)
            )

    back, odd_slope, odd_active = turn_around(received, act_grad, weights, 1)
    returned = to_experts(back)
    odd_down = jnp.dot(
        odd_active,
        jnp.where(core == 1, weights[1], weights[3]),
        preferred_element_type=f32,
    ).astype(bf16)
    upstream = last_grad
    even_grad = odd_grad = None
    for turn in range(last, -1, -1):
        if turn < last:
            upstream = shift_chips(even_now, -1)
            send = grad_pack(upstream, odd_tt, odd_gt, slots)
            received = to_experts(send)
            if turn == last - 1:
                back = expert_backward(received, odd_slope, weights, 1, odd_down, last)
            else:
                back = expert_backward(received, odd_slope, weights, 1)
            returned = to_experts(back)
            if turn == last - 1:
                final_out = combine(returned, middle, odd_t, odd_g)
                odd_out = jnp.where(chip == last, final_out, odd_out)
        odd_now, send = grad_combine_pack(
            returned, upstream, middle, odd_t, odd_gain, even_tt, even_gt,
            (odd_down,) if turn == last else (),
        )
        odd_grad = odd_now if odd_grad is None else jnp.where(chip == turn, odd_now, odd_grad)
        received = to_experts(send)
        back = expert_backward(received, even_slope, weights, 0)
        returned = to_experts(back)
        even_now = grad_combine(returned, odd_now, state, even_t, even_gain)
        even_grad = even_now if even_grad is None else jnp.where(chip == turn, even_now, even_grad)

    def gather_batches(even, odd):
        own = jnp.where(core == 0, even, odd)
        other = swap_cores(jnp.where(core == 0, odd, even))
        return jnp.where(core == 0, jnp.stack([own, other]), jnp.stack([other, own]))[None]

    return (gather_batches(middle, odd_out), gather_batches(even_grad, odd_grad))


def solution(mesh):
    return jax.shard_map(
        local,
        mesh=mesh,
        in_specs=(
            P(None, "expert", None),
            P("section", None),
            P("section", "expert", None, None),
            P("section", "expert", None, None),
            P("section", None, "expert", None),
            P("section", None, "expert", None),
            P(None, "expert", None),
        ),
        out_specs=(P("section", None, "expert", None), P("section", None, "expert", None)),
        check_vma=False,
    )
```

```python
import jax
import jax.numpy as jnp
from jax import lax
from jax.experimental import pallas as pl
from jax.experimental.pallas import tpu as pltpu
from jax.sharding import PartitionSpec as P

epsilon = 1e-05
gelu_coef = 0.7978845608028654
cubic_coef = 0.044715
contract_last = (((1,), (1,)), ((), ()))
f32 = jnp.float32
bf16 = jnp.bfloat16
vmem_spec = pl.BlockSpec(memory_space=pltpu.VMEM)
any_spec = pl.BlockSpec(memory_space=pl.ANY)
forward_cut = 512
backward_cut = 1024
feature_cut = 512
small_limit = 12 * 1024 * 1024
mlp_limit = 60 * 1024 * 1024
rows_limit = 52 * 1024 * 1024


def gelu_parts(pre):
    square = pre * pre
    tangent = jnp.tanh(pre * (gelu_coef + (gelu_coef * cubic_coef) * square))
    half = 0.5 + 0.5 * tangent
    bend = (0.5 * gelu_coef) + (1.5 * gelu_coef * cubic_coef) * square
    slope = half + pre * (1.0 - tangent * tangent) * bend
    return pre * half, slope


def inverse_rms(values):
    return lax.rsqrt(jnp.mean(values * values, axis=-1, keepdims=True) + epsilon)


def normalize(values, gain_row):
    return (values * inverse_rms(values) * gain_row).astype(bf16)


def chip_index():
    return lax.axis_index("section") // 2


def core_index():
    return lax.axis_index("section") % 2


def unpack_pairs(returned, targets):
    rows, slots = targets.shape[0], returned.shape[0]
    lanes = lax.broadcasted_iota(jnp.int32, (rows, slots), 1)
    picked = []
    for k in range(2):
        chosen = (targets[:, k : k + 1] == lanes).astype(f32).astype(bf16)
        picked.append(jnp.dot(chosen, returned, preferred_element_type=f32))
    return picked


def slot_hits(targets_t, slots):
    rows = targets_t.shape[1]
    sublanes = lax.broadcasted_iota(jnp.int32, (slots, rows), 0)
    return [targets_t[k : k + 1, :] == sublanes for k in range(2)]


def pack_rows(rows, hits):
    chosen = jnp.where(hits[0] | hits[1], 1.0, 0.0).astype(bf16)
    return jnp.dot(chosen, rows, preferred_element_type=f32)


def slot_gates(hits, gates_t):
    total = jnp.where(hits[0], gates_t[0:1, :], 0.0) + jnp.where(hits[1], gates_t[1:2, :], 0.0)
    return jnp.sum(total, axis=1, keepdims=True)


def small_call(body, out_shapes, args, earlier=()):
    def with_earlier(*refs):
        body(*refs[: len(args)], *refs[len(args) + len(earlier) :])

    return pl.pallas_call(
        with_earlier,
        out_shape=out_shapes,
        in_specs=[vmem_spec] * len(args) + [any_spec] * len(earlier),
        out_specs=[vmem_spec] * len(out_shapes),
        compiler_params=pltpu.CompilerParams(vmem_limit_bytes=small_limit),
    )(*args, *earlier)


def shape_of(rows, columns, kind=bf16):
    return jax.ShapeDtypeStruct((rows, columns), kind)


def gather_params(ids_t, gates_t, gain):
    def body(ids_hbm, gates_hbm, gain_hbm, own_ref, send_ref, ids_ref, gates_ref, gain_ref, sem):
        copies = [
            pltpu.make_async_copy(source, target, sem.at[i])
            for i, (source, target) in enumerate(
                ((ids_hbm, ids_ref), (gates_hbm, gates_ref), (gain_hbm, gain_ref))
            )
        ]
        for copy in copies:
            copy.start()
        for copy in copies:
            copy.wait()
        for out_ref, batch in ((own_ref, core_index()), (send_ref, 1 - core_index())):
            out_ref[0:2] = ids_ref[batch].astype(f32)
            out_ref[2:4] = gates_ref[batch]
            out_ref[4:] = gain_ref[...]

    rows = 4 + gain.shape[0]
    return pl.pallas_call(
        body,
        out_shape=[shape_of(rows, gain.shape[1], f32)] * 2,
        in_specs=[any_spec] * 3,
        out_specs=[vmem_spec] * 2,
        scratch_shapes=[
            pltpu.VMEM(ids_t.shape, jnp.int32),
            pltpu.VMEM(gates_t.shape, f32),
            pltpu.VMEM(gain.shape, f32),
            pltpu.SemaphoreType.DMA((3,)),
        ],
        compiler_params=pltpu.CompilerParams(vmem_limit_bytes=mlp_limit),
    )(ids_t, gates_t, gain)


def as_column(row):
    size = row.shape[1]
    down = lax.broadcasted_iota(jnp.int32, (size, size), 0)
    across = lax.broadcasted_iota(jnp.int32, (size, size), 1)
    return jnp.sum(jnp.where(down == across, row, 0.0), axis=1, keepdims=True)


def slot_rows(ids_t, experts, capacity):
    rows = ids_t.shape[1]
    expert = lax.broadcasted_iota(jnp.int32, (experts, rows), 0).astype(f32)
    hits = [(ids_t[k : k + 1, :] == expert).astype(f32) for k in range(2)]
    before = lax.broadcasted_iota(jnp.int32, (rows, rows), 0)
    after = lax.broadcasted_iota(jnp.int32, (rows, rows), 1)
    earlier = (before < after).astype(f32)
    rank = jnp.dot(hits[0] + hits[1], earlier, preferred_element_type=f32)
    return [
        ids_t[k : k + 1, :] * float(capacity) + jnp.sum(hits[k] * rank, axis=0, keepdims=True)
        for k in range(2)
    ]


def prepare_pack(own_small, sib_small, state, out_grad, experts, capacity, last_chip):
    rows, features = state.shape
    slots = experts * capacity
    params = [
        jax.ShapeDtypeStruct((2, rows), jnp.int32),
        jax.ShapeDtypeStruct((rows, 2), jnp.int32),
        shape_of(2, rows, f32),
        shape_of(rows, 2, f32),
        shape_of(1, features, f32),
    ]

    def body(own_ref, sib_ref, state_ref, grad_ref, *refs):
        even, odd, out_ref = refs[:5], refs[5:10], refs[10]
        for parity, (tt_ref, t_ref, gt_ref, g_ref, gain_ref) in ((0, even), (1, odd)):
            chosen = jnp.where(core_index() == parity, own_ref[...], sib_ref[...])
            gt_ref[...] = chosen[2:4]
            at = slot_rows(chosen[0:2], experts, capacity)
            for k in range(2):
                tt_ref[k : k + 1, :] = at[k].astype(jnp.int32)
                t_ref[:, k : k + 1] = as_column(at[k]).astype(jnp.int32)
                g_ref[:, k : k + 1] = as_column(chosen[2 + k : 3 + k])
            for i in range(features // rows):
                gain_ref[:, i * rows : (i + 1) * rows] = chosen[4 + i : 5 + i]
        is_last = chip_index() == last_chip

        @pl.when(is_last)
        def _():
            hits = slot_hits(odd[0][...], slots)
            out_ref[...] = (
                pack_rows(grad_ref[...], hits) * slot_gates(hits, odd[2][...])
            ).astype(bf16)

        @pl.when(jnp.logical_not(is_last))
        def _():
            normed = normalize(state_ref[...].astype(f32), even[4][...])
            out_ref[...] = pack_rows(normed, slot_hits(even[0][...], slots)).astype(bf16)

    out_shapes = params + params + [shape_of(slots, features)]
    made = small_call(body, out_shapes, (own_small, sib_small, state, out_grad))
    return made[:5], made[5:10], made[10]


def select_pack(arrived, state, gain, targets_t, slots, chip):
    def body(arrived_ref, state_ref, gain_ref, tt_ref, state_out, out_ref):
        mine = chip_index() == chip

        @pl.when(mine)
        def _():
            state_out[...] = arrived_ref[...]

        @pl.when(jnp.logical_not(mine))
        def _():
            state_out[...] = state_ref[...]

        normed = normalize(state_out[...].astype(f32), gain_ref[...])
        out_ref[...] = pack_rows(normed, slot_hits(tt_ref[...], slots)).astype(bf16)

    return small_call(
        body,
        [shape_of(*state.shape), shape_of(slots, state.shape[1])],
        (arrived, state, gain, targets_t),
    )


def mix(returned, state, targets, gates):
    first, second = unpack_pairs(returned, targets)
    return (state.astype(f32) + (gates[:, 0:1] * first + gates[:, 1:2] * second)).astype(bf16)


def combine(returned, state, targets, gates):
    def body(ret_ref, state_ref, t_ref, g_ref, out_ref):
        out_ref[...] = mix(ret_ref[...], state_ref[...], t_ref[...], g_ref[...])

    return small_call(body, [shape_of(*state.shape)], (returned, state, targets, gates))[0]


def combine_pack(returned, state, targets, gates, gain, targets_t, earlier=()):
    slots = returned.shape[0]

    def body(ret_ref, state_ref, t_ref, g_ref, gain_ref, tt_ref, state_out, out_ref):
        mixed = mix(ret_ref[...], state_ref[...], t_ref[...], g_ref[...])
        state_out[...] = mixed
        normed = normalize(mixed.astype(f32), gain_ref[...])
        out_ref[...] = pack_rows(normed, slot_hits(tt_ref[...], slots)).astype(bf16)

    return small_call(
        body,
        [shape_of(*state.shape), shape_of(slots, state.shape[1])],
        (returned, state, targets, gates, gain, targets_t),
        earlier,
    )


def grad_mix(returned, upstream, state, targets, gain_row):
    first, second = unpack_pairs(returned, targets)
    values = state.astype(f32)
    inv_rms = inverse_rms(values)
    spread = (first + second) * gain_row
    along = jnp.mean(spread * values, axis=-1, keepdims=True)
    return (
        upstream.astype(f32) + inv_rms * spread - values * inv_rms * inv_rms * inv_rms * along
    ).astype(bf16)


def grad_combine(returned, upstream, state, targets, gain):
    def body(ret_ref, up_ref, state_ref, t_ref, gain_ref, out_ref):
        out_ref[...] = grad_mix(
            ret_ref[...], up_ref[...], state_ref[...], t_ref[...], gain_ref[...]
        )

    return small_call(
        body, [shape_of(*state.shape)], (returned, upstream, state, targets, gain)
    )[0]


def grad_combine_pack(
    returned, upstream, state, targets, gain, targets_t, gates_t, earlier=()
):
    slots = returned.shape[0]

    def body(ret_ref, up_ref, state_ref, t_ref, gain_ref, tt_ref, gt_ref, grad_out, out_ref):
        mixed = grad_mix(ret_ref[...], up_ref[...], state_ref[...], t_ref[...], gain_ref[...])
        grad_out[...] = mixed
        hits = slot_hits(tt_ref[...], slots)
        out_ref[...] = (pack_rows(mixed, hits) * slot_gates(hits, gt_ref[...])).astype(bf16)

    return small_call(
        body,
        [shape_of(*state.shape), shape_of(slots, state.shape[1])],
        (returned, upstream, state, targets, gain, targets_t, gates_t),
        earlier,
    )


def grad_pack(upstream, targets_t, gates_t, slots):
    def body(up_ref, tt_ref, gt_ref, out_ref):
        hits = slot_hits(tt_ref[...], slots)
        out_ref[...] = (pack_rows(up_ref[...], hits) * slot_gates(hits, gt_ref[...])).astype(bf16)

    return small_call(body, [shape_of(slots, upstream.shape[1])], (upstream, targets_t, gates_t))[0]


def cuts(size, width):
    width = width if size % width == 0 else size
    return [slice(at, at + width) for at in range(0, size, width)]


class TileCopies:
    def __init__(self, where, semaphores):
        self.where = where
        self.semaphores = semaphores

    def copy(self, source, target, i):
        at = self.where[i]
        return pltpu.make_async_copy(source.at[at], target.at[at], self.semaphores.at[i])


def start_from(parity, own, sibling, begin):
    own_layer = core_index() == parity

    @pl.when(own_layer)
    def _():
        begin(*own)

    @pl.when(jnp.logical_not(own_layer))
    def _():
        begin(*sibling)


def column_tiles(size, width):
    return [(slice(None), cut) for cut in cuts(size, width)]


def row_tiles(size, width):
    return [(cut, slice(None)) for cut in cuts(size, width)]


def mlp_call(body, out_shapes, arrays, scratch, flops, moved, at_hand=False):
    first = vmem_spec if at_hand else any_spec
    return pl.pallas_call(
        body,
        out_shape=out_shapes,
        in_specs=[first] + [any_spec] * (len(arrays) - 1),
        out_specs=[first] + [any_spec] * (len(out_shapes) - 1),
        scratch_shapes=scratch,
        compiler_params=pltpu.CompilerParams(vmem_limit_bytes=rows_limit if at_hand else mlp_limit),
        cost_estimate=pl.CostEstimate(flops=flops, bytes_accessed=moved, transcendentals=0),
    )(*arrays)


def copy_slots(tiles):
    return pltpu.SemaphoreType.DMA((len(tiles),))


def expert_forward(rows, weights, parity, keep_slope):
    slots, features = rows.shape
    hidden = weights[0].shape[1]
    up_tiles, down_tiles = column_tiles(hidden, forward_cut), column_tiles(features, feature_cut)

    def body(x_ref, own_up, own_down, sib_up, sib_down, out_ref, *refs):
        if keep_slope:
            slope_ref, refs = refs[0], refs[1:]
            slope_buf, slope_sem = refs[-2:]
            slope_out = TileCopies(up_tiles, slope_sem)
        up_buf, down_buf, active, up_sem, down_sem = refs[:5]
        up_in, down_in = TileCopies(up_tiles, up_sem), TileCopies(down_tiles, down_sem)

        def begin_up(up):
            for i in range(len(up_tiles)):
                up_in.copy(up, up_buf, i).start()

        def begin_down(down):
            for i in range(len(down_tiles)):
                down_in.copy(down, down_buf, i).start()

        start_from(parity, (own_up,), (sib_up,), begin_up)
        for i, at in enumerate(up_tiles):
            up_in.copy(own_up, up_buf, i).wait()
            if i == 0:
                start_from(parity, (own_down,), (sib_down,), begin_down)
            pre = jnp.dot(x_ref[...], up_buf[at], preferred_element_type=f32)
            value, slope = gelu_parts(pre)
            active[at] = value.astype(bf16)
            if keep_slope:
                slope_buf[at] = slope.astype(bf16)
                slope_out.copy(slope_buf, slope_ref, i).start()
        for i, at in enumerate(down_tiles):
            down_in.copy(own_down, down_buf, i).wait()
            out_ref[at] = jnp.dot(active[...], down_buf[at], preferred_element_type=f32).astype(bf16)
        if keep_slope:
            for i in range(len(up_tiles)):
                slope_out.copy(slope_buf, slope_ref, i).wait()

    out_shapes = [shape_of(slots, features)]
    scratch = [
        pltpu.VMEM((features, hidden), bf16),
        pltpu.VMEM((hidden, features), bf16),
        pltpu.VMEM((slots, hidden), bf16),
        copy_slots(up_tiles),
        copy_slots(down_tiles),
    ]
    if keep_slope:
        out_shapes.append(shape_of(slots, hidden))
        scratch += [pltpu.VMEM((slots, hidden), bf16), copy_slots(up_tiles)]
    return mlp_call(
        body,
        out_shapes,
        (rows, *weights),
        scratch,
        4 * slots * features * hidden,
        4 * features * hidden + 4 * slots * features + 4 * slots * hidden * int(keep_slope),
        True,
    )


def expert_backward(grads, slope, weights, parity, other=None, other_chip=None):
    slots, features = grads.shape
    hidden = weights[0].shape[1]
    down_tiles, up_tiles = row_tiles(hidden, backward_cut), row_tiles(features, feature_cut)
    slope_tiles = column_tiles(hidden, backward_cut)
    out_tiles = column_tiles(features, feature_cut)
    arrays = (grads,) if other is None else (grads, other)

    def body(g_ref, *refs):
        if other is not None:
            other_ref, refs = refs[0], refs[1:]
        own_up, own_down, sib_up, sib_down, slope_ref, out_ref = refs[:6]
        up_buf, down_buf, slope_buf, pre_grad, up_sem, down_sem, slope_sem = refs[6:13]
        if other is not None:
            other_buf, other_sem = refs[13:]
            other_in = pltpu.make_async_copy(other_ref, other_buf, other_sem)
        up_in, down_in = TileCopies(up_tiles, up_sem), TileCopies(down_tiles, down_sem)
        slope_in = TileCopies(slope_tiles, slope_sem)

        def begin_down(down):
            for i in range(len(down_tiles)):
                down_in.copy(down, down_buf, i).start()
                slope_in.copy(slope_ref, slope_buf, i).start()

        def begin_up(up):
            for i in range(len(up_tiles)):
                up_in.copy(up, up_buf, i).start()

        start_from(parity, (own_down,), (sib_down,), begin_down)
        for i, at in enumerate(down_tiles):
            down_in.copy(own_down, down_buf, i).wait()
            if i == 0:
                start_from(parity, (own_up,), (sib_up,), begin_up)
                if other is not None:
                    other_in.start()
            act_grad = lax.dot_general(
                g_ref[...], down_buf[at], contract_last, preferred_element_type=f32
            )
            slope_in.copy(slope_ref, slope_buf, i).wait()
            pre_grad[slope_tiles[i]] = (act_grad * slope_buf[slope_tiles[i]].astype(f32)).astype(bf16)
        for i, at in enumerate(up_tiles):
            up_in.copy(own_up, up_buf, i).wait()
            out_ref[out_tiles[i]] = lax.dot_general(
                pre_grad[...], up_buf[at], contract_last, preferred_element_type=f32
            ).astype(bf16)
        if other is not None:
            other_in.wait()

            @pl.when(chip_index() == other_chip)
            def _():
                out_ref[...] = other_buf[...]

    return mlp_call(
        body,
        [shape_of(slots, features)],
        (*arrays, *weights, slope),
        [
            pltpu.VMEM((features, hidden), bf16),
            pltpu.VMEM((hidden, features), bf16),
            pltpu.VMEM((slots, hidden), bf16),
            pltpu.VMEM((slots, hidden), bf16),
            copy_slots(up_tiles),
            copy_slots(down_tiles),
            copy_slots(slope_tiles),
        ]
        + ([] if other is None else [pltpu.VMEM((slots, features), bf16), pltpu.SemaphoreType.DMA]),
        4 * slots * features * hidden,
        4 * features * hidden + 4 * slots * features + 4 * slots * hidden,
        True,
    )[0]


def act_gradient(grads, weights, parity):
    slots, features = grads.shape
    hidden = weights[0].shape[1]
    down_tiles, out_tiles = row_tiles(hidden, backward_cut), column_tiles(hidden, backward_cut)

    def body(grads_ref, own_down, sib_down, out_ref, down_buf, g_ref, out_buf, down_sem, g_sem, out_sem):
        grads_in = pltpu.make_async_copy(grads_ref, g_ref, g_sem)
        grads_in.start()
        down_in, grads_out = TileCopies(down_tiles, down_sem), TileCopies(out_tiles, out_sem)

        def begin(down):
            for i in range(len(down_tiles)):
                down_in.copy(down, down_buf, i).start()

        start_from(parity, (own_down,), (sib_down,), begin)
        for i, at in enumerate(down_tiles):
            down_in.copy(own_down, down_buf, i).wait()
            if i == 0:
                grads_in.wait()
            out_buf[out_tiles[i]] = lax.dot_general(
                g_ref[...], down_buf[at], contract_last, preferred_element_type=f32
            )
            grads_out.copy(out_buf, out_ref, i).start()
        for i in range(len(out_tiles)):
            grads_out.copy(out_buf, out_ref, i).wait()

    return mlp_call(
        body,
        [shape_of(slots, hidden, f32)],
        (grads, weights[1], weights[3]),
        [
            pltpu.VMEM((hidden, features), bf16),
            pltpu.VMEM((slots, features), bf16),
            pltpu.VMEM((slots, hidden), f32),
            copy_slots(down_tiles),
            pltpu.SemaphoreType.DMA,
            copy_slots(out_tiles),
        ],
        2 * slots * features * hidden,
        2 * features * hidden + 4 * slots * hidden,
    )[0]


def turn_around(rows, act_grad, weights, parity):
    slots, features = rows.shape
    hidden = weights[0].shape[1]
    tiles, out_tiles = column_tiles(hidden, backward_cut), column_tiles(features, feature_cut)
    up_rows = row_tiles(features, feature_cut)

    def body(rows_ref, own_up, sib_up, ag_ref, out_ref, slope_ref, active_ref, *refs):
        up_buf, ag_buf, slope_buf, active_buf, pre_grad, x_ref, out_buf = refs[:7]
        up_in, grad_in, slope_out, active_out = [TileCopies(tiles, sem) for sem in refs[7:11]]
        rows_out = TileCopies(out_tiles, refs[11])
        rows_in = pltpu.make_async_copy(rows_ref, x_ref, refs[12])
        rows_in.start()

        def begin(up):
            for i in range(len(tiles)):
                up_in.copy(up, up_buf, i).start()
                grad_in.copy(ag_ref, ag_buf, i).start()

        start_from(parity, (own_up,), (sib_up,), begin)
        for i, at in enumerate(tiles):
            up_in.copy(own_up, up_buf, i).wait()
            if i == 0:
                rows_in.wait()
            pre = jnp.dot(x_ref[...], up_buf[at], preferred_element_type=f32)
            value, slope = gelu_parts(pre)
            slope_buf[at] = slope.astype(bf16)
            active_buf[at] = value.astype(bf16)
            slope_out.copy(slope_buf, slope_ref, i).start()
            active_out.copy(active_buf, active_ref, i).start()
            grad_in.copy(ag_ref, ag_buf, i).wait()
            pre_grad[at] = (ag_buf[at] * slope).astype(bf16)
        for i, (at, rows_at) in enumerate(zip(out_tiles, up_rows)):
            out_buf[at] = lax.dot_general(
                pre_grad[...], up_buf[rows_at], contract_last, preferred_element_type=f32
            ).astype(bf16)
            rows_out.copy(out_buf, out_ref, i).start()
        for i in range(len(out_tiles)):
            rows_out.copy(out_buf, out_ref, i).wait()
        for i in range(len(tiles)):
            slope_out.copy(slope_buf, slope_ref, i).wait()
            active_out.copy(active_buf, active_ref, i).wait()

    return mlp_call(
        body,
        [shape_of(slots, features), shape_of(slots, hidden), shape_of(slots, hidden)],
        (rows, weights[0], weights[2], act_grad),
        [
            pltpu.VMEM((features, hidden), bf16),
            pltpu.VMEM((slots, hidden), f32),
            pltpu.VMEM((slots, hidden), bf16),
            pltpu.VMEM((slots, hidden), bf16),
            pltpu.VMEM((slots, hidden), bf16),
            pltpu.VMEM((slots, features), bf16),
            pltpu.VMEM((slots, features), bf16),
            copy_slots(tiles),
            copy_slots(tiles),
            copy_slots(tiles),
            copy_slots(tiles),
            copy_slots(out_tiles),
            pltpu.SemaphoreType.DMA,
        ],
        4 * slots * features * hidden,
        2 * features * hidden + 10 * slots * hidden,
    )


def local(inputs, norm_gain, w_up, w_down, expert_ids, gates, out_grad):
    sections = lax.axis_size("section")
    experts = lax.axis_size("expert")
    chips = sections // 2
    last = chips - 1
    chip, core = chip_index(), core_index()
    batches, rows_dev, features = inputs.shape
    capacity = max(2, 5 * rows_dev // (2 * experts))
    slots = experts * capacity

    def swap_cores(x):
        return lax.ppermute(x, "section", [(s, s ^ 1) for s in range(sections)])

    def shift_chips(x, by):
        return lax.ppermute(
            x, "section", [(s, (s + 2 * by) % sections) for s in range(sections)]
        )

    def to_experts(x):
        return lax.all_to_all(x, "expert", split_axis=0, concat_axis=0, tiled=True)

    own_small, to_send = gather_params(
        jnp.swapaxes(expert_ids[0], 1, 2),
        jnp.swapaxes(gates[0], 1, 2),
        norm_gain[0].reshape(features // rows_dev, rows_dev),
    )
    sib_small = swap_cores(to_send)
    state = jnp.where(core == 0, inputs[0], inputs[1])
    last_grad = jnp.where(core == 0, out_grad[0], out_grad[1])
    own_up, own_down = w_up[0, 0], w_down[0, 0]
    sib_small, state, last_grad, up_to_send, down_to_send = lax.optimization_barrier(
        (sib_small, state, last_grad, own_up, own_down)
    )
    weights = (own_up, own_down, swap_cores(up_to_send), swap_cores(down_to_send))

    even, odd, send = prepare_pack(
        own_small, sib_small, state, last_grad, experts, capacity, last
    )
    (even_tt, even_t, even_gt, even_g, even_gain) = even
    (odd_tt, odd_t, odd_gt, odd_g, odd_gain) = odd
    odd_out = None
    act_grad = None
    for turn in range(chips):
        if turn > 0:
            arrived = shift_chips(odd_out_now, 1)
            state, send = select_pack(arrived, state, even_gain, even_tt, slots, turn)
        received = to_experts(send)
        if turn < last:
            (outputs,) = expert_forward(received, weights, 0, False)
        else:
            outputs, even_slope = expert_forward(received, weights, 0, True)
        returned = to_experts(outputs)
        if turn == 0:
            act_grad = act_gradient(received, weights, 1)
        middle, send = combine_pack(
            returned, state, even_t, even_g, odd_gain, odd_tt, (act_grad[:8, :128],) if turn == last else ()
        )
        received = to_experts(send)
        if turn < last:
            (outputs,) = expert_forward(received, weights, 1, False)
            returned = to_experts(outputs)
            odd_out_now = combine(returned, middle, odd_t, odd_g)
            odd_out = (
                odd_out_now if odd_out is None else jnp.where(chip == turn, odd_out_now, odd_out)
            )

    back, odd_slope, odd_active = turn_around(received, act_grad, weights, 1)
    returned = to_experts(back)
    odd_down = jnp.dot(
        odd_active,
        jnp.where(core == 1, weights[1], weights[3]),
        preferred_element_type=f32,
    ).astype(bf16)
    upstream = last_grad
    even_grad = odd_grad = None
    for turn in range(last, -1, -1):
        if turn < last:
            upstream = shift_chips(even_now, -1)
            send = grad_pack(upstream, odd_tt, odd_gt, slots)
            received = to_experts(send)
            if turn == last - 1:
                back = expert_backward(received, odd_slope, weights, 1, odd_down, last)
            else:
                back = expert_backward(received, odd_slope, weights, 1)
            returned = to_experts(back)
            if turn == last - 1:
                final_out = combine(returned, middle, odd_t, odd_g)
                odd_out = jnp.where(chip == last, final_out, odd_out)
        odd_now, send = grad_combine_pack(
            returned, upstream, middle, odd_t, odd_gain, even_tt, even_gt,
            (odd_down,) if turn == last else (),
        )
        odd_grad = odd_now if odd_grad is None else jnp.where(chip == turn, odd_now, odd_grad)
        received = to_experts(send)
        back = expert_backward(received, even_slope, weights, 0)
        returned = to_experts(back)
        even_now = grad_combine(returned, odd_now, state, even_t, even_gain)
        even_grad = even_now if even_grad is None else jnp.where(chip == turn, even_now, even_grad)

    def gather_batches(even, odd):
        own = jnp.where(core == 0, even, odd)
        other = swap_cores(jnp.where(core == 0, odd, even))
        return jnp.where(core == 0, jnp.stack([own, other]), jnp.stack([other, own]))[None]

    return (gather_batches(middle, odd_out), gather_batches(even_grad, odd_grad))


def solution(mesh):
    return jax.shard_map(
        local,
        mesh=mesh,
        in_specs=(
            P(None, "expert", None),
            P("section", None),
            P("section", "expert", None, None),
            P("section", "expert", None, None),
            P("section", None, "expert", None),
            P("section", None, "expert", None),
            P(None, "expert", None),
        ),
        out_specs=(P("section", None, "expert", None), P("section", None, "expert", None)),
        check_vma=False,
    )
```

```python
import jax
import jax.numpy as jnp
from jax import lax
from jax.experimental import pallas as pl
from jax.experimental.pallas import tpu as pltpu
from jax.sharding import PartitionSpec as P

epsilon = 1e-05
gelu_coef = 0.7978845608028654
cubic_coef = 0.044715
contract_last = (((1,), (1,)), ((), ()))
f32 = jnp.float32
bf16 = jnp.bfloat16
vmem_spec = pl.BlockSpec(memory_space=pltpu.VMEM)
any_spec = pl.BlockSpec(memory_space=pl.ANY)
forward_cut = 512
backward_cut = 1024
feature_cut = 512
small_limit = 12 * 1024 * 1024
mlp_limit = 60 * 1024 * 1024
rows_limit = 52 * 1024 * 1024


def gelu_parts(pre):
    square = pre * pre
    tangent = jnp.tanh(pre * (gelu_coef + (gelu_coef * cubic_coef) * square))
    half = 0.5 + 0.5 * tangent
    bend = (0.5 * gelu_coef) + (1.5 * gelu_coef * cubic_coef) * square
    slope = half + pre * (1.0 - tangent * tangent) * bend
    return pre * half, slope


def inverse_rms(values):
    return lax.rsqrt(jnp.mean(values * values, axis=-1, keepdims=True) + epsilon)


def normalize(values, gain_row):
    return (values * inverse_rms(values) * gain_row).astype(bf16)


def chip_index():
    return lax.axis_index("section") // 2


def core_index():
    return lax.axis_index("section") % 2


def unpack_pairs(returned, targets):
    rows, slots = targets.shape[0], returned.shape[0]
    lanes = lax.broadcasted_iota(jnp.int32, (rows, slots), 1)
    picked = []
    for k in range(2):
        chosen = (targets[:, k : k + 1] == lanes).astype(f32).astype(bf16)
        picked.append(jnp.dot(chosen, returned, preferred_element_type=f32))
    return picked


def slot_hits(targets_t, slots):
    rows = targets_t.shape[1]
    sublanes = lax.broadcasted_iota(jnp.int32, (slots, rows), 0)
    return [targets_t[k : k + 1, :] == sublanes for k in range(2)]


def pack_rows(rows, hits):
    chosen = jnp.where(hits[0] | hits[1], 1.0, 0.0).astype(bf16)
    return jnp.dot(chosen, rows, preferred_element_type=f32)


def slot_gates(hits, gates_t):
    total = jnp.where(hits[0], gates_t[0:1, :], 0.0) + jnp.where(hits[1], gates_t[1:2, :], 0.0)
    return jnp.sum(total, axis=1, keepdims=True)


def small_call(body, out_shapes, args, earlier=()):
    def with_earlier(*refs):
        body(*refs[: len(args)], *refs[len(args) + len(earlier) :])

    return pl.pallas_call(
        with_earlier,
        out_shape=out_shapes,
        in_specs=[vmem_spec] * len(args) + [any_spec] * len(earlier),
        out_specs=[vmem_spec] * len(out_shapes),
        compiler_params=pltpu.CompilerParams(vmem_limit_bytes=small_limit),
    )(*args, *earlier)


def shape_of(rows, columns, kind=bf16):
    return jax.ShapeDtypeStruct((rows, columns), kind)


def gather_params(ids_t, gates_t, gain):
    def body(ids_hbm, gates_hbm, gain_hbm, own_ref, send_ref, ids_ref, gates_ref, gain_ref, sem):
        copies = [
            pltpu.make_async_copy(source, target, sem.at[i])
            for i, (source, target) in enumerate(
                ((ids_hbm, ids_ref), (gates_hbm, gates_ref), (gain_hbm, gain_ref))
            )
        ]
        for copy in copies:
            copy.start()
        for copy in copies:
            copy.wait()
        for out_ref, batch in ((own_ref, core_index()), (send_ref, 1 - core_index())):
            out_ref[0:2] = ids_ref[batch].astype(f32)
            out_ref[2:4] = gates_ref[batch]
            out_ref[4:] = gain_ref[...]

    rows = 4 + gain.shape[0]
    return pl.pallas_call(
        body,
        out_shape=[shape_of(rows, gain.shape[1], f32)] * 2,
        in_specs=[any_spec] * 3,
        out_specs=[vmem_spec] * 2,
        scratch_shapes=[
            pltpu.VMEM(ids_t.shape, jnp.int32),
            pltpu.VMEM(gates_t.shape, f32),
            pltpu.VMEM(gain.shape, f32),
            pltpu.SemaphoreType.DMA((3,)),
        ],
        compiler_params=pltpu.CompilerParams(vmem_limit_bytes=mlp_limit),
    )(ids_t, gates_t, gain)


def as_column(row):
    size = row.shape[1]
    down = lax.broadcasted_iota(jnp.int32, (size, size), 0)
    across = lax.broadcasted_iota(jnp.int32, (size, size), 1)
    return jnp.sum(jnp.where(down == across, row, 0.0), axis=1, keepdims=True)


def slot_rows(ids_t, experts, capacity):
    rows = ids_t.shape[1]
    expert = lax.broadcasted_iota(jnp.int32, (experts, rows), 0).astype(f32)
    hits = [(ids_t[k : k + 1, :] == expert).astype(f32) for k in range(2)]
    before = lax.broadcasted_iota(jnp.int32, (rows, rows), 0)
    after = lax.broadcasted_iota(jnp.int32, (rows, rows), 1)
    earlier = (before < after).astype(f32)
    rank = jnp.dot(hits[0] + hits[1], earlier, preferred_element_type=f32)
    return [
        ids_t[k : k + 1, :] * float(capacity) + jnp.sum(hits[k] * rank, axis=0, keepdims=True)
        for k in range(2)
    ]


def prepare_pack(own_small, sib_small, state, out_grad, experts, capacity, last_chip):
    rows, features = state.shape
    slots = experts * capacity
    params = [
        jax.ShapeDtypeStruct((2, rows), jnp.int32),
        jax.ShapeDtypeStruct((rows, 2), jnp.int32),
        shape_of(2, rows, f32),
        shape_of(rows, 2, f32),
        shape_of(1, features, f32),
    ]

    def body(own_ref, sib_ref, state_ref, grad_ref, *refs):
        even, odd, out_ref = refs[:5], refs[5:10], refs[10]
        for parity, (tt_ref, t_ref, gt_ref, g_ref, gain_ref) in ((0, even), (1, odd)):
            chosen = jnp.where(core_index() == parity, own_ref[...], sib_ref[...])
            gt_ref[...] = chosen[2:4]
            at = slot_rows(chosen[0:2], experts, capacity)
            for k in range(2):
                tt_ref[k : k + 1, :] = at[k].astype(jnp.int32)
                t_ref[:, k : k + 1] = as_column(at[k]).astype(jnp.int32)
                g_ref[:, k : k + 1] = as_column(chosen[2 + k : 3 + k])
            for i in range(features // rows):
                gain_ref[:, i * rows : (i + 1) * rows] = chosen[4 + i : 5 + i]
        is_last = chip_index() == last_chip

        @pl.when(is_last)
        def _():
            hits = slot_hits(odd[0][...], slots)
            out_ref[...] = (
                pack_rows(grad_ref[...], hits) * slot_gates(hits, odd[2][...])
            ).astype(bf16)

        @pl.when(jnp.logical_not(is_last))
        def _():
            normed = normalize(state_ref[...].astype(f32), even[4][...])
            out_ref[...] = pack_rows(normed, slot_hits(even[0][...], slots)).astype(bf16)

    out_shapes = params + params + [shape_of(slots, features)]
    made = small_call(body, out_shapes, (own_small, sib_small, state, out_grad))
    return made[:5], made[5:10], made[10]


def select_pack(arrived, state, gain, targets_t, slots, chip):
    def body(arrived_ref, state_ref, gain_ref, tt_ref, state_out, out_ref):
        mine = chip_index() == chip

        @pl.when(mine)
        def _():
            state_out[...] = arrived_ref[...]

        @pl.when(jnp.logical_not(mine))
        def _():
            state_out[...] = state_ref[...]

        normed = normalize(state_out[...].astype(f32), gain_ref[...])
        out_ref[...] = pack_rows(normed, slot_hits(tt_ref[...], slots)).astype(bf16)

    return small_call(
        body,
        [shape_of(*state.shape), shape_of(slots, state.shape[1])],
        (arrived, state, gain, targets_t),
    )


def mix(returned, state, targets, gates):
    first, second = unpack_pairs(returned, targets)
    return (state.astype(f32) + (gates[:, 0:1] * first + gates[:, 1:2] * second)).astype(bf16)


def combine(returned, state, targets, gates):
    def body(ret_ref, state_ref, t_ref, g_ref, out_ref):
        out_ref[...] = mix(ret_ref[...], state_ref[...], t_ref[...], g_ref[...])

    return small_call(body, [shape_of(*state.shape)], (returned, state, targets, gates))[0]


def combine_pack(returned, state, targets, gates, gain, targets_t, earlier=()):
    slots = returned.shape[0]

    def body(ret_ref, state_ref, t_ref, g_ref, gain_ref, tt_ref, state_out, out_ref):
        mixed = mix(ret_ref[...], state_ref[...], t_ref[...], g_ref[...])
        state_out[...] = mixed
        normed = normalize(mixed.astype(f32), gain_ref[...])
        out_ref[...] = pack_rows(normed, slot_hits(tt_ref[...], slots)).astype(bf16)

    return small_call(
        body,
        [shape_of(*state.shape), shape_of(slots, state.shape[1])],
        (returned, state, targets, gates, gain, targets_t),
        earlier,
    )


def grad_mix(returned, upstream, state, targets, gain_row):
    first, second = unpack_pairs(returned, targets)
    values = state.astype(f32)
    inv_rms = inverse_rms(values)
    spread = (first + second) * gain_row
    along = jnp.mean(spread * values, axis=-1, keepdims=True)
    return (
        upstream.astype(f32) + inv_rms * spread - values * inv_rms * inv_rms * inv_rms * along
    ).astype(bf16)


def grad_combine(returned, upstream, state, targets, gain):
    def body(ret_ref, up_ref, state_ref, t_ref, gain_ref, out_ref):
        out_ref[...] = grad_mix(
            ret_ref[...], up_ref[...], state_ref[...], t_ref[...], gain_ref[...]
        )

    return small_call(
        body, [shape_of(*state.shape)], (returned, upstream, state, targets, gain)
    )[0]


def grad_combine_pack(
    returned, upstream, state, targets, gain, targets_t, gates_t, earlier=()
):
    slots = returned.shape[0]

    def body(ret_ref, up_ref, state_ref, t_ref, gain_ref, tt_ref, gt_ref, grad_out, out_ref):
        mixed = grad_mix(ret_ref[...], up_ref[...], state_ref[...], t_ref[...], gain_ref[...])
        grad_out[...] = mixed
        hits = slot_hits(tt_ref[...], slots)
        out_ref[...] = (pack_rows(mixed, hits) * slot_gates(hits, gt_ref[...])).astype(bf16)

    return small_call(
        body,
        [shape_of(*state.shape), shape_of(slots, state.shape[1])],
        (returned, upstream, state, targets, gain, targets_t, gates_t),
        earlier,
    )


def grad_pack(upstream, targets_t, gates_t, slots):
    def body(up_ref, tt_ref, gt_ref, out_ref):
        hits = slot_hits(tt_ref[...], slots)
        out_ref[...] = (pack_rows(up_ref[...], hits) * slot_gates(hits, gt_ref[...])).astype(bf16)

    return small_call(body, [shape_of(slots, upstream.shape[1])], (upstream, targets_t, gates_t))[0]


def cuts(size, width):
    width = width if size % width == 0 else size
    return [slice(at, at + width) for at in range(0, size, width)]


class TileCopies:
    def __init__(self, where, semaphores):
        self.where = where
        self.semaphores = semaphores

    def copy(self, source, target, i):
        at = self.where[i]
        return pltpu.make_async_copy(source.at[at], target.at[at], self.semaphores.at[i])


def start_from(parity, own, sibling, begin):
    own_layer = core_index() == parity

    @pl.when(own_layer)
    def _():
        begin(*own)

    @pl.when(jnp.logical_not(own_layer))
    def _():
        begin(*sibling)


def column_tiles(size, width):
    return [(slice(None), cut) for cut in cuts(size, width)]


def row_tiles(size, width):
    return [(cut, slice(None)) for cut in cuts(size, width)]


def mlp_call(body, out_shapes, arrays, scratch, flops, moved, at_hand=False, limit=None):
    first = vmem_spec if at_hand else any_spec
    return pl.pallas_call(
        body,
        out_shape=out_shapes,
        in_specs=[first] + [any_spec] * (len(arrays) - 1),
        out_specs=[first] + [any_spec] * (len(out_shapes) - 1),
        scratch_shapes=scratch,
        compiler_params=pltpu.CompilerParams(
            vmem_limit_bytes=limit or (rows_limit if at_hand else mlp_limit)
        ),
        cost_estimate=pl.CostEstimate(flops=flops, bytes_accessed=moved, transcendentals=0),
    )(*arrays)


def copy_slots(tiles):
    return pltpu.SemaphoreType.DMA((len(tiles),))


def expert_forward(rows, weights, parity, keep_slope, limit=None):
    slots, features = rows.shape
    hidden = weights[0].shape[1]
    up_tiles, down_tiles = column_tiles(hidden, forward_cut), column_tiles(features, feature_cut)

    def body(x_ref, own_up, own_down, sib_up, sib_down, out_ref, *refs):
        if keep_slope:
            slope_ref, refs = refs[0], refs[1:]
            slope_buf, slope_sem = refs[-2:]
            slope_out = TileCopies(up_tiles, slope_sem)
        up_buf, down_buf, active, up_sem, down_sem = refs[:5]
        up_in, down_in = TileCopies(up_tiles, up_sem), TileCopies(down_tiles, down_sem)

        def begin_up(up):
            for i in range(len(up_tiles)):
                up_in.copy(up, up_buf, i).start()

        def begin_down(down):
            for i in range(len(down_tiles)):
                down_in.copy(down, down_buf, i).start()

        start_from(parity, (own_up,), (sib_up,), begin_up)
        for i, at in enumerate(up_tiles):
            up_in.copy(own_up, up_buf, i).wait()
            if i == 0:
                start_from(parity, (own_down,), (sib_down,), begin_down)
            pre = jnp.dot(x_ref[...], up_buf[at], preferred_element_type=f32)
            value, slope = gelu_parts(pre)
            active[at] = value.astype(bf16)
            if keep_slope:
                slope_buf[at] = slope.astype(bf16)
                slope_out.copy(slope_buf, slope_ref, i).start()
        for i, at in enumerate(down_tiles):
            down_in.copy(own_down, down_buf, i).wait()
            out_ref[at] = jnp.dot(active[...], down_buf[at], preferred_element_type=f32).astype(bf16)
        if keep_slope:
            for i in range(len(up_tiles)):
                slope_out.copy(slope_buf, slope_ref, i).wait()

    out_shapes = [shape_of(slots, features)]
    scratch = [
        pltpu.VMEM((features, hidden), bf16),
        pltpu.VMEM((hidden, features), bf16),
        pltpu.VMEM((slots, hidden), bf16),
        copy_slots(up_tiles),
        copy_slots(down_tiles),
    ]
    if keep_slope:
        out_shapes.append(shape_of(slots, hidden))
        scratch += [pltpu.VMEM((slots, hidden), bf16), copy_slots(up_tiles)]
    return mlp_call(
        body,
        out_shapes,
        (rows, *weights),
        scratch,
        4 * slots * features * hidden,
        4 * features * hidden + 4 * slots * features + 4 * slots * hidden * int(keep_slope),
        True,
        limit,
    )


def expert_backward(grads, slope, weights, parity, other=None, other_chip=None):
    slots, features = grads.shape
    hidden = weights[0].shape[1]
    down_tiles, up_tiles = row_tiles(hidden, backward_cut), row_tiles(features, feature_cut)
    slope_tiles = column_tiles(hidden, backward_cut)
    out_tiles = column_tiles(features, feature_cut)
    arrays = (grads,) if other is None else (grads, other)

    def body(g_ref, *refs):
        if other is not None:
            other_ref, refs = refs[0], refs[1:]
        own_up, own_down, sib_up, sib_down, slope_ref, out_ref = refs[:6]
        up_buf, down_buf, slope_buf, pre_grad, up_sem, down_sem, slope_sem = refs[6:13]
        if other is not None:
            other_buf, other_sem = refs[13:]
            other_in = pltpu.make_async_copy(other_ref, other_buf, other_sem)
        up_in, down_in = TileCopies(up_tiles, up_sem), TileCopies(down_tiles, down_sem)
        slope_in = TileCopies(slope_tiles, slope_sem)

        def begin_down(down):
            for i in range(len(down_tiles)):
                down_in.copy(down, down_buf, i).start()
                slope_in.copy(slope_ref, slope_buf, i).start()

        def begin_up(up):
            for i in range(len(up_tiles)):
                up_in.copy(up, up_buf, i).start()

        start_from(parity, (own_down,), (sib_down,), begin_down)
        for i, at in enumerate(down_tiles):
            down_in.copy(own_down, down_buf, i).wait()
            if i == 0:
                start_from(parity, (own_up,), (sib_up,), begin_up)
                if other is not None:
                    other_in.start()
            act_grad = lax.dot_general(
                g_ref[...], down_buf[at], contract_last, preferred_element_type=f32
            )
            slope_in.copy(slope_ref, slope_buf, i).wait()
            pre_grad[slope_tiles[i]] = (act_grad * slope_buf[slope_tiles[i]].astype(f32)).astype(bf16)
        for i, at in enumerate(up_tiles):
            up_in.copy(own_up, up_buf, i).wait()
            out_ref[out_tiles[i]] = lax.dot_general(
                pre_grad[...], up_buf[at], contract_last, preferred_element_type=f32
            ).astype(bf16)
        if other is not None:
            other_in.wait()

            @pl.when(chip_index() == other_chip)
            def _():
                out_ref[...] = other_buf[...]

    return mlp_call(
        body,
        [shape_of(slots, features)],
        (*arrays, *weights, slope),
        [
            pltpu.VMEM((features, hidden), bf16),
            pltpu.VMEM((hidden, features), bf16),
            pltpu.VMEM((slots, hidden), bf16),
            pltpu.VMEM((slots, hidden), bf16),
            copy_slots(up_tiles),
            copy_slots(down_tiles),
            copy_slots(slope_tiles),
        ]
        + ([] if other is None else [pltpu.VMEM((slots, features), bf16), pltpu.SemaphoreType.DMA]),
        4 * slots * features * hidden,
        4 * features * hidden + 4 * slots * features + 4 * slots * hidden,
        True,
    )[0]


def act_gradient(grads, weights, parity):
    slots, features = grads.shape
    hidden = weights[0].shape[1]
    down_tiles, out_tiles = row_tiles(hidden, backward_cut), column_tiles(hidden, backward_cut)

    def body(grads_ref, own_down, sib_down, out_ref, down_buf, g_ref, out_buf, down_sem, g_sem, out_sem):
        grads_in = pltpu.make_async_copy(grads_ref, g_ref, g_sem)
        grads_in.start()
        down_in, grads_out = TileCopies(down_tiles, down_sem), TileCopies(out_tiles, out_sem)

        def begin(down):
            for i in range(len(down_tiles)):
                down_in.copy(down, down_buf, i).start()

        start_from(parity, (own_down,), (sib_down,), begin)
        for i, at in enumerate(down_tiles):
            down_in.copy(own_down, down_buf, i).wait()
            if i == 0:
                grads_in.wait()
            out_buf[out_tiles[i]] = lax.dot_general(
                g_ref[...], down_buf[at], contract_last, preferred_element_type=f32
            )
            grads_out.copy(out_buf, out_ref, i).start()
        for i in range(len(out_tiles)):
            grads_out.copy(out_buf, out_ref, i).wait()

    return mlp_call(
        body,
        [shape_of(slots, hidden, f32)],
        (grads, weights[1], weights[3]),
        [
            pltpu.VMEM((hidden, features), bf16),
            pltpu.VMEM((slots, features), bf16),
            pltpu.VMEM((slots, hidden), f32),
            copy_slots(down_tiles),
            pltpu.SemaphoreType.DMA,
            copy_slots(out_tiles),
        ],
        2 * slots * features * hidden,
        2 * features * hidden + 4 * slots * hidden,
    )[0]


def turn_around(rows, act_grad, weights, parity):
    slots, features = rows.shape
    hidden = weights[0].shape[1]
    tiles, out_tiles = column_tiles(hidden, backward_cut), column_tiles(features, feature_cut)
    up_rows = row_tiles(features, feature_cut)

    def body(rows_ref, own_up, sib_up, ag_ref, out_ref, slope_ref, active_ref, *refs):
        up_buf, ag_buf, slope_buf, active_buf, pre_grad, x_ref, out_buf = refs[:7]
        up_in, grad_in, slope_out, active_out = [TileCopies(tiles, sem) for sem in refs[7:11]]
        rows_out = TileCopies(out_tiles, refs[11])
        rows_in = pltpu.make_async_copy(rows_ref, x_ref, refs[12])
        rows_in.start()

        def begin(up):
            for i in range(len(tiles)):
                up_in.copy(up, up_buf, i).start()
                grad_in.copy(ag_ref, ag_buf, i).start()

        start_from(parity, (own_up,), (sib_up,), begin)
        for i, at in enumerate(tiles):
            up_in.copy(own_up, up_buf, i).wait()
            if i == 0:
                rows_in.wait()
            pre = jnp.dot(x_ref[...], up_buf[at], preferred_element_type=f32)
            value, slope = gelu_parts(pre)
            slope_buf[at] = slope.astype(bf16)
            active_buf[at] = value.astype(bf16)
            slope_out.copy(slope_buf, slope_ref, i).start()
            active_out.copy(active_buf, active_ref, i).start()
            grad_in.copy(ag_ref, ag_buf, i).wait()
            pre_grad[at] = (ag_buf[at] * slope).astype(bf16)
        for i, (at, rows_at) in enumerate(zip(out_tiles, up_rows)):
            out_buf[at] = lax.dot_general(
                pre_grad[...], up_buf[rows_at], contract_last, preferred_element_type=f32
            ).astype(bf16)
            rows_out.copy(out_buf, out_ref, i).start()
        for i in range(len(out_tiles)):
            rows_out.copy(out_buf, out_ref, i).wait()
        for i in range(len(tiles)):
            slope_out.copy(slope_buf, slope_ref, i).wait()
            active_out.copy(active_buf, active_ref, i).wait()

    return mlp_call(
        body,
        [shape_of(slots, features), shape_of(slots, hidden), shape_of(slots, hidden)],
        (rows, weights[0], weights[2], act_grad),
        [
            pltpu.VMEM((features, hidden), bf16),
            pltpu.VMEM((slots, hidden), f32),
            pltpu.VMEM((slots, hidden), bf16),
            pltpu.VMEM((slots, hidden), bf16),
            pltpu.VMEM((slots, hidden), bf16),
            pltpu.VMEM((slots, features), bf16),
            pltpu.VMEM((slots, features), bf16),
            copy_slots(tiles),
            copy_slots(tiles),
            copy_slots(tiles),
            copy_slots(tiles),
            copy_slots(out_tiles),
            pltpu.SemaphoreType.DMA,
        ],
        4 * slots * features * hidden,
        2 * features * hidden + 10 * slots * hidden,
    )


def local(inputs, norm_gain, w_up, w_down, expert_ids, gates, out_grad):
    sections = lax.axis_size("section")
    experts = lax.axis_size("expert")
    chips = sections // 2
    last = chips - 1
    chip, core = chip_index(), core_index()
    batches, rows_dev, features = inputs.shape
    capacity = max(2, 5 * rows_dev // (2 * experts))
    slots = experts * capacity

    def swap_cores(x):
        return lax.ppermute(x, "section", [(s, s ^ 1) for s in range(sections)])

    def shift_chips(x, by):
        return lax.ppermute(
            x, "section", [(s, (s + 2 * by) % sections) for s in range(sections)]
        )

    def to_experts(x):
        return lax.all_to_all(x, "expert", split_axis=0, concat_axis=0, tiled=True)

    own_small, to_send = gather_params(
        jnp.swapaxes(expert_ids[0], 1, 2),
        jnp.swapaxes(gates[0], 1, 2),
        norm_gain[0].reshape(features // rows_dev, rows_dev),
    )
    sib_small = swap_cores(to_send)
    state = jnp.where(core == 0, inputs[0], inputs[1])
    last_grad = jnp.where(core == 0, out_grad[0], out_grad[1])
    own_up, own_down = w_up[0, 0], w_down[0, 0]
    sib_small, state, last_grad, up_to_send, down_to_send = lax.optimization_barrier(
        (sib_small, state, last_grad, own_up, own_down)
    )
    weights = (own_up, own_down, swap_cores(up_to_send), swap_cores(down_to_send))

    even, odd, send = prepare_pack(
        own_small, sib_small, state, last_grad, experts, capacity, last
    )
    (even_tt, even_t, even_gt, even_g, even_gain) = even
    (odd_tt, odd_t, odd_gt, odd_g, odd_gain) = odd
    odd_out = None
    act_grad = None
    for turn in range(chips):
        if turn > 0:
            arrived = shift_chips(odd_out_now, 1)
            state, send = select_pack(arrived, state, even_gain, even_tt, slots, turn)
        received = to_experts(send)
        if turn < last:
            limit = mlp_limit if turn == 0 else None
            (outputs,) = expert_forward(received, weights, 0, False, limit)
        else:
            outputs, even_slope = expert_forward(received, weights, 0, True)
        returned = to_experts(outputs)
        if turn == 0:
            act_grad = act_gradient(received, weights, 1)
        middle, send = combine_pack(
            returned, state, even_t, even_g, odd_gain, odd_tt, (act_grad[:8, :128],) if turn == last else ()
        )
        received = to_experts(send)
        if turn < last:
            (outputs,) = expert_forward(received, weights, 1, False)
            returned = to_experts(outputs)
            odd_out_now = combine(returned, middle, odd_t, odd_g)
            odd_out = (
                odd_out_now if odd_out is None else jnp.where(chip == turn, odd_out_now, odd_out)
            )

    back, odd_slope, odd_active = turn_around(received, act_grad, weights, 1)
    returned = to_experts(back)
    odd_down = jnp.dot(
        odd_active,
        jnp.where(core == 1, weights[1], weights[3]),
        preferred_element_type=f32,
    ).astype(bf16)
    upstream = last_grad
    even_grad = odd_grad = None
    for turn in range(last, -1, -1):
        if turn < last:
            upstream = shift_chips(even_now, -1)
            send = grad_pack(upstream, odd_tt, odd_gt, slots)
            received = to_experts(send)
            if turn == last - 1:
                back = expert_backward(received, odd_slope, weights, 1, odd_down, last)
            else:
                back = expert_backward(received, odd_slope, weights, 1)
            returned = to_experts(back)
            if turn == last - 1:
                final_out = combine(returned, middle, odd_t, odd_g)
                odd_out = jnp.where(chip == last, final_out, odd_out)
        odd_now, send = grad_combine_pack(
            returned, upstream, middle, odd_t, odd_gain, even_tt, even_gt,
            (odd_down,) if turn == last else (),
        )
        odd_grad = odd_now if odd_grad is None else jnp.where(chip == turn, odd_now, odd_grad)
        received = to_experts(send)
        back = expert_backward(received, even_slope, weights, 0)
        returned = to_experts(back)
        even_now = grad_combine(returned, odd_now, state, even_t, even_gain)
        even_grad = even_now if even_grad is None else jnp.where(chip == turn, even_now, even_grad)

    def gather_batches(even, odd):
        own = jnp.where(core == 0, even, odd)
        other = swap_cores(jnp.where(core == 0, odd, even))
        return jnp.where(core == 0, jnp.stack([own, other]), jnp.stack([other, own]))[None]

    return (gather_batches(middle, odd_out), gather_batches(even_grad, odd_grad))


def solution(mesh):
    return jax.shard_map(
        local,
        mesh=mesh,
        in_specs=(
            P(None, "expert", None),
            P("section", None),
            P("section", "expert", None, None),
            P("section", "expert", None, None),
            P("section", None, "expert", None),
            P("section", None, "expert", None),
            P(None, "expert", None),
        ),
        out_specs=(P("section", None, "expert", None), P("section", None, "expert", None)),
        check_vma=False,
    )
```

```python
import jax
import jax.numpy as jnp
from jax import lax
from jax.experimental import pallas as pl
from jax.experimental.pallas import tpu as pltpu
from jax.sharding import PartitionSpec as P

epsilon = 1e-05
gelu_coef = 0.7978845608028654
cubic_coef = 0.044715
contract_last = (((1,), (1,)), ((), ()))
f32 = jnp.float32
bf16 = jnp.bfloat16
vmem_spec = pl.BlockSpec(memory_space=pltpu.VMEM)
any_spec = pl.BlockSpec(memory_space=pl.ANY)
forward_cut = 512
backward_cut = 1024
feature_cut = 512
small_limit = 12 * 1024 * 1024
mlp_limit = 60 * 1024 * 1024
rows_limit = 52 * 1024 * 1024


def gelu_parts(pre):
    square = pre * pre
    tangent = jnp.tanh(pre * (gelu_coef + (gelu_coef * cubic_coef) * square))
    half = 0.5 + 0.5 * tangent
    bend = (0.5 * gelu_coef) + (1.5 * gelu_coef * cubic_coef) * square
    slope = half + pre * (1.0 - tangent * tangent) * bend
    return pre * half, slope


def inverse_rms(values):
    return lax.rsqrt(jnp.mean(values * values, axis=-1, keepdims=True) + epsilon)


def normalize(values, gain_row):
    return (values * inverse_rms(values) * gain_row).astype(bf16)


def chip_index():
    return lax.axis_index("section") // 2


def core_index():
    return lax.axis_index("section") % 2


def unpack_pairs(returned, targets):
    rows, slots = targets.shape[0], returned.shape[0]
    lanes = lax.broadcasted_iota(jnp.int32, (rows, slots), 1)
    picked = []
    for k in range(2):
        chosen = (targets[:, k : k + 1] == lanes).astype(f32).astype(bf16)
        picked.append(jnp.dot(chosen, returned, preferred_element_type=f32))
    return picked


def slot_hits(targets_t, slots):
    rows = targets_t.shape[1]
    sublanes = lax.broadcasted_iota(jnp.int32, (slots, rows), 0)
    return [targets_t[k : k + 1, :] == sublanes for k in range(2)]


def pack_rows(rows, hits):
    chosen = jnp.where(hits[0] | hits[1], 1.0, 0.0).astype(bf16)
    return jnp.dot(chosen, rows, preferred_element_type=f32)


def slot_gates(hits, gates_t):
    total = jnp.where(hits[0], gates_t[0:1, :], 0.0) + jnp.where(hits[1], gates_t[1:2, :], 0.0)
    return jnp.sum(total, axis=1, keepdims=True)


def small_call(body, out_shapes, args, earlier=()):
    def with_earlier(*refs):
        body(*refs[: len(args)], *refs[len(args) + len(earlier) :])

    return pl.pallas_call(
        with_earlier,
        out_shape=out_shapes,
        in_specs=[vmem_spec] * len(args) + [any_spec] * len(earlier),
        out_specs=[vmem_spec] * len(out_shapes),
        compiler_params=pltpu.CompilerParams(vmem_limit_bytes=small_limit),
    )(*args, *earlier)


def shape_of(rows, columns, kind=bf16):
    return jax.ShapeDtypeStruct((rows, columns), kind)


def gather_params(ids_t, gates_t, gain):
    def body(ids_hbm, gates_hbm, gain_hbm, own_ref, send_ref, ids_ref, gates_ref, gain_ref, sem):
        copies = [
            pltpu.make_async_copy(source, target, sem.at[i])
            for i, (source, target) in enumerate(
                ((ids_hbm, ids_ref), (gates_hbm, gates_ref), (gain_hbm, gain_ref))
            )
        ]
        for copy in copies:
            copy.start()
        for copy in copies:
            copy.wait()
        for out_ref, batch in ((own_ref, core_index()), (send_ref, 1 - core_index())):
            out_ref[0:2] = ids_ref[batch].astype(f32)
            out_ref[2:4] = gates_ref[batch]
            out_ref[4:] = gain_ref[...]

    rows = 4 + gain.shape[0]
    return pl.pallas_call(
        body,
        out_shape=[shape_of(rows, gain.shape[1], f32)] * 2,
        in_specs=[any_spec] * 3,
        out_specs=[vmem_spec] * 2,
        scratch_shapes=[
            pltpu.VMEM(ids_t.shape, jnp.int32),
            pltpu.VMEM(gates_t.shape, f32),
            pltpu.VMEM(gain.shape, f32),
            pltpu.SemaphoreType.DMA((3,)),
        ],
        compiler_params=pltpu.CompilerParams(vmem_limit_bytes=mlp_limit),
    )(ids_t, gates_t, gain)


def as_column(row):
    size = row.shape[1]
    down = lax.broadcasted_iota(jnp.int32, (size, size), 0)
    across = lax.broadcasted_iota(jnp.int32, (size, size), 1)
    return jnp.sum(jnp.where(down == across, row, 0.0), axis=1, keepdims=True)


def slot_rows(ids_t, experts, capacity):
    rows = ids_t.shape[1]
    expert = lax.broadcasted_iota(jnp.int32, (experts, rows), 0).astype(f32)
    hits = [(ids_t[k : k + 1, :] == expert).astype(f32) for k in range(2)]
    before = lax.broadcasted_iota(jnp.int32, (rows, rows), 0)
    after = lax.broadcasted_iota(jnp.int32, (rows, rows), 1)
    earlier = (before < after).astype(f32)
    rank = jnp.dot(hits[0] + hits[1], earlier, preferred_element_type=f32)
    return [
        ids_t[k : k + 1, :] * float(capacity) + jnp.sum(hits[k] * rank, axis=0, keepdims=True)
        for k in range(2)
    ]


def prepare_pack(own_small, sib_small, state, out_grad, experts, capacity, last_chip):
    rows, features = state.shape
    slots = experts * capacity
    params = [
        jax.ShapeDtypeStruct((2, rows), jnp.int32),
        jax.ShapeDtypeStruct((rows, 2), jnp.int32),
        shape_of(2, rows, f32),
        shape_of(rows, 2, f32),
        shape_of(1, features, f32),
    ]

    def body(own_ref, sib_ref, state_ref, grad_ref, *refs):
        even, odd, out_ref = refs[:5], refs[5:10], refs[10]
        for parity, (tt_ref, t_ref, gt_ref, g_ref, gain_ref) in ((0, even), (1, odd)):
            chosen = jnp.where(core_index() == parity, own_ref[...], sib_ref[...])
            gt_ref[...] = chosen[2:4]
            at = slot_rows(chosen[0:2], experts, capacity)
            for k in range(2):
                tt_ref[k : k + 1, :] = at[k].astype(jnp.int32)
                t_ref[:, k : k + 1] = as_column(at[k]).astype(jnp.int32)
                g_ref[:, k : k + 1] = as_column(chosen[2 + k : 3 + k])
            for i in range(features // rows):
                gain_ref[:, i * rows : (i + 1) * rows] = chosen[4 + i : 5 + i]
        is_last = chip_index() == last_chip

        @pl.when(is_last)
        def _():
            hits = slot_hits(odd[0][...], slots)
            out_ref[...] = (
                pack_rows(grad_ref[...], hits) * slot_gates(hits, odd[2][...])
            ).astype(bf16)

        @pl.when(jnp.logical_not(is_last))
        def _():
            normed = normalize(state_ref[...].astype(f32), even[4][...])
            out_ref[...] = pack_rows(normed, slot_hits(even[0][...], slots)).astype(bf16)

    out_shapes = params + params + [shape_of(slots, features)]
    made = small_call(body, out_shapes, (own_small, sib_small, state, out_grad))
    return made[:5], made[5:10], made[10]


def select_pack(arrived, state, gain, targets_t, slots, chip):
    def body(arrived_ref, state_ref, gain_ref, tt_ref, state_out, out_ref):
        mine = chip_index() == chip

        @pl.when(mine)
        def _():
            state_out[...] = arrived_ref[...]

        @pl.when(jnp.logical_not(mine))
        def _():
            state_out[...] = state_ref[...]

        normed = normalize(state_out[...].astype(f32), gain_ref[...])
        out_ref[...] = pack_rows(normed, slot_hits(tt_ref[...], slots)).astype(bf16)

    return small_call(
        body,
        [shape_of(*state.shape), shape_of(slots, state.shape[1])],
        (arrived, state, gain, targets_t),
    )


def mix(returned, state, targets, gates):
    first, second = unpack_pairs(returned, targets)
    return (state.astype(f32) + (gates[:, 0:1] * first + gates[:, 1:2] * second)).astype(bf16)


def combine(returned, state, targets, gates):
    def body(ret_ref, state_ref, t_ref, g_ref, out_ref):
        out_ref[...] = mix(ret_ref[...], state_ref[...], t_ref[...], g_ref[...])

    return small_call(body, [shape_of(*state.shape)], (returned, state, targets, gates))[0]


def combine_pack(returned, state, targets, gates, gain, targets_t, earlier=()):
    slots = returned.shape[0]

    def body(ret_ref, state_ref, t_ref, g_ref, gain_ref, tt_ref, state_out, out_ref):
        mixed = mix(ret_ref[...], state_ref[...], t_ref[...], g_ref[...])
        state_out[...] = mixed
        normed = normalize(mixed.astype(f32), gain_ref[...])
        out_ref[...] = pack_rows(normed, slot_hits(tt_ref[...], slots)).astype(bf16)

    return small_call(
        body,
        [shape_of(*state.shape), shape_of(slots, state.shape[1])],
        (returned, state, targets, gates, gain, targets_t),
        earlier,
    )


def grad_mix(returned, upstream, state, targets, gain_row):
    first, second = unpack_pairs(returned, targets)
    values = state.astype(f32)
    inv_rms = inverse_rms(values)
    spread = (first + second) * gain_row
    along = jnp.mean(spread * values, axis=-1, keepdims=True)
    return (
        upstream.astype(f32) + inv_rms * spread - values * inv_rms * inv_rms * inv_rms * along
    ).astype(bf16)


def grad_combine(returned, upstream, state, targets, gain):
    def body(ret_ref, up_ref, state_ref, t_ref, gain_ref, out_ref):
        out_ref[...] = grad_mix(
            ret_ref[...], up_ref[...], state_ref[...], t_ref[...], gain_ref[...]
        )

    return small_call(
        body, [shape_of(*state.shape)], (returned, upstream, state, targets, gain)
    )[0]


def grad_combine_pack(
    returned, upstream, state, targets, gain, targets_t, gates_t, earlier=()
):
    slots = returned.shape[0]

    def body(ret_ref, up_ref, state_ref, t_ref, gain_ref, tt_ref, gt_ref, grad_out, out_ref):
        mixed = grad_mix(ret_ref[...], up_ref[...], state_ref[...], t_ref[...], gain_ref[...])
        grad_out[...] = mixed
        hits = slot_hits(tt_ref[...], slots)
        out_ref[...] = (pack_rows(mixed, hits) * slot_gates(hits, gt_ref[...])).astype(bf16)

    return small_call(
        body,
        [shape_of(*state.shape), shape_of(slots, state.shape[1])],
        (returned, upstream, state, targets, gain, targets_t, gates_t),
        earlier,
    )


def grad_pack(upstream, targets_t, gates_t, slots):
    def body(up_ref, tt_ref, gt_ref, out_ref):
        hits = slot_hits(tt_ref[...], slots)
        out_ref[...] = (pack_rows(up_ref[...], hits) * slot_gates(hits, gt_ref[...])).astype(bf16)

    return small_call(body, [shape_of(slots, upstream.shape[1])], (upstream, targets_t, gates_t))[0]


def cuts(size, width):
    width = width if size % width == 0 else size
    return [slice(at, at + width) for at in range(0, size, width)]


class TileCopies:
    def __init__(self, where, semaphores):
        self.where = where
        self.semaphores = semaphores

    def copy(self, source, target, i):
        at = self.where[i]
        return pltpu.make_async_copy(source.at[at], target.at[at], self.semaphores.at[i])


def start_from(parity, own, sibling, begin):
    own_layer = core_index() == parity

    @pl.when(own_layer)
    def _():
        begin(*own)

    @pl.when(jnp.logical_not(own_layer))
    def _():
        begin(*sibling)


def column_tiles(size, width):
    return [(slice(None), cut) for cut in cuts(size, width)]


def row_tiles(size, width):
    return [(cut, slice(None)) for cut in cuts(size, width)]


def mlp_call(body, out_shapes, arrays, scratch, flops, moved, at_hand=False, limit=None):
    first = vmem_spec if at_hand else any_spec
    return pl.pallas_call(
        body,
        out_shape=out_shapes,
        in_specs=[first] + [any_spec] * (len(arrays) - 1),
        out_specs=[first] + [any_spec] * (len(out_shapes) - 1),
        scratch_shapes=scratch,
        compiler_params=pltpu.CompilerParams(
            vmem_limit_bytes=limit or (rows_limit if at_hand else mlp_limit)
        ),
        cost_estimate=pl.CostEstimate(flops=flops, bytes_accessed=moved, transcendentals=0),
    )(*arrays)


def copy_slots(tiles):
    return pltpu.SemaphoreType.DMA((len(tiles),))


def expert_forward(rows, weights, parity, keep_slope, limit=None):
    slots, features = rows.shape
    hidden = weights[0].shape[1]
    up_tiles, down_tiles = column_tiles(hidden, forward_cut), column_tiles(features, feature_cut)

    def body(x_ref, own_up, own_down, sib_up, sib_down, out_ref, *refs):
        if keep_slope:
            slope_ref, refs = refs[0], refs[1:]
            slope_buf, slope_sem = refs[-2:]
            slope_out = TileCopies(up_tiles, slope_sem)
        up_buf, down_buf, active, up_sem, down_sem = refs[:5]
        up_in, down_in = TileCopies(up_tiles, up_sem), TileCopies(down_tiles, down_sem)

        def begin_up(up):
            for i in range(len(up_tiles)):
                up_in.copy(up, up_buf, i).start()

        def begin_down(down):
            for i in range(len(down_tiles)):
                down_in.copy(down, down_buf, i).start()

        start_from(parity, (own_up,), (sib_up,), begin_up)
        for i, at in enumerate(up_tiles):
            up_in.copy(own_up, up_buf, i).wait()
            if i == 0:
                start_from(parity, (own_down,), (sib_down,), begin_down)
            pre = jnp.dot(x_ref[...], up_buf[at], preferred_element_type=f32)
            value, slope = gelu_parts(pre)
            active[at] = value.astype(bf16)
            if keep_slope:
                slope_buf[at] = slope.astype(bf16)
                slope_out.copy(slope_buf, slope_ref, i).start()
        for i, at in enumerate(down_tiles):
            down_in.copy(own_down, down_buf, i).wait()
            out_ref[at] = jnp.dot(active[...], down_buf[at], preferred_element_type=f32).astype(bf16)
        if keep_slope:
            for i in range(len(up_tiles)):
                slope_out.copy(slope_buf, slope_ref, i).wait()

    out_shapes = [shape_of(slots, features)]
    scratch = [
        pltpu.VMEM((features, hidden), bf16),
        pltpu.VMEM((hidden, features), bf16),
        pltpu.VMEM((slots, hidden), bf16),
        copy_slots(up_tiles),
        copy_slots(down_tiles),
    ]
    if keep_slope:
        out_shapes.append(shape_of(slots, hidden))
        scratch += [pltpu.VMEM((slots, hidden), bf16), copy_slots(up_tiles)]
    return mlp_call(
        body,
        out_shapes,
        (rows, *weights),
        scratch,
        4 * slots * features * hidden,
        4 * features * hidden + 4 * slots * features + 4 * slots * hidden * int(keep_slope),
        True,
        limit,
    )


def expert_backward(grads, slope, weights, parity, other=None, other_chip=None):
    slots, features = grads.shape
    hidden = weights[0].shape[1]
    down_tiles, up_tiles = row_tiles(hidden, backward_cut), row_tiles(features, feature_cut)
    slope_tiles = column_tiles(hidden, backward_cut)
    out_tiles = column_tiles(features, feature_cut)
    arrays = (grads,) if other is None else (grads, other)

    def body(g_ref, *refs):
        if other is not None:
            other_ref, refs = refs[0], refs[1:]
        own_up, own_down, sib_up, sib_down, slope_ref, out_ref = refs[:6]
        up_buf, down_buf, slope_buf, pre_grad, up_sem, down_sem, slope_sem = refs[6:13]
        if other is not None:
            other_buf, other_sem = refs[13:]
            other_in = pltpu.make_async_copy(other_ref, other_buf, other_sem)
        up_in, down_in = TileCopies(up_tiles, up_sem), TileCopies(down_tiles, down_sem)
        slope_in = TileCopies(slope_tiles, slope_sem)

        def begin_down(down):
            for i in range(len(down_tiles)):
                down_in.copy(down, down_buf, i).start()
                slope_in.copy(slope_ref, slope_buf, i).start()

        def begin_up(up):
            for i in range(len(up_tiles)):
                up_in.copy(up, up_buf, i).start()

        start_from(parity, (own_down,), (sib_down,), begin_down)
        for i, at in enumerate(down_tiles):
            down_in.copy(own_down, down_buf, i).wait()
            if i == 0:
                start_from(parity, (own_up,), (sib_up,), begin_up)
                if other is not None:
                    other_in.start()
            act_grad = lax.dot_general(
                g_ref[...], down_buf[at], contract_last, preferred_element_type=f32
            )
            slope_in.copy(slope_ref, slope_buf, i).wait()
            pre_grad[slope_tiles[i]] = (act_grad * slope_buf[slope_tiles[i]].astype(f32)).astype(bf16)
        for i, at in enumerate(up_tiles):
            up_in.copy(own_up, up_buf, i).wait()
            out_ref[out_tiles[i]] = lax.dot_general(
                pre_grad[...], up_buf[at], contract_last, preferred_element_type=f32
            ).astype(bf16)
        if other is not None:
            other_in.wait()

            @pl.when(chip_index() == other_chip)
            def _():
                out_ref[...] = other_buf[...]

    return mlp_call(
        body,
        [shape_of(slots, features)],
        (*arrays, *weights, slope),
        [
            pltpu.VMEM((features, hidden), bf16),
            pltpu.VMEM((hidden, features), bf16),
            pltpu.VMEM((slots, hidden), bf16),
            pltpu.VMEM((slots, hidden), bf16),
            copy_slots(up_tiles),
            copy_slots(down_tiles),
            copy_slots(slope_tiles),
        ]
        + ([] if other is None else [pltpu.VMEM((slots, features), bf16), pltpu.SemaphoreType.DMA]),
        4 * slots * features * hidden,
        4 * features * hidden + 4 * slots * features + 4 * slots * hidden,
        True,
    )[0]


def act_gradient(grads, weights, parity):
    slots, features = grads.shape
    hidden = weights[0].shape[1]
    down_tiles, out_tiles = row_tiles(hidden, backward_cut), column_tiles(hidden, backward_cut)

    def body(grads_ref, own_down, sib_down, out_ref, down_buf, g_ref, out_buf, down_sem, g_sem, out_sem):
        grads_in = pltpu.make_async_copy(grads_ref, g_ref, g_sem)
        grads_in.start()
        down_in, grads_out = TileCopies(down_tiles, down_sem), TileCopies(out_tiles, out_sem)

        def begin(down):
            for i in range(len(down_tiles)):
                down_in.copy(down, down_buf, i).start()

        start_from(parity, (own_down,), (sib_down,), begin)
        for i, at in enumerate(down_tiles):
            down_in.copy(own_down, down_buf, i).wait()
            if i == 0:
                grads_in.wait()
            out_buf[out_tiles[i]] = lax.dot_general(
                g_ref[...], down_buf[at], contract_last, preferred_element_type=f32
            )
            grads_out.copy(out_buf, out_ref, i).start()
        for i in range(len(out_tiles)):
            grads_out.copy(out_buf, out_ref, i).wait()

    return mlp_call(
        body,
        [shape_of(slots, hidden, f32)],
        (grads, weights[1], weights[3]),
        [
            pltpu.VMEM((hidden, features), bf16),
            pltpu.VMEM((slots, features), bf16),
            pltpu.VMEM((slots, hidden), f32),
            copy_slots(down_tiles),
            pltpu.SemaphoreType.DMA,
            copy_slots(out_tiles),
        ],
        2 * slots * features * hidden,
        2 * features * hidden + 4 * slots * hidden,
    )[0]


def turn_around(rows, act_grad, weights, parity):
    slots, features = rows.shape
    hidden = weights[0].shape[1]
    tiles, out_tiles = column_tiles(hidden, backward_cut), column_tiles(features, feature_cut)
    up_rows = row_tiles(features, feature_cut)

    def body(x_ref, own_up, sib_up, ag_ref, out_ref, slope_ref, active_ref, *refs):
        up_buf, ag_buf, slope_buf, active_buf, pre_grad = refs[:5]
        up_in, grad_in, slope_out, active_out = [TileCopies(tiles, sem) for sem in refs[5:9]]

        def begin(up):
            for i in range(len(tiles)):
                up_in.copy(up, up_buf, i).start()
                grad_in.copy(ag_ref, ag_buf, i).start()

        start_from(parity, (own_up,), (sib_up,), begin)
        for i, at in enumerate(tiles):
            up_in.copy(own_up, up_buf, i).wait()
            pre = jnp.dot(x_ref[...], up_buf[at], preferred_element_type=f32)
            value, slope = gelu_parts(pre)
            slope_buf[at] = slope.astype(bf16)
            active_buf[at] = value.astype(bf16)
            slope_out.copy(slope_buf, slope_ref, i).start()
            active_out.copy(active_buf, active_ref, i).start()
            grad_in.copy(ag_ref, ag_buf, i).wait()
            pre_grad[at] = (ag_buf[at] * slope).astype(bf16)
        for at, rows_at in zip(out_tiles, up_rows):
            out_ref[at] = lax.dot_general(
                pre_grad[...], up_buf[rows_at], contract_last, preferred_element_type=f32
            ).astype(bf16)
        for i in range(len(tiles)):
            slope_out.copy(slope_buf, slope_ref, i).wait()
            active_out.copy(active_buf, active_ref, i).wait()

    return mlp_call(
        body,
        [shape_of(slots, features), shape_of(slots, hidden), shape_of(slots, hidden)],
        (rows, weights[0], weights[2], act_grad),
        [
            pltpu.VMEM((features, hidden), bf16),
            pltpu.VMEM((slots, hidden), f32),
            pltpu.VMEM((slots, hidden), bf16),
            pltpu.VMEM((slots, hidden), bf16),
            pltpu.VMEM((slots, hidden), bf16),
            copy_slots(tiles),
            copy_slots(tiles),
            copy_slots(tiles),
            copy_slots(tiles),
        ],
        4 * slots * features * hidden,
        2 * features * hidden + 10 * slots * hidden,
        True,
    )


def local(inputs, norm_gain, w_up, w_down, expert_ids, gates, out_grad):
    sections = lax.axis_size("section")
    experts = lax.axis_size("expert")
    chips = sections // 2
    last = chips - 1
    chip, core = chip_index(), core_index()
    batches, rows_dev, features = inputs.shape
    capacity = max(2, 5 * rows_dev // (2 * experts))
    slots = experts * capacity

    def swap_cores(x):
        return lax.ppermute(x, "section", [(s, s ^ 1) for s in range(sections)])

    def shift_chips(x, by):
        return lax.ppermute(
            x, "section", [(s, (s + 2 * by) % sections) for s in range(sections)]
        )

    def to_experts(x):
        return lax.all_to_all(x, "expert", split_axis=0, concat_axis=0, tiled=True)

    own_small, to_send = gather_params(
        jnp.swapaxes(expert_ids[0], 1, 2),
        jnp.swapaxes(gates[0], 1, 2),
        norm_gain[0].reshape(features // rows_dev, rows_dev),
    )
    sib_small = swap_cores(to_send)
    state = jnp.where(core == 0, inputs[0], inputs[1])
    last_grad = jnp.where(core == 0, out_grad[0], out_grad[1])
    own_up, own_down = w_up[0, 0], w_down[0, 0]
    sib_small, state, last_grad, up_to_send, down_to_send = lax.optimization_barrier(
        (sib_small, state, last_grad, own_up, own_down)
    )
    weights = (own_up, own_down, swap_cores(up_to_send), swap_cores(down_to_send))

    even, odd, send = prepare_pack(
        own_small, sib_small, state, last_grad, experts, capacity, last
    )
    (even_tt, even_t, even_gt, even_g, even_gain) = even
    (odd_tt, odd_t, odd_gt, odd_g, odd_gain) = odd
    odd_out = None
    act_grad = None
    for turn in range(chips):
        if turn > 0:
            arrived = shift_chips(odd_out_now, 1)
            state, send = select_pack(arrived, state, even_gain, even_tt, slots, turn)
        received = to_experts(send)
        if turn < last:
            limit = mlp_limit if turn == 0 else None
            (outputs,) = expert_forward(received, weights, 0, False, limit)
        else:
            outputs, even_slope = expert_forward(received, weights, 0, True)
        returned = to_experts(outputs)
        if turn == 0:
            act_grad = act_gradient(received, weights, 1)
        middle, send = combine_pack(
            returned, state, even_t, even_g, odd_gain, odd_tt, (act_grad[:8, :128],) if turn == last else ()
        )
        received = to_experts(send)
        if turn < last:
            (outputs,) = expert_forward(received, weights, 1, False)
            returned = to_experts(outputs)
            odd_out_now = combine(returned, middle, odd_t, odd_g)
            odd_out = (
                odd_out_now if odd_out is None else jnp.where(chip == turn, odd_out_now, odd_out)
            )

    back, odd_slope, odd_active = turn_around(received, act_grad, weights, 1)
    returned = to_experts(back)
    odd_down = jnp.dot(
        odd_active,
        jnp.where(core == 1, weights[1], weights[3]),
        preferred_element_type=f32,
    ).astype(bf16)
    upstream = last_grad
    even_grad = odd_grad = None
    for turn in range(last, -1, -1):
        if turn < last:
            upstream = shift_chips(even_now, -1)
            send = grad_pack(upstream, odd_tt, odd_gt, slots)
            received = to_experts(send)
            if turn == last - 1:
                back = expert_backward(received, odd_slope, weights, 1, odd_down, last)
            else:
                back = expert_backward(received, odd_slope, weights, 1)
            returned = to_experts(back)
            if turn == last - 1:
                final_out = combine(returned, middle, odd_t, odd_g)
                odd_out = jnp.where(chip == last, final_out, odd_out)
        odd_now, send = grad_combine_pack(
            returned, upstream, middle, odd_t, odd_gain, even_tt, even_gt,
            (odd_down,) if turn == last else (),
        )
        odd_grad = odd_now if odd_grad is None else jnp.where(chip == turn, odd_now, odd_grad)
        received = to_experts(send)
        back = expert_backward(received, even_slope, weights, 0)
        returned = to_experts(back)
        even_now = grad_combine(returned, odd_now, state, even_t, even_gain)
        even_grad = even_now if even_grad is None else jnp.where(chip == turn, even_now, even_grad)

    def gather_batches(even, odd):
        own = jnp.where(core == 0, even, odd)
        other = swap_cores(jnp.where(core == 0, odd, even))
        return jnp.where(core == 0, jnp.stack([own, other]), jnp.stack([other, own]))[None]

    return (gather_batches(middle, odd_out), gather_batches(even_grad, odd_grad))


def solution(mesh):
    return jax.shard_map(
        local,
        mesh=mesh,
        in_specs=(
            P(None, "expert", None),
            P("section", None),
            P("section", "expert", None, None),
            P("section", "expert", None, None),
            P("section", None, "expert", None),
            P("section", None, "expert", None),
            P(None, "expert", None),
        ),
        out_specs=(P("section", None, "expert", None), P("section", None, "expert", None)),
        check_vma=False,
    )
```
